512 devices in a mesh: view: 8 (over x, core), blk: 64 (over z, y).
Axes of the slice: x: 4, y: 8, z: 8, core: 2. Of those that a mesh axis runs over, the one named last changes fastest.
Arguments:
- estimate: float32 [2, 1024, 1024], P(None, 'blk'), may hold values from 0.5 to 2
- measured: float32 [8, 2, 1024, 1024], P('view', None, 'blk'), may hold values from 0.25 to 4
- psf_z: float32 [8, 3, 31], P('view'), may hold values from 0.05 to 1
- psf_y: float32 [8, 3, 31], P('view'), may hold values from 0.05 to 1
- psf_x: float32 [8, 3, 31], P('view'), may hold values from 0.05 to 1
- psf_mix: float32 [8, 3], P('view'), may hold values from 0.2 to 1
- weight_tiles: float32 [8, 8, 1024], replicated, may hold values from 0.1 to 1
- tile_index: int32 [8, 128], P('view', 'blk'), may hold values from 0 to 7
- src_row: int32 [8, 1024], P('view', 'blk'), may hold values from 0 to 1023, as said below
- dst_row: int32 [8, 1024], P('view', 'blk'), may hold values from 0 to 1023, as said below
- col_shift: int32 [8, 1024], P('view', 'blk'), may hold values from -8 to 8
- back_shift: int32 [8, 1024], P('view', 'blk'), may hold values from -8 to 8, as said below
Outputs:
- estimate_out: float32 [2, 1024, 1024], P(None, 'blk')
The draws below stay inside these ranges and needn't reach their ends.
Inputs may be any that keep to these rules, and one draw needn't show every extreme that they name: For each view, src_row is a permutation of the 1024 output rows. The slab's rows form device blocks of 16 rows, and for each view the blocks pair up with an adjacent block (or stay alone at an end); a row's source lies in its own block or in its partner's, equally many rows cross each way between partners, at most 8, and exactly 8 for some pair in every view. dst_row[v] is the inverse permutation of src_row[v]. back_shift[v, i] = col_shift[v, dst_row[v, i]].
All inputs are finite; a program needn't handle non-finite values.
Results may differ from the reference program's by a relative error of at most 0.0003.
Values sent between devices are 32-bit elements; how exact they have to be, the bound alone decides.
No kernel may reach another device: no remote copies, remote signals or barrier semaphores. Data moves between devices by JAX's collectives and lax.ppermute only.
A program may use at most 64 MiB of HBM per device.

```python
import math
import jax
import jax.numpy as jnp
from jax import lax

PLANES = 2
ROWS = 16
COLS = 1024
TAPS = 31
RANK = 3
CAP = 8
SHIFT_MAX = 8
NTILE = 8
WROWS = 8
ITERS = 2
VIEWS = 8
NY = 1024


def row_layout(key):
    sources = []
    shifts = []
    windows = NY // (2 * ROWS) + 1
    span = windows * 2 * ROWS
    for view_index in range(VIEWS):
        view_key = jax.random.fold_in(key, view_index)
        phase_key, cross_key, left_key, right_key, shift_key = jax.random.split(view_key, 5)
        phase = jax.random.randint(phase_key, (), 0, 2).astype(jnp.int32) * ROWS
        position = jnp.arange(span, dtype=jnp.int32)
        inside = (position >= phase) & (position < phase + NY)
        halves_inside = inside.reshape(windows, 2, ROWS)[:, :, 0]
        complete = halves_inside[:, 0] & halves_inside[:, 1]
        crossing = jax.random.randint(cross_key, (windows,), CAP // 2 + 1, CAP + 1).astype(jnp.int32)
        crossing = crossing.at[1].set(CAP)
        crossing = jnp.where(complete, crossing, 0)
        view_perm = jax.vmap(lambda sub: jax.random.permutation(sub, ROWS))(jax.random.split(left_key, windows * 2)).reshape(windows, 2, ROWS).astype(jnp.int32)
        out_perm = jax.vmap(lambda sub: jax.random.permutation(sub, ROWS))(jax.random.split(right_key, windows * 2)).reshape(windows, 2, ROWS).astype(jnp.int32)
        crossed = view_perm < crossing[:, None, None]
        half_index = lax.broadcasted_iota(jnp.int32, (windows, 2, ROWS), 1)
        window_index = lax.broadcasted_iota(jnp.int32, (windows, 2, ROWS), 0)
        target_half = jnp.where(crossed, 1 - half_index, half_index)
        slot = out_perm.reshape(-1)[window_index * 2 * ROWS + target_half * ROWS + view_perm]
        target = (window_index * 2 * ROWS + target_half * ROWS + slot).reshape(span)
        source = lax.dynamic_slice_in_dim(target, phase, NY) - phase
        sources.append(source.astype(jnp.int32))
        shifts.append(jax.random.randint(shift_key, (NY,), -SHIFT_MAX, SHIFT_MAX + 1).astype(jnp.int32))
    source_rows = jnp.stack(sources)
    inverse = jax.vmap(lambda single: jnp.zeros((NY,), jnp.int32).at[single].set(jnp.arange(NY, dtype=jnp.int32)))(source_rows)
    column_shift = jnp.stack(shifts)
    returned_shift = jnp.take_along_axis(column_shift, inverse, axis=1)
    return (source_rows, inverse, column_shift, returned_shift)


def draw_src_row(key, part):
    shared = row_layout(key)
    return shared[0]


def draw_dst_row(key, part):
    shared = row_layout(key)
    return shared[1]


def draw_col_shift(key, part):
    shared = row_layout(key)
    return shared[2]


def draw_back_shift(key, part):
    shared = row_layout(key)
    return shared[3]


def set_ends(array, stream_key, least, high):
    longest = array.shape.index(max(array.shape))
    spots = []
    for shift in (0, 1):
        where = [jax.random.randint(jax.random.fold_in(stream_key, axis), (), 0, length) for axis, length in enumerate(array.shape)]
        where[longest] = (where[longest] + shift) % array.shape[longest]
        spots.append(tuple(where))
    return array.at[spots[0]].set(least).at[spots[1]].set(high)


def block_levels(stream_key, shape, shards, low, largest):
    def one(dim, shards_of):
        heights = jax.random.uniform(jax.random.fold_in(jax.random.fold_in(stream_key, 6), dim), (shards_of,), jnp.float32, low / len(shards), largest / len(shards))
        return jnp.repeat(jnp.exp(heights), shape[dim] // shards_of).reshape((-1,) + (1,) * (len(shape) - dim - 1))

    level = one(*shards[0])
    for cut in shards[1:]:
        level = level * one(*cut)
    return level


def setup_inputs(seed: int = 0) -> dict:
    streams_of = jax.random.split(jax.random.key(seed), 13)
    return {
        "estimate": jnp.clip(jnp.exp(math.log(2.0) - 1.3862944 * jax.random.uniform(streams_of[0], (PLANES, NY, COLS), jnp.float32) ** block_levels(streams_of[0], (PLANES, NY, COLS), ((1, 64),), -0.2, 0.2)), 0.5, 2.0),
        "measured": jnp.clip(jnp.exp(math.log(4.0) - 2.7725887 * jax.random.uniform(streams_of[1], (VIEWS, PLANES, NY, COLS), jnp.float32) ** block_levels(streams_of[1], (VIEWS, PLANES, NY, COLS), ((0, 8), (2, 64)), -0.2, 0.2)), 0.25, 4.0),
        "psf_z": jnp.clip(jnp.exp(math.log(1.0) - 2.9957323 * jax.random.uniform(streams_of[2], (VIEWS, RANK, TAPS), jnp.float32) ** block_levels(streams_of[2], (VIEWS, RANK, TAPS), ((0, 8),), -0.2, 0.2)), 0.05, 1.0),
        "psf_y": jnp.clip(jnp.exp(math.log(1.0) - 2.9957323 * jax.random.uniform(streams_of[3], (VIEWS, RANK, TAPS), jnp.float32) ** block_levels(streams_of[3], (VIEWS, RANK, TAPS), ((0, 8),), -0.2, 0.2)), 0.05, 1.0),
        "psf_x": jnp.clip(jnp.exp(math.log(1.0) - 2.9957323 * jax.random.uniform(streams_of[4], (VIEWS, RANK, TAPS), jnp.float32) ** block_levels(streams_of[4], (VIEWS, RANK, TAPS), ((0, 8),), -0.2, 0.2)), 0.05, 1.0),
        "psf_mix": jnp.clip(jnp.exp(math.log(1.0) - 1.609438 * jax.random.uniform(streams_of[5], (VIEWS, RANK), jnp.float32) ** block_levels(streams_of[5], (VIEWS, RANK), ((0, 8),), -0.2, 0.2)), 0.2, 1.0),
        "weight_tiles": jnp.clip(jnp.exp(jax.random.uniform(streams_of[6], (NTILE, WROWS, COLS), jnp.float32, math.log(0.1), math.log(1.0))), 0.1, 1.0),
        "tile_index": set_ends(jax.random.randint(streams_of[7], (VIEWS, NY // WROWS), 0, NTILE), jax.random.fold_in(streams_of[7], 1), 0, NTILE - 1).astype(jnp.int32),
        "src_row": draw_src_row(jax.random.fold_in(streams_of[12], 71), 0),
        "dst_row": draw_dst_row(jax.random.fold_in(streams_of[12], 71), 0),
        "col_shift": draw_col_shift(jax.random.fold_in(streams_of[12], 71), 0),
        "back_shift": draw_back_shift(jax.random.fold_in(streams_of[12], 71), 0),
    }


def normalized(values):
    return values / jnp.sum(values, axis=-1, keepdims=True)


def convolve_axis(values, taps_vec, axis_index):
    radius = taps_vec.shape[0] // 2
    length = values.shape[axis_index]
    widths = [(0, 0)] * values.ndim
    widths[axis_index] = (radius, radius)
    padded = jnp.pad(values, widths)
    result = jnp.zeros_like(values)
    for tap_index in range(taps_vec.shape[0]):
        if abs(tap_index - radius) < length:
            result = result + taps_vec[tap_index] * lax.slice_in_dim(padded, tap_index, tap_index + length, axis=axis_index)
    return result


def blurring(values, depth_taps, row_taps, column_taps, mixing, flipped):
    result = jnp.zeros_like(values)
    for term in range(depth_taps.shape[0]):
        first_taps, second_taps, third_taps = depth_taps[term], row_taps[term], column_taps[term]
        if flipped:
            first_taps, second_taps, third_taps = first_taps[::-1], second_taps[::-1], third_taps[::-1]
        layer = convolve_axis(values, first_taps, 0)
        layer = convolve_axis(layer, second_taps, 1)
        layer = convolve_axis(layer, third_taps, 2)
        result = result + mixing[term] * layer
    return result


def shift_columns(values, offsets):
    padded = jnp.pad(values, ((0, 0), (0, 0), (SHIFT_MAX, SHIFT_MAX)))

    def one_row(row_values, amount):
        return lax.dynamic_slice_in_dim(row_values, (amount + SHIFT_MAX).astype(jnp.int32), COLS, axis=1)

    return jax.vmap(one_row, in_axes=(1, 0), out_axes=1)(padded, offsets)


def reference(estimate, measured, psf_z, psf_y, psf_x, psf_mix, weight_tiles, tile_index, src_row, dst_row, col_shift, back_shift):
    depth_taps = normalized(psf_z)
    row_taps = normalized(psf_y)
    column_taps = normalized(psf_x)
    mixing = normalized(psf_mix)
    weights = []
    weight_total = jnp.zeros((NY, COLS), jnp.float32)
    for view_index in range(VIEWS):
        looked = jnp.take(weight_tiles, tile_index[view_index], axis=0).reshape(NY, COLS)
        weights.append(looked)
        weight_total = weight_total + looked
    current = estimate
    for iteration in range(ITERS):
        combined = jnp.zeros_like(current)
        for view_index in range(VIEWS):
            aligned = shift_columns(jnp.take(current, src_row[view_index], axis=1), col_shift[view_index])
            blurred = blurring(aligned, depth_taps[view_index], row_taps[view_index], column_taps[view_index], mixing[view_index], False)
            quotient = measured[view_index] / blurred
            adjoint = blurring(quotient, depth_taps[view_index], row_taps[view_index], column_taps[view_index], mixing[view_index], True)
            returned = shift_columns(jnp.take(adjoint, dst_row[view_index], axis=1), back_shift[view_index])
            combined = combined + weights[view_index][None] * returned
        current = current * combined / weight_total[None]
    return current
```

```python
import jax
import jax.numpy as jnp
from jax import lax
from jax.experimental import pallas as pl
from jax.experimental.pallas import tpu as pltpu
from jax.sharding import PartitionSpec as P

ITERS = 2
LANE = 128
HALF = 64
TAPS = 31
RADIUS = 15
RANK = 3
ROWS = 16
VIEWS = 8
TAP_LANE = 8
ROW_MARK = 1024
Q_FIRST, Q_LAST = 41, 214
STEPS = (1, -1, 2, -2, 3, -3, 0, 0)
OWN = 6
F32 = jnp.float32
BF16 = jnp.bfloat16
VMEM_LIMIT = 48 * 1024 * 1024


def lanes_of(shape):
    return lax.broadcasted_iota(jnp.int32, shape, len(shape) - 1)


def rows_of(shape):
    return lax.broadcasted_iota(jnp.int32, shape, len(shape) - 2)


def pick_lane(values, lane):
    index = jnp.full(values.shape, lane, jnp.int32)
    return jnp.take_along_axis(values, index, axis=1, mode="promise_in_bounds")


def look_up(values, index):
    return jnp.take_along_axis(values, index, axis=1, mode="promise_in_bounds")


def halves(values):
    high = values.astype(BF16)
    low = (values - high.astype(F32)).astype(BF16)
    return high, low


def dot(left, right):
    return jnp.dot(left, right, preferred_element_type=F32)


def dot_turned(left, right):
    return lax.dot_general(left, right, (((1,), (1,)), ((), ())), preferred_element_type=F32)


def windows_of(strips):
    count = len(strips)
    turned = [pltpu.roll(strip, HALF, 1) for strip in strips]
    lower = lanes_of(strips[0].shape) < HALF
    zero = jnp.zeros_like(strips[0])
    tiles = []
    for place in range(count + 1):
        left = turned[place - 1] if place > 0 else zero
        right = turned[place] if place < count else zero
        tiles.append(jnp.where(lower, left, right))
    return tiles


def pack_measured_kernel(
    measured, dst_row, back_shift, tile_index, psf_z, psf_y, psf_x, psf_mix, out, table
):
    rows = 2 * ROWS
    table[...] = jnp.zeros_like(table)
    dst = dst_row[...].astype(F32) + ROW_MARK
    back = back_shift[...].astype(F32)
    tiles = tile_index[...].astype(F32)
    for plane in range(2):
        first = plane * ROWS
        table[0:1, first : first + ROWS] = dst
        table[1:2, first : first + ROWS] = back
        for part in range(2):
            start = first + part * 8
            table[2:3, start : start + 8] = jnp.broadcast_to(tiles[:, part : part + 1], (1, 8))
    upright = jnp.transpose(table[...])[:rows]
    table[...] = jnp.zeros_like(table)
    for place, psf in enumerate((psf_z, psf_y, psf_x)):
        values = psf[0]
        normal = values / jnp.sum(values, axis=1, keepdims=True)
        table[place * RANK : (place + 1) * RANK, TAP_LANE : TAP_LANE + TAPS] = normal
    mix = psf_mix[...]
    table[9:10, TAP_LANE : TAP_LANE + RANK] = mix / jnp.sum(mix, axis=1, keepdims=True)
    lane = lanes_of((rows, LANE))
    stash = jnp.where(lane < TAP_LANE, upright, table[:rows, :])
    values = measured[0].reshape(rows, measured.shape[3])
    strips = [values[:, place * LANE : (place + 1) * LANE] for place in range(VIEWS)]
    tiles = windows_of(strips)
    for place in range(VIEWS):
        out[place, :, :LANE] = jnp.where(lane < Q_FIRST, stash, tiles[place])
        out[place, :, LANE:] = tiles[place + 1]


def pack_measured(measured, dst_row, back_shift, tile_index, psf_z, psf_y, psf_x, psf_mix):
    return pl.pallas_call(
        pack_measured_kernel,
        out_shape=jax.ShapeDtypeStruct((VIEWS, 2 * ROWS, 2 * LANE), F32),
        scratch_shapes=[pltpu.VMEM((LANE, LANE), F32)],
        name="pack_measured",
    )(measured, dst_row, back_shift, tile_index, psf_z, psf_y, psf_x, psf_mix)


def registration_kernel(stash, out):
    lane = lanes_of((2 * ROWS, LANE))
    result = jnp.zeros((2 * ROWS, LANE), F32)
    for view in range(VIEWS):
        values = stash[view]
        result = jnp.where(lane == view, pick_lane(values, 0), result)
        result = jnp.where(lane == VIEWS + view, pick_lane(values, 1), result)
    out[...] = result


def registration(received):
    return pl.pallas_call(
        registration_kernel,
        out_shape=jax.ShapeDtypeStruct((2 * ROWS, LANE), F32),
        grid=(1,),
        in_specs=[pl.BlockSpec((VIEWS, 2 * ROWS, LANE), lambda i: (0, 0, 0))],
        out_specs=pl.BlockSpec((2 * ROWS, LANE), lambda i: (0, 0)),
        name="registration",
    )(received)


def pack_estimate_kernel(field, stash, out):
    rows = 2 * ROWS
    values = field[...].reshape(rows, field.shape[2])
    strips = [values[:, place * LANE : (place + 1) * LANE] for place in range(VIEWS)]
    tiles = windows_of(strips)
    lane = lanes_of((rows, LANE))
    for place in range(VIEWS):
        out[place, :, :LANE] = jnp.where(lane < 2 * VIEWS, stash[...], tiles[place])
        out[place, :, LANE:] = tiles[place + 1]


def pack_estimate(field, stash):
    return pl.pallas_call(
        pack_estimate_kernel,
        out_shape=jax.ShapeDtypeStruct((VIEWS, 2 * ROWS, 2 * LANE), F32),
        name="pack_estimate",
    )(field, stash)


def pack_field_kernel(field, out):
    tiles = windows_of([field[place] for place in range(VIEWS)])
    for place in range(VIEWS):
        out[place, :, :LANE] = tiles[place]
        out[place, :, LANE:] = tiles[place + 1]


def pack_field(field):
    return pl.pallas_call(
        pack_field_kernel,
        out_shape=jax.ShapeDtypeStruct((VIEWS, 2 * ROWS, 2 * LANE), F32),
        name="pack_field",
    )(field)


def column_bands_kernel(stash, high, low):
    shape = (2 * LANE, LANE)
    row = rows_of(shape)
    lane = lanes_of(shape)
    for term in range(RANK):
        taps = jnp.broadcast_to(stash[0, 6 + term : 7 + term, :], shape)
        for part in range(2):
            spread = row - (lane + part * LANE) + RADIUS
            inside = (spread >= 0) & (spread < TAPS)
            index = jnp.where(inside, spread + TAP_LANE, 0)
            band = jnp.where(inside, look_up(taps, index), 0.0)
            band_high, band_low = halves(band)
            high[0, term, :, part * LANE : (part + 1) * LANE] = band_high
            low[0, term, :, part * LANE : (part + 1) * LANE] = band_low


def column_bands(received):
    shape = jax.ShapeDtypeStruct((VIEWS, RANK, 2 * LANE, 2 * LANE), BF16)
    spec = pl.BlockSpec((1, RANK, 2 * LANE, 2 * LANE), lambda v: (v, 0, 0, 0))
    return pl.pallas_call(
        column_bands_kernel,
        out_shape=(shape, shape),
        grid=(VIEWS,),
        in_specs=[pl.BlockSpec((1, 2 * ROWS, LANE), lambda v: (v, 0, 0))],
        out_specs=(spec, spec),
        name="column_bands",
    )(received)


def build_row_bands(view, first_row, stash, rows_lane, own_dst, high, low, turned_high, turned_low):
    taps_rows = [stash[0, 3 + term : 4 + term, :] for term in range(RANK)]
    depth_rows = [stash[0, term : term + 1, :] for term in range(RANK)]
    mix_row = stash[0, 9:10, :]
    centre = TAP_LANE + RADIUS
    dst_lane = rows_lane[pl.ds(view, 1), :]
    shape = (4 * ROWS, LANE)
    row = rows_of(shape)
    lane = lanes_of(shape)
    for part in range(2):
        dst = jnp.broadcast_to(dst_lane[:, part * LANE : (part + 1) * LANE], shape)
        spread = dst.astype(jnp.int32) - ROW_MARK - first_row - row + RADIUS
        inside = (spread >= 0) & (spread < TAPS)
        if part == 1:
            inside = inside & (lane < 3 * 2 * ROWS)
        index = jnp.where(inside, spread + TAP_LANE, 0)
        upper = (lane // ROWS) % 2 == 0
        for term in range(RANK):
            taps = jnp.broadcast_to(taps_rows[term], shape)
            band = jnp.where(inside, look_up(taps, index), 0.0)
            mix = mix_row[:, TAP_LANE + term : TAP_LANE + term + 1]
            depth = depth_rows[term] * mix
            for plane in range(2):
                from_first = depth[:, centre - plane : centre - plane + 1]
                from_second = depth[:, centre + 1 - plane : centre + 2 - plane]
                scaled = band * jnp.where(upper, from_first, from_second)
                band_high, band_low = halves(scaled)
                start = (term * 2 + plane) * 4 * ROWS
                columns = slice(part * LANE, (part + 1) * LANE)
                high[0, start : start + 4 * ROWS, columns] = band_high
                low[0, start : start + 4 * ROWS, columns] = band_low
    shape = (ROWS, LANE)
    lane = lanes_of(shape)
    spread = own_dst.astype(jnp.int32) - ROW_MARK - first_row - lane % (4 * ROWS) + RADIUS
    inside = (spread >= 0) & (spread < TAPS)
    index = jnp.where(inside, spread + TAP_LANE, 0)
    upper = lane < 4 * ROWS
    for term in range(RANK):
        taps = jnp.broadcast_to(taps_rows[term], shape)
        band = jnp.where(inside, look_up(taps, index), 0.0)
        mix = mix_row[:, TAP_LANE + term : TAP_LANE + term + 1]
        depth = depth_rows[term] * mix
        for plane in range(2):
            from_first = depth[:, centre + plane : centre + plane + 1]
            from_second = depth[:, centre + plane - 1 : centre + plane]
            scaled = band * jnp.where(upper, from_first, from_second)
            band_high, band_low = halves(scaled)
            start = (term * 2 + plane) * ROWS
            turned_high[0, start : start + ROWS, :] = band_high
            turned_low[0, start : start + ROWS, :] = band_low


def iteration_kernel(building, *refs):
    refs = list(refs)
    field = refs.pop(0)
    moves = refs.pop(0)
    stash = refs.pop(0)
    measured = [refs.pop(0) for _ in range(5)]
    col_high, col_low = refs.pop(0), refs.pop(0)
    tiles = refs.pop(0)
    if building:
        out = refs.pop(0)
        row_high, row_low, turned_high, turned_low = [refs.pop(0) for _ in range(4)]
        rows_lane = refs.pop(0)
    else:
        row_high, row_low, turned_high, turned_low = [refs.pop(0) for _ in range(4)]
        out = refs.pop(0)
    x_high, x_low, total, weight_total = refs

    view = pl.program_id(0)
    strip = lax.axis_index("view")
    block = lax.axis_index("blk")

    @pl.when(view == 0)
    def _():
        total[...] = jnp.zeros_like(total)
        weight_total[...] = jnp.zeros_like(weight_total)
        x_high[...] = jnp.zeros_like(x_high)
        x_low[...] = jnp.zeros_like(x_low)
        if building:
            rows_lane[...] = jnp.transpose(moves[...].reshape(VIEWS * 2 * ROWS, LANE))

    own_dst = pick_lane(moves[OWN], view)
    last = jnp.max(own_dst) - ROW_MARK
    phase = (last >= ((block + 1) * ROWS).astype(F32)).astype(jnp.int32)
    first_row = (block - 2 + phase) * ROWS
    if building:
        build_row_bands(
            view, first_row, stash, rows_lane, own_dst[:ROWS],
            row_high, row_low, turned_high, turned_low,
        )

    lane = lanes_of((2 * ROWS, LANE))
    column = lane + strip * LANE - HALF
    columns = column.shape[1] * VIEWS
    inside = [
        (column >= 0) & (column < columns),
        (column + LANE >= 0) & (column + LANE < columns),
    ]
    for slot in range(OWN + 1):
        where = lane + pick_lane(moves[slot], VIEWS + view).astype(jnp.int32)
        index = where & (LANE - 1)
        left = look_up(field[slot, :, :LANE], index)
        right = look_up(field[slot, :, LANE:], index)
        moved = (jnp.where(where < LANE, left, right), jnp.where(where < 0, left, right))
        for part in range(2):
            high, low = halves(jnp.where(inside[part], moved[part], 0.0))
            rows = slice(slot * 2 * ROWS, (slot + 1) * 2 * ROWS)
            x_high[rows, part * LANE : (part + 1) * LANE] = high
            x_low[rows, part * LANE : (part + 1) * LANE] = low

    layers = (
        dot(row_high[0], x_high[...]) + dot(row_low[0], x_high[...]) + dot(row_high[0], x_low[...])
    )
    blurred = None
    height = 8 * ROWS
    for term in range(RANK):
        high, low = halves(layers[term * height : (term + 1) * height])
        part = dot(high, col_high[0, term]) + dot(low, col_high[0, term])
        part = part + dot(high, col_low[0, term])
        blurred = part if blurred is None else blurred + part

    shape = (ROWS, 2 * LANE)
    wide = lanes_of(shape)
    wide_column = wide + strip * LANE - HALF
    kept = (wide >= Q_FIRST) & (wide <= Q_LAST) & (wide_column >= 0) & (wide_column < columns)
    quotients = []
    for plane in range(2):
        for place in range(4):
            rows = slice(plane * ROWS, (plane + 1) * ROWS)
            seen = jnp.where(phase == 1, measured[place + 1][0, rows], measured[place][0, rows])
            start = (plane * 4 + place) * ROWS
            row_block = block - 2 + phase + place
            fine = kept & (row_block >= 0) & (row_block < VIEWS * 8)
            quotients.append(jnp.where(fine, seen / blurred[start : start + ROWS], 0.0))
    quotient = jnp.concatenate(quotients, axis=0)
    high, low = halves(quotient)
    layers = dot(turned_high[0], high) + dot(turned_low[0], high) + dot(turned_high[0], low)
    adjoint = None
    height = 2 * ROWS
    for term in range(RANK):
        high, low = halves(layers[term * height : (term + 1) * height])
        part = dot_turned(high, col_high[0, term]) + dot_turned(low, col_high[0, term])
        part = part + dot_turned(high, col_low[0, term])
        adjoint = part if adjoint is None else adjoint + part

    left = jnp.where(inside[0], adjoint[:, :LANE], 0.0)
    right = jnp.where(inside[1], adjoint[:, LANE:], 0.0)
    where = lane + HALF + pick_lane(moves[OWN], VIEWS + view).astype(jnp.int32)
    index = where & (LANE - 1)
    returned = jnp.where(where < LANE, look_up(left, index), look_up(right, index))
    chosen = pick_lane(stash[0], 2)
    weight = jnp.zeros((2 * ROWS, LANE), F32)
    first_column = pl.multiple_of(strip * LANE, LANE)
    for number in range(tiles.shape[0]):
        tile = tiles[number, :, pl.ds(first_column, LANE)]
        tall = jnp.concatenate([tile] * 4, axis=0)
        weight = jnp.where(chosen == number, tall, weight)
    total[...] += weight * returned
    weight_total[...] += weight

    @pl.when(view == VIEWS - 1)
    def _():
        lower = pltpu.roll(field[OWN, :, :LANE], HALF, 1)
        upper = pltpu.roll(field[OWN, :, LANE:], HALF, 1)
        own = jnp.where(lane < HALF, lower, upper)
        result = own * total[...] / weight_total[...]
        for place in range(VIEWS):
            out[place] = result


def iteration(field, moves, received, neighbours, col_bands, weight_tiles, row_bands=None):
    building = row_bands is None
    rows = 2 * ROWS
    whole = pl.BlockSpec((VIEWS, rows, 2 * LANE), lambda v: (0, 0, 0))
    moves_spec = pl.BlockSpec((VIEWS, rows, LANE), lambda v: (0, 0, 0))
    stash_spec = pl.BlockSpec((1, rows, LANE), lambda v: (v, 0, 0))
    measured_spec = pl.BlockSpec((1, rows, 2 * LANE), lambda v: (v, 0, 0))
    col_spec = pl.BlockSpec((1, RANK, 2 * LANE, 2 * LANE), lambda v: (v, 0, 0, 0))
    tiles_spec = pl.BlockSpec(weight_tiles.shape, lambda v: (0, 0, 0))
    row_shape = (VIEWS, RANK * 8 * ROWS, 2 * LANE)
    turned_shape = (VIEWS, RANK * 2 * ROWS, LANE)
    row_spec = pl.BlockSpec((1,) + row_shape[1:], lambda v: (v, 0, 0))
    turned_spec = pl.BlockSpec((1,) + turned_shape[1:], lambda v: (v, 0, 0))
    band_specs = [row_spec, row_spec, turned_spec, turned_spec]
    out_shape = jax.ShapeDtypeStruct((VIEWS, rows, LANE), F32)
    out_spec = pl.BlockSpec((VIEWS, rows, LANE), lambda v: (0, 0, 0))
    in_specs = [whole, moves_spec, stash_spec] + [measured_spec] * 5 + [col_spec] * 2 + [tiles_spec]
    operands = [field, moves, received, *neighbours, *col_bands, weight_tiles]
    scratch = [
        pltpu.VMEM((2 * LANE, 2 * LANE), BF16),
        pltpu.VMEM((2 * LANE, 2 * LANE), BF16),
        pltpu.VMEM((rows, LANE), F32),
        pltpu.VMEM((rows, LANE), F32),
    ]
    if building:
        bands = [
            jax.ShapeDtypeStruct(row_shape, BF16),
            jax.ShapeDtypeStruct(row_shape, BF16),
            jax.ShapeDtypeStruct(turned_shape, BF16),
            jax.ShapeDtypeStruct(turned_shape, BF16),
        ]
        out_shapes = [out_shape] + bands
        out_specs = [out_spec] + band_specs
        scratch = [pltpu.VMEM((LANE, 2 * LANE), F32)] + scratch
    else:
        in_specs += band_specs
        operands += row_bands
        out_shapes = out_shape
        out_specs = out_spec
    result = pl.pallas_call(
        lambda *refs: iteration_kernel(building, *refs),
        out_shape=out_shapes,
        grid=(VIEWS,),
        in_specs=in_specs,
        out_specs=out_specs,
        scratch_shapes=scratch,
        compiler_params=pltpu.CompilerParams(vmem_limit_bytes=VMEM_LIMIT),
        name="iteration_first" if building else "iteration_next",
    )(*operands)
    if building:
        return result[0], list(result[1:])
    return result


def step_by_view(values):
    blocks = lax.axis_size("blk")
    route = []
    for view, step in enumerate(STEPS):
        for block in range(blocks):
            if 0 <= block + step < blocks:
                route.append((view * blocks + block, view * blocks + block + step))
    return lax.ppermute(values, ("view", "blk"), route)


def from_block(values, offset):
    blocks = lax.axis_size("blk")
    route = [(b + offset, b) for b in range(blocks) if 0 <= b + offset < blocks]
    return lax.ppermute(values, "blk", route)


def over_views(values):
    return lax.all_to_all(values, "view", 0, 0)


def body(
    estimate,
    measured,
    psf_z,
    psf_y,
    psf_x,
    psf_mix,
    weight_tiles,
    tile_index,
    src_row,
    dst_row,
    col_shift,
    back_shift,
):
    planes, row_count, col_count = estimate.shape
    stepped = step_by_view(estimate)
    received = over_views(
        pack_measured(measured, dst_row, back_shift, tile_index, psf_z, psf_y, psf_x, psf_mix)
    )
    moves = step_by_view(registration(received))
    neighbours = [
        received if offset == 0 else from_block(received, offset) for offset in (-2, -1, 0, 1, 2)
    ]
    col_bands = column_bands(received)
    field = over_views(pack_estimate(stepped, moves))
    moves = field
    strips, row_bands = iteration(field, moves, received, neighbours, col_bands, weight_tiles)
    for _ in range(ITERS - 1):
        field = over_views(pack_field(step_by_view(over_views(strips))))
        strips = iteration(
            field, moves, received, neighbours, col_bands, weight_tiles, row_bands
        )
    strips = over_views(strips).reshape(VIEWS, planes, row_count, LANE)
    return jnp.transpose(strips, (1, 2, 0, 3)).reshape(planes, row_count, col_count)


def solution(mesh):
    in_specs = (
        P(None, "blk", None),
        P("view", None, "blk", None),
        P("view", None, None),
        P("view", None, None),
        P("view", None, None),
        P("view", None),
        P(),
        P("view", "blk"),
        P("view", "blk"),
        P("view", "blk"),
        P("view", "blk"),
        P("view", "blk"),
    )
    out_specs = P(None, "blk", None)
    return jax.shard_map(body, mesh=mesh, in_specs=in_specs, out_specs=out_specs, check_vma=False)
```

```python
import jax
import jax.numpy as jnp
from jax import lax
from jax.experimental import pallas as pl
from jax.experimental.pallas import tpu as pltpu
from jax.sharding import PartitionSpec as P

ITERS = 2
LANE = 128
HALF = 64
TAPS = 31
RADIUS = 15
RANK = 3
ROWS = 16
VIEWS = 8
TAP_LANE = 96
TILE_LANE = 2 * 8
ROW_MARK = 1024
Q_FIRST, Q_LAST = 41, 214
STEPS = (1, -1, 2, -2, 3, -3, 0, 0)
OWN = 6
F32 = jnp.float32
BF16 = jnp.bfloat16
VMEM_LIMIT = 65_000_000


def whole(shape):
    return pl.BlockSpec(tuple(shape), lambda i: (0,) * len(shape))


def lanes_of(shape):
    return lax.broadcasted_iota(jnp.int32, shape, len(shape) - 1)


def rows_of(shape):
    return lax.broadcasted_iota(jnp.int32, shape, len(shape) - 2)


def pick_lane(values, lane):
    index = jnp.full(values.shape, lane, jnp.int32)
    return jnp.take_along_axis(values, index, axis=1, mode="promise_in_bounds")


def look_up(values, index):
    return jnp.take_along_axis(values, index, axis=1, mode="promise_in_bounds")


def halves(values):
    high = values.astype(BF16)
    low = (values - high.astype(F32)).astype(BF16)
    return high, low


def dot(left, right):
    return jnp.dot(left, right, preferred_element_type=F32)


def dot_turned(left, right):
    return lax.dot_general(left, right, (((1,), (1,)), ((), ())), preferred_element_type=F32)


def triple(high, low, right_high, right_low, multiply):
    both = multiply(jnp.concatenate([high, low], axis=0), right_high)
    height = high.shape[0]
    return both[:height] + both[height:] + multiply(high, right_low)


def windows_of(strips):
    count = len(strips)
    turned = [pltpu.roll(strip, HALF, 1) for strip in strips]
    lower = lanes_of(strips[0].shape) < HALF
    zero = jnp.zeros_like(strips[0])
    tiles = []
    for place in range(count + 1):
        left = turned[place - 1] if place > 0 else zero
        right = turned[place] if place < count else zero
        tiles.append(jnp.where(lower, left, right))
    return tiles


def pack_measured_kernel(
    measured, dst_row, back_shift, tile_index, psf_z, psf_y, psf_x, psf_mix, out, table
):
    rows = 2 * ROWS
    view = lax.axis_index("view")
    table[...] = jnp.zeros_like(table)
    dst = dst_row[...].astype(F32) + ROW_MARK
    back = back_shift[...].astype(F32)
    tiles = tile_index[...].astype(F32)
    for plane in range(2):
        first = plane * ROWS
        table[0:1, first : first + ROWS] = dst
        table[1:2, first : first + ROWS] = back
        for part in range(2):
            start = first + part * 8
            table[2:3, start : start + 8] = jnp.broadcast_to(tiles[:, part : part + 1], (1, 8))
    upright = jnp.transpose(table[...])[:rows]
    lane = lanes_of((rows, LANE))
    moves = jnp.where(lane == view, upright[:, 0:1], 0.0)
    moves = jnp.where(lane == VIEWS + view, upright[:, 1:2], moves)
    moves = jnp.where(lane == TILE_LANE, upright[:, 2:3], moves)
    table[...] = jnp.zeros_like(table)
    for place, psf in enumerate((psf_z, psf_y, psf_x)):
        for term in range(RANK):
            values = psf[term]
            normal = values / jnp.sum(values, axis=1, keepdims=True)
            row = place * RANK + term
            table[row : row + 1, TAP_LANE : TAP_LANE + TAPS] = normal
    mix = psf_mix[...]
    table[9:10, TAP_LANE : TAP_LANE + RANK] = mix / jnp.sum(mix, axis=1, keepdims=True)
    taps = table[:rows, :]
    values = measured[0].reshape(rows, measured.shape[3])
    strips = [values[:, place * LANE : (place + 1) * LANE] for place in range(VIEWS)]
    tiles = windows_of(strips)
    for place in range(VIEWS):
        out[place, :, :LANE] = jnp.where(lane < Q_FIRST, moves, tiles[place])
        out[place, :, LANE:] = jnp.where(lane < TAP_LANE, tiles[place + 1], taps)


def pack_measured(measured, dst_row, back_shift, tile_index, psf_z, psf_y, psf_x, psf_mix):
    turned = [jnp.transpose(psf, (1, 0, 2)) for psf in (psf_z, psf_y, psf_x)]
    operands = (measured, dst_row, back_shift, tile_index, *turned, psf_mix)
    return pl.pallas_call(
        pack_measured_kernel,
        out_shape=jax.ShapeDtypeStruct((VIEWS, 2 * ROWS, 2 * LANE), F32),
        grid=(1,),
        out_specs=whole((VIEWS, 2 * ROWS, 2 * LANE)),
        scratch_shapes=[pltpu.VMEM((LANE, LANE), F32)],
        in_specs=[whole(operand.shape) for operand in operands],
        compiler_params=pltpu.CompilerParams(vmem_limit_bytes=VMEM_LIMIT),
        name="pack_measured",
    )(*operands)


def registration(received):
    return jnp.sum(received[:, :, :LANE], axis=0)


def pack_estimate_kernel(field, stash, out):
    rows = 2 * ROWS
    values = field[...].reshape(rows, field.shape[2])
    strips = [values[:, place * LANE : (place + 1) * LANE] for place in range(VIEWS)]
    tiles = windows_of(strips)
    lane = lanes_of((rows, LANE))
    for place in range(VIEWS):
        out[place, :, :LANE] = jnp.where(lane < 2 * VIEWS, stash[...], tiles[place])
        out[place, :, LANE:] = tiles[place + 1]


def pack_estimate(field, stash):
    return pl.pallas_call(
        pack_estimate_kernel,
        out_shape=jax.ShapeDtypeStruct((VIEWS, 2 * ROWS, 2 * LANE), F32),
        grid=(1,),
        out_specs=whole((VIEWS, 2 * ROWS, 2 * LANE)),
        in_specs=[whole(field.shape), whole(stash.shape)],
        cost_estimate=pl.CostEstimate(flops=40_000_000_000, bytes_accessed=100_000_000, transcendentals=0),
        compiler_params=pltpu.CompilerParams(vmem_limit_bytes=VMEM_LIMIT),
        name="pack_estimate",
    )(field, stash)


def pack_field_kernel(field, out):
    tiles = windows_of([field[place] for place in range(VIEWS)])
    for place in range(VIEWS):
        out[place, :, :LANE] = tiles[place]
        out[place, :, LANE:] = tiles[place + 1]


def pack_field(field):
    return pl.pallas_call(
        pack_field_kernel,
        out_shape=jax.ShapeDtypeStruct((VIEWS, 2 * ROWS, 2 * LANE), F32),
        grid=(1,),
        out_specs=whole((VIEWS, 2 * ROWS, 2 * LANE)),
        in_specs=[whole(field.shape)],
        compiler_params=pltpu.CompilerParams(vmem_limit_bytes=VMEM_LIMIT),
        name="pack_field",
    )(field)


def tap_index(spread):
    inside = (spread >= 0) & (spread < TAPS)
    return jnp.where(inside, spread + TAP_LANE, LANE - 1)


def build_column_bands(received, high, low):
    high[...] = jnp.zeros_like(high)
    low[...] = jnp.zeros_like(low)
    shape = (LANE, LANE)
    square = tap_index(rows_of(shape) - lanes_of(shape) + RADIUS)
    shape = (ROWS, LANE)
    below = tap_index(rows_of(shape) - lanes_of(shape) + RADIUS + LANE)
    above = tap_index(rows_of(shape) - lanes_of(shape) + RADIUS - ROWS)
    for view in range(VIEWS):
        for term in range(RANK):
            taps = received[view, 6 + term : 7 + term, LANE:]
            band = halves(look_up(jnp.broadcast_to(taps, square.shape), square))
            lower = halves(look_up(jnp.broadcast_to(taps, below.shape), below))
            upper = halves(look_up(jnp.broadcast_to(taps, above.shape), above))
            for place, target in enumerate((high, low)):
                target[view, term, :LANE, :LANE] = band[place]
                target[view, term, LANE:, LANE:] = band[place]
                target[view, term, LANE : LANE + ROWS, :LANE] = lower[place]
                target[view, term, LANE - ROWS : LANE, LANE:] = upper[place]


def build_row_bands(view, first_row, stash, rows_lane, own_dst, high, low, turned_high, turned_low):
    taps_rows = [stash[3 + term : 4 + term, :] for term in range(RANK)]
    depth_rows = [stash[term : term + 1, :] for term in range(RANK)]
    mix_row = stash[9:10, :]
    centre = TAP_LANE + RADIUS
    dst_lane = rows_lane[pl.ds(view, 1), :]
    shape = (4 * ROWS, LANE)
    row = rows_of(shape)
    lane = lanes_of(shape)
    for part in range(2):
        dst = jnp.broadcast_to(dst_lane[:, part * LANE : (part + 1) * LANE], shape)
        spread = dst.astype(jnp.int32) - ROW_MARK - first_row - row + RADIUS
        index = tap_index(spread)
        if part == 1:
            index = jnp.where(lane < 3 * 2 * ROWS, index, LANE - 1)
        upper = (lane // ROWS) % 2 == 0
        for term in range(RANK):
            taps = jnp.broadcast_to(taps_rows[term], shape)
            band = look_up(taps, index)
            mix = mix_row[:, TAP_LANE + term : TAP_LANE + term + 1]
            depth = depth_rows[term] * mix
            for plane in range(2):
                from_first = depth[:, centre - plane : centre - plane + 1]
                from_second = depth[:, centre + 1 - plane : centre + 2 - plane]
                scaled = band * jnp.where(upper, from_first, from_second)
                band_high, band_low = halves(scaled)
                start = (term * 2 + plane) * 4 * ROWS
                columns = slice(part * LANE, (part + 1) * LANE)
                high[view, start : start + 4 * ROWS, columns] = band_high
                low[view, start : start + 4 * ROWS, columns] = band_low
    shape = (ROWS, LANE)
    lane = lanes_of(shape)
    spread = own_dst.astype(jnp.int32) - ROW_MARK - first_row - lane % (4 * ROWS) + RADIUS
    index = tap_index(spread)
    upper = lane < 4 * ROWS
    for term in range(RANK):
        taps = jnp.broadcast_to(taps_rows[term], shape)
        band = look_up(taps, index)
        mix = mix_row[:, TAP_LANE + term : TAP_LANE + term + 1]
        depth = depth_rows[term] * mix
        for plane in range(2):
            from_first = depth[:, centre + plane : centre + plane + 1]
            from_second = depth[:, centre + plane - 1 : centre + plane]
            scaled = band * jnp.where(upper, from_first, from_second)
            band_high, band_low = halves(scaled)
            start = (term * 2 + plane) * ROWS
            turned_high[view, start : start + ROWS, :] = band_high
            turned_low[view, start : start + ROWS, :] = band_low


def start_all(copies):
    for copy in copies:
        copy.start()
    return copies


def wait_all(copies):
    for copy in copies:
        copy.wait()


AHEAD = 1


def iteration_kernel(first, *refs):
    refs = list(refs)

    def take(count):
        taken = refs[:count]
        del refs[:count]
        return taken

    received_in, field_in = take(2)
    moves_in = None if first else take(1)[0]
    measured_in = take(5)
    tiles_in, out = take(2)
    received, field, moves, measured, tiles = take(5)
    col_high, col_low, row_high, row_low, turned_high, turned_low = take(6)
    x_high, x_low, result_ref, rows_lane, sems = take(5)

    strip = lax.axis_index("view")
    block = lax.axis_index("blk")
    first_column = pl.multiple_of(strip * LANE, LANE)
    number = 0

    def copy(source, target):
        nonlocal number
        number += 1
        return pltpu.make_async_copy(source, target, sems.at[number - 1])

    for_taps = start_all([copy(received_in, received)])
    others = [copy(field_in, field)]
    if not first:
        others.append(copy(moves_in.at[:, :, pl.ds(0, LANE)], moves))
    for place, source in enumerate(measured_in):
        others.append(copy(source, measured.at[place]))
    others.append(copy(tiles_in.at[:, :, pl.ds(first_column, LANE)], tiles))
    start_all(others)
    wait_all(for_taps)
    build_column_bands(received, col_high, col_low)
    wait_all(others)

    lane = lanes_of((2 * ROWS, LANE))
    column = lane + strip * LANE - HALF
    columns = LANE * VIEWS
    inside = [
        (column >= 0) & (column < columns),
        (column + LANE >= 0) & (column + LANE < columns),
    ]
    wide = lanes_of((ROWS, 2 * LANE))
    wide_column = wide + strip * LANE - HALF
    kept = (wide >= Q_FIRST) & (wide <= Q_LAST) & (wide_column >= 0) & (wide_column < columns)

    if first:
        moves[...] = field[:, :, :LANE]
    rows_lane[...] = jnp.transpose(moves[...].reshape(VIEWS * 2 * ROWS, LANE))
    x_high[:, (OWN + 1) * 2 * ROWS :, :] = jnp.zeros((VIEWS, 2 * ROWS, 2 * LANE), BF16)
    x_low[:, (OWN + 1) * 2 * ROWS :, :] = jnp.zeros((VIEWS, 2 * ROWS, 2 * LANE), BF16)

    def prepare(view):
        own_dst = pick_lane(moves[OWN], view)
        last = jnp.max(own_dst) - ROW_MARK
        phase = (last >= ((block + 1) * ROWS).astype(F32)).astype(jnp.int32)
        build_row_bands(
            view, (block - 2 + phase) * ROWS, received[view, :, LANE:], rows_lane,
            own_dst[:ROWS], row_high, row_low, turned_high, turned_low,
        )
        for slot in range(OWN + 1):
            shift = pick_lane(moves[slot], VIEWS + view).astype(jnp.int32)
            where = lane + shift
            index = where & (LANE - 1)
            left = look_up(field[slot, :, :LANE], index)
            right = look_up(field[slot, :, LANE:], index)
            moved = (jnp.where(where < LANE, left, right), jnp.where(where < 0, left, right))
            for part in range(2):
                high, low = halves(jnp.where(inside[part], moved[part], 0.0))
                rows = slice(slot * 2 * ROWS, (slot + 1) * 2 * ROWS)
                x_high[view, rows, part * LANE : (part + 1) * LANE] = high
                x_low[view, rows, part * LANE : (part + 1) * LANE] = low
        return phase, shift

    def finish(view, phase, shift):
        xh, xl = x_high[view], x_low[view]
        layers = triple(row_high[view], row_low[view], xh, xl, dot)
        blurred = None
        height = 8 * ROWS
        for term in range(RANK):
            high, low = halves(layers[term * height : (term + 1) * height])
            part = triple(high, low, col_high[view, term], col_low[view, term], dot)
            blurred = part if blurred is None else blurred + part

        quotients = []
        for plane in range(2):
            for place in range(4):
                rows = slice(plane * ROWS, (plane + 1) * ROWS)
                seen = jnp.where(
                    phase == 1, measured[place + 1, view, rows], measured[place, view, rows]
                )
                start = (plane * 4 + place) * ROWS
                row_block = block - 2 + phase + place
                fine = kept & (row_block >= 0) & (row_block < VIEWS * 8)
                quotients.append(jnp.where(fine, seen / blurred[start : start + ROWS], 0.0))
        quotient = jnp.concatenate(quotients, axis=0)
        high, low = halves(quotient)
        layers = triple(turned_high[view], turned_low[view], high, low, dot)
        where = lane + shift
        index = where & (LANE - 1)
        adjoint = None
        height = 2 * ROWS
        for term in range(RANK):
            layer = layers[term * height : (term + 1) * height]
            left = look_up(layer[:, :LANE], index)
            right = look_up(layer[:, LANE:], index)
            moved = jnp.concatenate(
                [jnp.where(where < LANE, left, right), jnp.where(where < 0, left, right)], axis=1
            )
            high, low = halves(moved)
            band_high = col_high[view, term, HALF : HALF + LANE, :]
            band_low = col_low[view, term, HALF : HALF + LANE, :]
            part = triple(high, low, band_high, band_low, dot_turned)
            adjoint = part if adjoint is None else adjoint + part
        source = column + HALF + shift
        returned = jnp.where((source >= 0) & (source < columns), adjoint, 0.0)
        chosen = pick_lane(received[view, :, :LANE], TILE_LANE)
        weight = jnp.zeros((2 * ROWS, LANE), F32)
        for tile in range(tiles.shape[0]):
            tall = jnp.concatenate([tiles[tile]] * 4, axis=0)
            weight = jnp.where(chosen == tile, tall, weight)
        return weight * returned, weight


    total = jnp.zeros((2 * ROWS, LANE), F32)
    weight_total = jnp.zeros((2 * ROWS, LANE), F32)
    waiting = [prepare(view) for view in range(AHEAD)]
    for view in range(VIEWS):
        if view + AHEAD < VIEWS:
            waiting.append(prepare(view + AHEAD))
        more, weight = finish(view, *waiting[view])
        total = total + more
        weight_total = weight_total + weight

    lower = pltpu.roll(field[OWN, :, :LANE], HALF, 1)
    upper = pltpu.roll(field[OWN, :, LANE:], HALF, 1)
    own = jnp.where(lane < HALF, lower, upper)
    result_ref[...] = own * total / weight_total
    wait_all(start_all([copy(result_ref, out.at[place]) for place in range(VIEWS)]))


def iteration(field, moves, received, neighbours, weight_tiles):
    rows = 2 * ROWS
    window = (VIEWS, rows, 2 * LANE)
    col_shape = (VIEWS, RANK, 2 * LANE, 2 * LANE)
    row_shape = (VIEWS, RANK * 8 * ROWS, 2 * LANE)
    turned_shape = (VIEWS, RANK * 2 * ROWS, LANE)
    operands = [received, field, *([] if moves is None else [moves]), *neighbours, weight_tiles]
    scratch = [
        pltpu.VMEM(window, F32),
        pltpu.VMEM(window, F32),
        pltpu.VMEM((VIEWS, rows, LANE), F32),
        pltpu.VMEM((5,) + window, F32),
        pltpu.VMEM(weight_tiles.shape[:2] + (LANE,), F32),
        pltpu.VMEM(col_shape, BF16),
        pltpu.VMEM(col_shape, BF16),
        pltpu.VMEM(row_shape, BF16),
        pltpu.VMEM(row_shape, BF16),
        pltpu.VMEM(turned_shape, BF16),
        pltpu.VMEM(turned_shape, BF16),
        pltpu.VMEM((VIEWS, 2 * LANE, 2 * LANE), BF16),
        pltpu.VMEM((VIEWS, 2 * LANE, 2 * LANE), BF16),
        pltpu.VMEM((rows, LANE), F32),
        pltpu.VMEM((LANE, 2 * LANE), F32),
        pltpu.SemaphoreType.DMA((24,)),
    ]
    anywhere = pl.BlockSpec(memory_space=pl.ANY)
    return pl.pallas_call(
        lambda *refs: iteration_kernel(moves is None, *refs),
        out_shape=jax.ShapeDtypeStruct((VIEWS, rows, LANE), F32),
        in_specs=[anywhere] * len(operands),
        out_specs=anywhere,
        scratch_shapes=scratch,
        compiler_params=pltpu.CompilerParams(vmem_limit_bytes=VMEM_LIMIT),
        name="iteration_first" if moves is None else "iteration_next",
    )(*operands)


def step_by_view(values):
    blocks = lax.axis_size("blk")
    route = []
    for view, step in enumerate(STEPS):
        for block in range(blocks):
            if 0 <= block + step < blocks:
                route.append((view * blocks + block, view * blocks + block + step))
    return lax.ppermute(values, ("view", "blk"), route)


def from_block(values, offset):
    blocks = lax.axis_size("blk")
    route = [(b + offset, b) for b in range(blocks) if 0 <= b + offset < blocks]
    return lax.ppermute(values, "blk", route)


def over_views(values):
    return lax.all_to_all(values, "view", 0, 0)


def body(
    estimate,
    measured,
    psf_z,
    psf_y,
    psf_x,
    psf_mix,
    weight_tiles,
    tile_index,
    src_row,
    dst_row,
    col_shift,
    back_shift,
):
    planes, row_count, col_count = estimate.shape
    stepped = step_by_view(estimate)
    received = over_views(
        pack_measured(measured, dst_row, back_shift, tile_index, psf_z, psf_y, psf_x, psf_mix)
    )
    moves, later = lax.optimization_barrier((registration(received), received))
    moves = step_by_view(moves)
    packed = pack_estimate(stepped, moves)
    far = [from_block(later, offset) for offset in (-2, 2)]
    near = [from_block(later, offset) for offset in (-1, 1)]
    neighbours = [far[0], near[0], received, near[1], far[1]]
    field = over_views(packed)
    moves = field
    strips = iteration(field, None, received, neighbours, weight_tiles)
    for _ in range(ITERS - 1):
        field = over_views(pack_field(step_by_view(over_views(strips))))
        strips = iteration(field, moves, received, neighbours, weight_tiles)
    strips = over_views(strips).reshape(VIEWS, planes, row_count, LANE)
    return jnp.transpose(strips, (1, 2, 0, 3)).reshape(planes, row_count, col_count)


def solution(mesh):
    in_specs = (
        P(None, "blk", None),
        P("view", None, "blk", None),
        P("view", None, None),
        P("view", None, None),
        P("view", None, None),
        P("view", None),
        P(),
        P("view", "blk"),
        P("view", "blk"),
        P("view", "blk"),
        P("view", "blk"),
        P("view", "blk"),
    )
    out_specs = P(None, "blk", None)
    return jax.shard_map(body, mesh=mesh, in_specs=in_specs, out_specs=out_specs, check_vma=False)
```

```python
import jax
import jax.numpy as jnp
from jax import lax
from jax.experimental import pallas as pl
from jax.experimental.pallas import tpu as pltpu
from jax.sharding import PartitionSpec as P

ITERS = 2
LANE = 128
HALF = 64
TAPS = 31
RADIUS = 15
RANK = 3
ROWS = 16
VIEWS = 8
TAP_LANE = 96
TILE_LANE = 2 * 8
ROW_MARK = 1024
Q_FIRST, Q_LAST = 41, 214
STEPS = (1, -1, 2, -2, 3, -3, 0, 0)
OWN = 6
SEEN = 3 * LANE
F32 = jnp.float32
BF16 = jnp.bfloat16
VMEM_LIMIT = 24 * 1024 * 1024
SMALL_LIMIT = 4 * 1024 * 1024


def whole(shape):
    return pl.BlockSpec(tuple(shape), lambda i: (0,) * len(shape))


def start_all(copies):
    for copy in copies:
        copy.start()
    return copies


def wait_all(copies):
    for copy in copies:
        copy.wait()


def lanes_of(shape):
    return lax.broadcasted_iota(jnp.int32, shape, len(shape) - 1)


def rows_of(shape):
    return lax.broadcasted_iota(jnp.int32, shape, len(shape) - 2)


def pick_lane(values, lane):
    index = jnp.full(values.shape, lane, jnp.int32)
    return jnp.take_along_axis(values, index, axis=1, mode="promise_in_bounds")


def look_up(values, index):
    return jnp.take_along_axis(values, index, axis=1, mode="promise_in_bounds")


def halves(values):
    high = values.astype(BF16)
    low = (values - high.astype(F32)).astype(BF16)
    return high, low


def dot(left, right):
    return jnp.dot(left, right, preferred_element_type=F32)


def dot_turned(left, right):
    return lax.dot_general(left, right, (((1,), (1,)), ((), ())), preferred_element_type=F32)


def triple(high, low, right_high, right_low, multiply):
    both = multiply(jnp.concatenate([high, low], axis=0), right_high)
    height = high.shape[0]
    return both[:height] + both[height:] + multiply(high, right_low)


def windows_of(strips):
    count = len(strips)
    turned = [pltpu.roll(strip, HALF, 1) for strip in strips]
    lower = lanes_of(strips[0].shape) < HALF
    zero = jnp.zeros_like(strips[0])
    tiles = []
    for place in range(count + 1):
        left = turned[place - 1] if place > 0 else zero
        right = turned[place] if place < count else zero
        tiles.append(jnp.where(lower, left, right))
    return tiles


def pack_measured_kernel(
    measured, dst_row, back_shift, tile_index, psf_z, psf_y, psf_x, psf_mix, out_ref, table, out, sems
):
    rows = 2 * ROWS
    view = lax.axis_index("view")
    table[...] = jnp.zeros_like(table)
    dst = dst_row[...].astype(F32) + ROW_MARK
    back = back_shift[...].astype(F32)
    tiles = tile_index[...].astype(F32)
    for plane in range(2):
        first = plane * ROWS
        table[0:1, first : first + ROWS] = dst
        table[1:2, first : first + ROWS] = back
        for part in range(2):
            start = first + part * 8
            table[2:3, start : start + 8] = jnp.broadcast_to(tiles[:, part : part + 1], (1, 8))
    upright = jnp.transpose(table[...])[:rows]
    lane = lanes_of((rows, LANE))
    moves = jnp.where(lane == view, upright[:, 0:1], 0.0)
    moves = jnp.where(lane == VIEWS + view, upright[:, 1:2], moves)
    moves = jnp.where(lane == TILE_LANE, upright[:, 2:3], moves)
    table[...] = jnp.zeros_like(table)
    for place, psf in enumerate((psf_z, psf_y, psf_x)):
        for term in range(RANK):
            values = psf[term]
            normal = values / jnp.sum(values, axis=1, keepdims=True)
            row = place * RANK + term
            table[row : row + 1, TAP_LANE : TAP_LANE + TAPS] = normal
    mix = psf_mix[...]
    table[9:10, TAP_LANE : TAP_LANE + RANK] = mix / jnp.sum(mix, axis=1, keepdims=True)
    taps = table[:rows, :]
    stash = jnp.where(lane < TAP_LANE, moves, taps)[:ROWS]
    lane = lanes_of((ROWS, LANE))
    zero = jnp.zeros((ROWS, LANE), F32)
    strips = []
    for plane in range(2):
        values = measured[0, plane]
        strips.append([values[:, place * LANE : (place + 1) * LANE] for place in range(VIEWS)])
    for place in range(VIEWS):
        before = [row[place - 1] if place > 0 else zero for row in strips]
        after = [row[place + 1] if place < VIEWS - 1 else zero for row in strips]
        edges = jnp.where(lane < 96, pltpu.roll(after[1], HALF, 1), before[1])
        edges = jnp.where(lane < HALF, pltpu.roll(before[0], HALF, 1), edges)
        edges = jnp.where(lane < 32, after[0], edges)
        turned = [pltpu.roll(row[place], HALF, 1) for row in strips]
        for number, tile in enumerate((turned[0], turned[1], edges, stash)):
            out[place, :, number * LANE : (number + 1) * LANE] = tile
    wait_all(start_all([pltpu.make_async_copy(out, out_ref, sems.at[0])]))


ANYWHERE = pl.BlockSpec(memory_space=pl.ANY)


def pack_measured(measured, dst_row, back_shift, tile_index, psf_z, psf_y, psf_x, psf_mix):
    turned = [jnp.transpose(psf, (1, 0, 2)) for psf in (psf_z, psf_y, psf_x)]
    operands = (measured, dst_row, back_shift, tile_index, *turned, psf_mix)
    shape = (VIEWS, ROWS, 4 * LANE)
    return pl.pallas_call(
        pack_measured_kernel,
        out_shape=jax.ShapeDtypeStruct(shape, F32),
        grid=(1,),
        in_specs=[whole(operand.shape) for operand in operands],
        out_specs=ANYWHERE,
        scratch_shapes=[
            pltpu.VMEM((LANE, LANE), F32),
            pltpu.VMEM(shape, F32),
            pltpu.SemaphoreType.DMA((1,)),
        ],
        name="pack_measured",
    )(*operands)


def pack_estimate_kernel(field_in, moves_in, out_ref, field, moves, out, sems):
    fetches = [
        pltpu.make_async_copy(field_in, field, sems.at[0]),
        pltpu.make_async_copy(moves_in, moves, sems.at[1]),
    ]
    start_all(fetches)
    wait_all(fetches)
    lane = lanes_of((ROWS, LANE))
    for plane in range(2):
        strips = [field[plane, :, place * LANE : (place + 1) * LANE] for place in range(VIEWS)]
        tiles = windows_of(strips)
        for place in range(VIEWS):
            out[place, plane] = jnp.where(lane < 2 * VIEWS, moves[...], tiles[place])
            out[place, 2 + plane] = tiles[place + 1]
    wait_all(start_all([pltpu.make_async_copy(out, out_ref, sems.at[2])]))


def pack_estimate(field, moves):
    shape = (VIEWS, 4, ROWS, LANE)
    return pl.pallas_call(
        pack_estimate_kernel,
        out_shape=jax.ShapeDtypeStruct(shape, F32),
        in_specs=[ANYWHERE] * 2,
        out_specs=ANYWHERE,
        scratch_shapes=[
            pltpu.VMEM(field.shape, F32),
            pltpu.VMEM(moves.shape, F32),
            pltpu.VMEM(shape, F32),
            pltpu.SemaphoreType.DMA((3,)),
        ],
        cost_estimate=pl.CostEstimate(
            flops=40_000_000_000, bytes_accessed=100_000_000, transcendentals=0
        ),
        compiler_params=pltpu.CompilerParams(vmem_limit_bytes=SMALL_LIMIT),
        name="pack_estimate",
    )(field, moves)


def hand_on_kernel(*refs):
    del refs


def hand_on(arrays):
    count = len(arrays)
    return pl.pallas_call(
        hand_on_kernel,
        out_shape=[jax.ShapeDtypeStruct(array.shape, array.dtype) for array in arrays],
        in_specs=[ANYWHERE] * count,
        out_specs=[ANYWHERE] * count,
        input_output_aliases={number: number for number in range(count)},
        cost_estimate=pl.CostEstimate(
            flops=2_000_000_000, bytes_accessed=1_000_000, transcendentals=0
        ),
        compiler_params=pltpu.CompilerParams(vmem_limit_bytes=SMALL_LIMIT),
        name="hand_on",
    )(*arrays)


def pack_field_kernel(field_in, out_ref, field, out, sems):
    fetch = pltpu.make_async_copy(field_in, field, sems.at[0])
    fetch.start()
    fetch.wait()
    tiles = windows_of([field[place] for place in range(VIEWS)])
    for place in range(VIEWS):
        out[place, 0:2] = tiles[place].reshape(2, ROWS, LANE)
        out[place, 2:4] = tiles[place + 1].reshape(2, ROWS, LANE)
    send = pltpu.make_async_copy(out, out_ref, sems.at[1])
    send.start()
    send.wait()


def pack_field(field):
    shape = (VIEWS, 4, ROWS, LANE)
    return pl.pallas_call(
        pack_field_kernel,
        out_shape=jax.ShapeDtypeStruct(shape, F32),
        in_specs=[ANYWHERE],
        out_specs=ANYWHERE,
        scratch_shapes=[
            pltpu.VMEM(field.shape, F32),
            pltpu.VMEM(shape, F32),
            pltpu.SemaphoreType.DMA((2,)),
        ],
        compiler_params=pltpu.CompilerParams(vmem_limit_bytes=SMALL_LIMIT),
        name="pack_field",
    )(field)


def tap_index(spread):
    inside = (spread >= 0) & (spread < TAPS)
    return jnp.where(inside, spread + TAP_LANE, LANE - 1)


def build_column_bands(received, high, low):
    high[...] = jnp.zeros_like(high)
    low[...] = jnp.zeros_like(low)
    shape = (LANE, LANE)
    square = tap_index(rows_of(shape) - lanes_of(shape) + RADIUS)
    shape = (ROWS, LANE)
    below = tap_index(rows_of(shape) - lanes_of(shape) + RADIUS + LANE)
    above = tap_index(rows_of(shape) - lanes_of(shape) + RADIUS - ROWS)
    for view in range(VIEWS):
        for term in range(RANK):
            taps = received[view, 6 + term : 7 + term, :]
            band = halves(look_up(jnp.broadcast_to(taps, square.shape), square))
            lower = halves(look_up(jnp.broadcast_to(taps, below.shape), below))
            upper = halves(look_up(jnp.broadcast_to(taps, above.shape), above))
            for place, target in enumerate((high, low)):
                target[view, term, :LANE, :LANE] = band[place]
                target[view, term, LANE:, LANE:] = band[place]
                target[view, term, LANE : LANE + ROWS, :LANE] = lower[place]
                target[view, term, LANE - ROWS : LANE, LANE:] = upper[place]


def build_row_bands(view, first_row, stash, rows_lane, high, low):
    taps_rows = [stash[3 + term : 4 + term, :] for term in range(RANK)]
    depth_rows = [stash[term : term + 1, :] for term in range(RANK)]
    mix_row = stash[9:10, :]
    centre = TAP_LANE + RADIUS
    dst_lane = rows_lane[pl.ds(view, 1), :]
    shape = (4 * ROWS, LANE)
    row = rows_of(shape)
    lane = lanes_of(shape)
    for part in range(2):
        dst = jnp.broadcast_to(dst_lane[:, part * LANE : (part + 1) * LANE], shape)
        spread = dst.astype(jnp.int32) - ROW_MARK - first_row - row + RADIUS
        index = tap_index(spread)
        if part == 1:
            index = jnp.where(lane < 3 * 2 * ROWS, index, LANE - 1)
        upper = (lane // ROWS) % 2 == 0
        for term in range(RANK):
            taps = jnp.broadcast_to(taps_rows[term], shape)
            band = look_up(taps, index)
            mix = mix_row[:, TAP_LANE + term : TAP_LANE + term + 1]
            depth = depth_rows[term] * mix
            for plane in range(2):
                from_first = depth[:, centre - plane : centre - plane + 1]
                from_second = depth[:, centre + 1 - plane : centre + 2 - plane]
                scaled = band * jnp.where(upper, from_first, from_second)
                band_high, band_low = halves(scaled)
                start = (term * 2 + plane) * 4 * ROWS
                columns = slice(part * LANE, (part + 1) * LANE)
                high[view, start : start + 4 * ROWS, columns] = band_high
                low[view, start : start + 4 * ROWS, columns] = band_low

def build_turned_bands(view, first_row, stash, own_dst, high, low):
    taps_rows = [stash[3 + term : 4 + term, :] for term in range(RANK)]
    depth_rows = [stash[term : term + 1, :] for term in range(RANK)]
    mix_row = stash[9:10, :]
    centre = TAP_LANE + RADIUS
    shape = (ROWS, LANE)
    lane = lanes_of(shape)
    spread = own_dst.astype(jnp.int32) - ROW_MARK - first_row - lane % (4 * ROWS) + RADIUS
    index = tap_index(spread)
    upper = lane < 4 * ROWS
    for term in range(RANK):
        taps = jnp.broadcast_to(taps_rows[term], shape)
        band = look_up(taps, index)
        mix = mix_row[:, TAP_LANE + term : TAP_LANE + term + 1]
        depth = depth_rows[term] * mix
        for plane in range(2):
            from_first = depth[:, centre + plane : centre + plane + 1]
            from_second = depth[:, centre + plane - 1 : centre + plane]
            scaled = band * jnp.where(upper, from_first, from_second)
            band_high, band_low = halves(scaled)
            start = (term * 2 + plane) * ROWS
            high[view, start : start + ROWS, :] = band_high
            low[view, start : start + ROWS, :] = band_low


def iteration_kernel(mode, *refs):
    refs = list(refs)

    def take(count):
        taken = refs[:count]
        del refs[:count]
        return taken

    forward = mode != "adjoint"
    backward = mode != "forward"
    received_in, field_in = take(2)
    moves_in = take(1)[0] if mode == "both" else None
    blurred_in = take(1)[0] if mode == "adjoint" else None
    if backward:
        sides = take(4)
        sides.insert(2, received_in.at[:, :, pl.ds(0, SEEN)])
        (tiles_in,) = take(1)
    (out,) = take(1)
    received, field, moves, col_high, col_low = take(5)
    if forward:
        row_high, row_low, x_high, x_low, rows_lane = take(5)
    if backward:
        turned_high, turned_low, measured, tiles, result_ref = take(5)
    if mode != "both":
        (blurred_ref,) = take(1)
    (sems,) = take(1)

    strip = lax.axis_index("view")
    block = lax.axis_index("blk")
    first_column = pl.multiple_of(strip * LANE, LANE)
    number = 0

    def copy(source, target):
        nonlocal number
        number += 1
        return pltpu.make_async_copy(source, target, sems.at[number - 1])

    for_taps = start_all([copy(received_in.at[:, :, pl.ds(SEEN, LANE)], received)])
    others = [copy(field_in, field)]
    if mode == "both":
        others.append(copy(moves_in.at[:, pl.ds(0, 2)], moves))
    if mode == "adjoint":
        others.append(copy(blurred_in, blurred_ref))
    if backward:
        for place, source in enumerate(sides):
            others.append(copy(source, measured.at[place]))
        others.append(copy(tiles_in.at[:, :, pl.ds(first_column, LANE)], tiles))
    start_all(others)
    wait_all(for_taps)
    build_column_bands(received, col_high, col_low)
    wait_all(others)

    lane = lanes_of((2 * ROWS, LANE))
    column = lane + strip * LANE - HALF
    columns = LANE * VIEWS
    inside = [
        (column >= 0) & (column < columns),
        (column + LANE >= 0) & (column + LANE < columns),
    ]
    wide = lanes_of((ROWS, 2 * LANE))
    wide_column = wide + strip * LANE - HALF
    kept = (wide >= Q_FIRST) & (wide <= Q_LAST) & (wide_column >= 0) & (wide_column < columns)

    if mode != "both":
        moves[...] = field[:, 0:2]
    if forward:
        rows_lane[...] = jnp.transpose(moves[...].reshape(VIEWS * 2 * ROWS, LANE))
        unused = slice((OWN + 1) * 2 * ROWS, VIEWS * 2 * ROWS)
        x_high[:, unused, :] = jnp.zeros((VIEWS, 2 * ROWS, 2 * LANE), BF16)
        x_low[:, unused, :] = jnp.zeros((VIEWS, 2 * ROWS, 2 * LANE), BF16)

    def prepare(view):
        own_dst = pick_lane(moves[OWN].reshape(2 * ROWS, LANE), view)
        last = jnp.max(own_dst) - ROW_MARK
        phase = (last >= ((block + 1) * ROWS).astype(F32)).astype(jnp.int32)
        first_row = (block - 2 + phase) * ROWS
        shift = pick_lane(moves[OWN].reshape(2 * ROWS, LANE), VIEWS + view).astype(jnp.int32)
        if backward:
            build_turned_bands(
                view, first_row, received[view], own_dst[:ROWS], turned_high, turned_low
            )
        if not forward:
            return phase, shift
        build_row_bands(view, first_row, received[view], rows_lane, row_high, row_low)
        for slot in range(OWN + 1):
            step = pick_lane(moves[slot].reshape(2 * ROWS, LANE), VIEWS + view)
            where = lane + step.astype(jnp.int32)
            index = where & (LANE - 1)
            left = look_up(field[slot, 0:2].reshape(2 * ROWS, LANE), index)
            right = look_up(field[slot, 2:4].reshape(2 * ROWS, LANE), index)
            moved = (jnp.where(where < LANE, left, right), jnp.where(where < 0, left, right))
            for part in range(2):
                high, low = halves(jnp.where(inside[part], moved[part], 0.0))
                rows = slice(slot * 2 * ROWS, (slot + 1) * 2 * ROWS)
                x_high[view, rows, part * LANE : (part + 1) * LANE] = high
                x_low[view, rows, part * LANE : (part + 1) * LANE] = low
        return phase, shift

    def blur(view):
        xh, xl = x_high[view], x_low[view]
        layers = triple(row_high[view], row_low[view], xh, xl, dot)
        blurred = None
        height = 8 * ROWS
        for term in range(RANK):
            high, low = halves(layers[term * height : (term + 1) * height])
            part = triple(high, low, col_high[view, term], col_low[view, term], dot)
            blurred = part if blurred is None else blurred + part
        return blurred

    def finish(view, blurred, phase, shift):
        quotients = [None] * 8
        lower = lanes_of((ROWS, LANE)) < HALF
        for place in range(4):
            seen = [
                jnp.where(
                    phase == 1,
                    measured[place + 1, view, :, tile * LANE : (tile + 1) * LANE],
                    measured[place, view, :, tile * LANE : (tile + 1) * LANE],
                )
                for tile in range(3)
            ]
            edges = (seen[2], pltpu.roll(seen[2], HALF, 1))
            row_block = block - 2 + phase + place
            fine = kept & (row_block >= 0) & (row_block < VIEWS * 8)
            for plane in range(2):
                middle = seen[plane]
                left = jnp.where(lower, edges[plane], middle)
                right = jnp.where(lower, middle, edges[1 - plane])
                both = jnp.concatenate([left, right], axis=1)
                start = (plane * 4 + place) * ROWS
                ratio = both / blurred[start : start + ROWS]
                quotients[plane * 4 + place] = jnp.where(fine, ratio, 0.0)
        quotient = jnp.concatenate(quotients, axis=0)
        high, low = halves(quotient)
        layers = triple(turned_high[view], turned_low[view], high, low, dot)
        where = lane + shift
        index = where & (LANE - 1)
        adjoint = None
        height = 2 * ROWS
        for term in range(RANK):
            layer = layers[term * height : (term + 1) * height]
            left = look_up(layer[:, :LANE], index)
            right = look_up(layer[:, LANE:], index)
            moved = jnp.concatenate(
                [jnp.where(where < LANE, left, right), jnp.where(where < 0, left, right)], axis=1
            )
            high, low = halves(moved)
            band_high = col_high[view, term, HALF : HALF + LANE, :]
            band_low = col_low[view, term, HALF : HALF + LANE, :]
            part = triple(high, low, band_high, band_low, dot_turned)
            adjoint = part if adjoint is None else adjoint + part
        source = column + HALF + shift
        returned = jnp.where((source >= 0) & (source < columns), adjoint, 0.0)
        chosen = pick_lane(received[view], TILE_LANE)
        weight = jnp.zeros((ROWS, LANE), F32)
        for tile in range(tiles.shape[0]):
            tall = jnp.concatenate([tiles[tile]] * 2, axis=0)
            weight = jnp.where(chosen == tile, tall, weight)
        weight = jnp.concatenate([weight, weight], axis=0)
        return weight * returned, weight


    total = jnp.zeros((2 * ROWS, LANE), F32)
    weight_total = jnp.zeros((2 * ROWS, LANE), F32)
    for view in range(VIEWS):
        phase, shift = prepare(view)
        blurred = blur(view) if forward else blurred_ref[view]
        if not backward:
            blurred_ref[view] = blurred
            continue
        more, weight = finish(view, blurred, phase, shift)
        total = total + more
        weight_total = weight_total + weight

    if not backward:
        wait_all(start_all([copy(blurred_ref, out)]))
        return
    lower = pltpu.roll(field[OWN, 0:2].reshape(2 * ROWS, LANE), HALF, 1)
    upper = pltpu.roll(field[OWN, 2:4].reshape(2 * ROWS, LANE), HALF, 1)
    own = jnp.where(lane < HALF, lower, upper)
    result_ref[...] = own * total / weight_total
    wait_all(start_all([copy(result_ref, out.at[place]) for place in range(VIEWS)]))


def iteration(mode, operands, weight_tiles=None):
    rows = 2 * ROWS
    strips = (VIEWS, rows, LANE)
    blurred = (VIEWS, 8 * ROWS, 2 * LANE)
    col_shape = (VIEWS, RANK, 2 * LANE, 2 * LANE)
    row_shape = (VIEWS, RANK * 8 * ROWS, 2 * LANE)
    turned_shape = (VIEWS, RANK * 2 * ROWS, LANE)
    scratch = [
        pltpu.VMEM((VIEWS, ROWS, LANE), F32),
        pltpu.VMEM((VIEWS, 4, ROWS, LANE), F32),
        pltpu.VMEM((VIEWS, 2, ROWS, LANE), F32),
        pltpu.VMEM(col_shape, BF16),
        pltpu.VMEM(col_shape, BF16),
    ]
    if mode != "adjoint":
        scratch += [
            pltpu.VMEM(row_shape, BF16),
            pltpu.VMEM(row_shape, BF16),
            pltpu.VMEM((VIEWS, 2 * LANE, 2 * LANE), BF16),
            pltpu.VMEM((VIEWS, 2 * LANE, 2 * LANE), BF16),
            pltpu.VMEM((LANE, 2 * LANE), F32),
        ]
    if mode != "forward":
        operands = [*operands, weight_tiles]
        scratch += [
            pltpu.VMEM(turned_shape, BF16),
            pltpu.VMEM(turned_shape, BF16),
            pltpu.VMEM((5, VIEWS, ROWS, SEEN), F32),
            pltpu.VMEM(weight_tiles.shape[:2] + (LANE,), F32),
            pltpu.VMEM((rows, LANE), F32),
        ]
    if mode != "both":
        scratch.append(pltpu.VMEM(blurred, F32))
    scratch.append(pltpu.SemaphoreType.DMA((24,)))
    return pl.pallas_call(
        lambda *refs: iteration_kernel(mode, *refs),
        out_shape=jax.ShapeDtypeStruct(blurred if mode == "forward" else strips, F32),
        in_specs=[ANYWHERE] * len(operands),
        out_specs=ANYWHERE,
        scratch_shapes=scratch,
        compiler_params=pltpu.CompilerParams(vmem_limit_bytes=VMEM_LIMIT),
        cost_estimate=pl.CostEstimate(
            flops=8_000_000_000, bytes_accessed=1_000_000, transcendentals=0
        ),
        name=f"iteration_{mode}",
    )(*operands)


def step_by_view(values):
    blocks = lax.axis_size("blk")
    route = []
    for view, step in enumerate(STEPS):
        for block in range(blocks):
            if 0 <= block + step < blocks:
                route.append((view * blocks + block, view * blocks + block + step))
    return lax.ppermute(values, ("view", "blk"), route)


def from_block(values, offset):
    blocks = lax.axis_size("blk")
    route = [(b + offset, b) for b in range(blocks) if 0 <= b + offset < blocks]
    return lax.ppermute(values, "blk", route)


def over_views(values):
    return lax.all_to_all(values, "view", 0, 0)


def body(
    estimate,
    measured,
    psf_z,
    psf_y,
    psf_x,
    psf_mix,
    weight_tiles,
    tile_index,
    src_row,
    dst_row,
    col_shift,
    back_shift,
):
    planes, row_count, col_count = estimate.shape
    stepped = step_by_view(estimate)
    received = over_views(
        pack_measured(measured, dst_row, back_shift, tile_index, psf_z, psf_y, psf_x, psf_mix)
    )
    moves = jnp.sum(received[:, :, SEEN:], axis=0)
    moves, seen = lax.optimization_barrier((moves, received[:, :, :SEEN]))
    packed = pack_estimate(stepped, step_by_view(moves))
    far = hand_on([from_block(seen, offset) for offset in (-2, 2)])
    packed, seen = lax.optimization_barrier((packed, seen))
    near = [from_block(seen, offset) for offset in (-1, 1)]
    sides = [far[0], near[0], near[1], far[1]]
    field = over_views(packed)
    moves = field
    blurred = iteration("forward", [received, field])
    strips = iteration("adjoint", [received, field, blurred, *sides], weight_tiles)
    for _ in range(ITERS - 1):
        field = over_views(pack_field(step_by_view(over_views(strips))))
        strips = iteration("both", [received, field, moves, *sides], weight_tiles)
    strips = over_views(strips).reshape(VIEWS, planes, row_count, LANE)
    return jnp.transpose(strips, (1, 2, 0, 3)).reshape(planes, row_count, col_count)


def solution(mesh):
    in_specs = (
        P(None, "blk", None),
        P("view", None, "blk", None),
        P("view", None, None),
        P("view", None, None),
        P("view", None, None),
        P("view", None),
        P(),
        P("view", "blk"),
        P("view", "blk"),
        P("view", "blk"),
        P("view", "blk"),
        P("view", "blk"),
    )
    out_specs = P(None, "blk", None)
    return jax.shard_map(body, mesh=mesh, in_specs=in_specs, out_specs=out_specs, check_vma=False)
```

```python
import jax
import jax.numpy as jnp
from jax import lax
from jax.experimental import pallas as pl
from jax.experimental.pallas import tpu as pltpu
from jax.sharding import PartitionSpec as P

ITERS = 2
LANE = 128
HALF = 64
TAPS = 31
RADIUS = 15
RANK = 3
ROWS = 16
VIEWS = 8
TAP_LANE = 96
TILE_LANE = 2 * 8
ROW_MARK = 1024
Q_FIRST, Q_LAST = 41, 214
STEPS = (1, -1, 2, -2, 3, -3, 0, 0)
OWN = 6
SEEN = 3 * LANE
F32 = jnp.float32
BF16 = jnp.bfloat16
VMEM_LIMIT = 24 * 1024 * 1024
SMALL_LIMIT = 4 * 1024 * 1024


def whole(shape):
    return pl.BlockSpec(tuple(shape), lambda i: (0,) * len(shape))


def start_all(copies):
    for copy in copies:
        copy.start()
    return copies


def wait_all(copies):
    for copy in copies:
        copy.wait()


def lanes_of(shape):
    return lax.broadcasted_iota(jnp.int32, shape, len(shape) - 1)


def rows_of(shape):
    return lax.broadcasted_iota(jnp.int32, shape, len(shape) - 2)


def pick_lane(values, lane):
    index = jnp.full(values.shape, lane, jnp.int32)
    return jnp.take_along_axis(values, index, axis=1, mode="promise_in_bounds")


def look_up(values, index):
    return jnp.take_along_axis(values, index, axis=1, mode="promise_in_bounds")


def halves(values):
    high = values.astype(BF16)
    low = (values - high.astype(F32)).astype(BF16)
    return high, low


def dot(left, right):
    return jnp.dot(left, right, preferred_element_type=F32)


def dot_turned(left, right):
    return lax.dot_general(left, right, (((1,), (1,)), ((), ())), preferred_element_type=F32)


def triple(high, low, right_high, right_low, multiply):
    both = multiply(jnp.concatenate([high, low], axis=0), right_high)
    height = high.shape[0]
    return both[:height] + both[height:] + multiply(high, right_low)


def windows_of(strips):
    count = len(strips)
    turned = [pltpu.roll(strip, HALF, 1) for strip in strips]
    lower = lanes_of(strips[0].shape) < HALF
    zero = jnp.zeros_like(strips[0])
    tiles = []
    for place in range(count + 1):
        left = turned[place - 1] if place > 0 else zero
        right = turned[place] if place < count else zero
        tiles.append(jnp.where(lower, left, right))
    return tiles


def pack_measured_kernel(
    measured, dst_row, back_shift, tile_index, psf_z, psf_y, psf_x, psf_mix, out_ref, table, out, sems
):
    rows = 2 * ROWS
    view = lax.axis_index("view")
    table[...] = jnp.zeros_like(table)
    dst = dst_row[...].astype(F32) + ROW_MARK
    back = back_shift[...].astype(F32)
    tiles = tile_index[...].astype(F32)
    for plane in range(2):
        first = plane * ROWS
        table[0:1, first : first + ROWS] = dst
        table[1:2, first : first + ROWS] = back
        for part in range(2):
            start = first + part * 8
            table[2:3, start : start + 8] = jnp.broadcast_to(tiles[:, part : part + 1], (1, 8))
    upright = jnp.transpose(table[...])[:rows]
    lane = lanes_of((rows, LANE))
    moves = jnp.where(lane == view, upright[:, 0:1], 0.0)
    moves = jnp.where(lane == VIEWS + view, upright[:, 1:2], moves)
    moves = jnp.where(lane == TILE_LANE, upright[:, 2:3], moves)
    table[...] = jnp.zeros_like(table)
    for place, psf in enumerate((psf_z, psf_y, psf_x)):
        for term in range(RANK):
            values = psf[term]
            normal = values / jnp.sum(values, axis=1, keepdims=True)
            row = place * RANK + term
            table[row : row + 1, TAP_LANE : TAP_LANE + TAPS] = normal
    mix = psf_mix[...]
    table[9:10, TAP_LANE : TAP_LANE + RANK] = mix / jnp.sum(mix, axis=1, keepdims=True)
    taps = table[:rows, :]
    stash = jnp.where(lane < TAP_LANE, moves, taps)[:ROWS]
    lane = lanes_of((ROWS, LANE))
    zero = jnp.zeros((ROWS, LANE), F32)
    strips = []
    for plane in range(2):
        values = measured[0, plane]
        strips.append([values[:, place * LANE : (place + 1) * LANE] for place in range(VIEWS)])
    for place in range(VIEWS):
        before = [row[place - 1] if place > 0 else zero for row in strips]
        after = [row[place + 1] if place < VIEWS - 1 else zero for row in strips]
        edges = jnp.where(lane < 96, pltpu.roll(after[1], HALF, 1), before[1])
        edges = jnp.where(lane < HALF, pltpu.roll(before[0], HALF, 1), edges)
        edges = jnp.where(lane < 32, after[0], edges)
        turned = [pltpu.roll(row[place], HALF, 1) for row in strips]
        for number, tile in enumerate((turned[0], turned[1], edges, stash)):
            out[place, :, number * LANE : (number + 1) * LANE] = tile
    wait_all(start_all([pltpu.make_async_copy(out, out_ref, sems.at[0])]))


ANYWHERE = pl.BlockSpec(memory_space=pl.ANY)
IN_VMEM = pl.BlockSpec(memory_space=pltpu.VMEM)


def pack_measured(measured, dst_row, back_shift, tile_index, psf_z, psf_y, psf_x, psf_mix):
    turned = [jnp.transpose(psf, (1, 0, 2)) for psf in (psf_z, psf_y, psf_x)]
    operands = (measured, dst_row, back_shift, tile_index, *turned, psf_mix)
    shape = (VIEWS, ROWS, 4 * LANE)
    return pl.pallas_call(
        pack_measured_kernel,
        out_shape=jax.ShapeDtypeStruct(shape, F32),
        grid=(1,),
        in_specs=[whole(operand.shape) for operand in operands],
        out_specs=ANYWHERE,
        scratch_shapes=[
            pltpu.VMEM((LANE, LANE), F32),
            pltpu.VMEM(shape, F32),
            pltpu.SemaphoreType.DMA((1,)),
        ],
        name="pack_measured",
    )(*operands)


def pack_estimate_kernel(field, moves, out):
    lane = lanes_of((ROWS, LANE))
    for plane in range(2):
        strips = [field[plane, :, place * LANE : (place + 1) * LANE] for place in range(VIEWS)]
        tiles = windows_of(strips)
        for place in range(VIEWS):
            out[place, plane] = jnp.where(lane < 2 * VIEWS, moves[...], tiles[place])
            out[place, 2 + plane] = tiles[place + 1]


def pack_estimate(field, moves):
    return pl.pallas_call(
        pack_estimate_kernel,
        out_shape=jax.ShapeDtypeStruct((VIEWS, 4, ROWS, LANE), F32),
        in_specs=[IN_VMEM] * 2,
        out_specs=IN_VMEM,
        cost_estimate=pl.CostEstimate(
            flops=40_000_000_000, bytes_accessed=100_000_000, transcendentals=0
        ),
        compiler_params=pltpu.CompilerParams(vmem_limit_bytes=SMALL_LIMIT),
        name="pack_estimate",
    )(field, moves)


def hand_on_kernel(*refs):
    del refs


def hand_on(arrays):
    count = len(arrays)
    return pl.pallas_call(
        hand_on_kernel,
        out_shape=[jax.ShapeDtypeStruct(array.shape, array.dtype) for array in arrays],
        in_specs=[ANYWHERE] * count,
        out_specs=[ANYWHERE] * count,
        input_output_aliases={number: number for number in range(count)},
        cost_estimate=pl.CostEstimate(
            flops=2_000_000_000, bytes_accessed=1_000_000, transcendentals=0
        ),
        compiler_params=pltpu.CompilerParams(vmem_limit_bytes=SMALL_LIMIT),
        name="hand_on",
    )(*arrays)


def pack_field_kernel(field, out):
    tiles = windows_of([field[place] for place in range(VIEWS)])
    for place in range(VIEWS):
        out[place, 0:2] = tiles[place].reshape(2, ROWS, LANE)
        out[place, 2:4] = tiles[place + 1].reshape(2, ROWS, LANE)


def pack_field(field):
    return pl.pallas_call(
        pack_field_kernel,
        out_shape=jax.ShapeDtypeStruct((VIEWS, 4, ROWS, LANE), F32),
        in_specs=[IN_VMEM],
        out_specs=IN_VMEM,
        compiler_params=pltpu.CompilerParams(vmem_limit_bytes=SMALL_LIMIT),
        name="pack_field",
    )(field)


def tap_index(spread):
    inside = (spread >= 0) & (spread < TAPS)
    return jnp.where(inside, spread + TAP_LANE, LANE - 1)


def build_column_bands(received, high, low):
    high[...] = jnp.zeros_like(high)
    low[...] = jnp.zeros_like(low)
    shape = (LANE, LANE)
    square = tap_index(rows_of(shape) - lanes_of(shape) + RADIUS)
    shape = (ROWS, LANE)
    below = tap_index(rows_of(shape) - lanes_of(shape) + RADIUS + LANE)
    above = tap_index(rows_of(shape) - lanes_of(shape) + RADIUS - ROWS)
    for view in range(VIEWS):
        for term in range(RANK):
            taps = received[view, 6 + term : 7 + term, SEEN:]
            band = halves(look_up(jnp.broadcast_to(taps, square.shape), square))
            lower = halves(look_up(jnp.broadcast_to(taps, below.shape), below))
            upper = halves(look_up(jnp.broadcast_to(taps, above.shape), above))
            for place, target in enumerate((high, low)):
                target[view, term, :LANE, :LANE] = band[place]
                target[view, term, LANE:, LANE:] = band[place]
                target[view, term, LANE : LANE + ROWS, :LANE] = lower[place]
                target[view, term, LANE - ROWS : LANE, LANE:] = upper[place]


def build_row_bands(view, first_row, stash, rows_lane, high, low):
    taps_rows = [stash[3 + term : 4 + term, :] for term in range(RANK)]
    depth_rows = [stash[term : term + 1, :] for term in range(RANK)]
    mix_row = stash[9:10, :]
    centre = TAP_LANE + RADIUS
    dst_lane = rows_lane[pl.ds(view, 1), :]
    shape = (4 * ROWS, LANE)
    row = rows_of(shape)
    lane = lanes_of(shape)
    for part in range(2):
        dst = jnp.broadcast_to(dst_lane[:, part * LANE : (part + 1) * LANE], shape)
        spread = dst.astype(jnp.int32) - ROW_MARK - first_row - row + RADIUS
        index = tap_index(spread)
        if part == 1:
            index = jnp.where(lane < 3 * 2 * ROWS, index, LANE - 1)
        upper = (lane // ROWS) % 2 == 0
        for term in range(RANK):
            taps = jnp.broadcast_to(taps_rows[term], shape)
            band = look_up(taps, index)
            mix = mix_row[:, TAP_LANE + term : TAP_LANE + term + 1]
            depth = depth_rows[term] * mix
            for plane in range(2):
                from_first = depth[:, centre - plane : centre - plane + 1]
                from_second = depth[:, centre + 1 - plane : centre + 2 - plane]
                scaled = band * jnp.where(upper, from_first, from_second)
                band_high, band_low = halves(scaled)
                start = (term * 2 + plane) * 4 * ROWS
                columns = slice(part * LANE, (part + 1) * LANE)
                high[view, start : start + 4 * ROWS, columns] = band_high
                low[view, start : start + 4 * ROWS, columns] = band_low

def build_turned_bands(view, first_row, stash, own_dst, high, low):
    taps_rows = [stash[3 + term : 4 + term, :] for term in range(RANK)]
    depth_rows = [stash[term : term + 1, :] for term in range(RANK)]
    mix_row = stash[9:10, :]
    centre = TAP_LANE + RADIUS
    shape = (ROWS, LANE)
    lane = lanes_of(shape)
    spread = own_dst.astype(jnp.int32) - ROW_MARK - first_row - lane % (4 * ROWS) + RADIUS
    index = tap_index(spread)
    upper = lane < 4 * ROWS
    for term in range(RANK):
        taps = jnp.broadcast_to(taps_rows[term], shape)
        band = look_up(taps, index)
        mix = mix_row[:, TAP_LANE + term : TAP_LANE + term + 1]
        depth = depth_rows[term] * mix
        for plane in range(2):
            from_first = depth[:, centre + plane : centre + plane + 1]
            from_second = depth[:, centre + plane - 1 : centre + plane]
            scaled = band * jnp.where(upper, from_first, from_second)
            band_high, band_low = halves(scaled)
            start = (term * 2 + plane) * ROWS
            high[view, start : start + ROWS, :] = band_high
            low[view, start : start + ROWS, :] = band_low


def iteration_kernel(mode, *refs):
    refs = list(refs)

    def take(count):
        taken = refs[:count]
        del refs[:count]
        return taken

    forward = mode != "adjoint"
    backward = mode != "forward"
    received, field = take(2)
    moves = take(1)[0] if mode == "both" else field
    blurred = take(1)[0] if mode == "adjoint" else None
    if backward:
        sides = take(4)
        sides.insert(2, received)
        tiles, col_high, col_low = take(3)
    if mode == "both":
        row_high, row_low, turned_high, turned_low = take(4)
    (out,) = take(1)
    if mode == "forward":
        col_high, col_low, row_high, row_low = take(4)
    if mode == "adjoint":
        turned_high, turned_low = take(2)
    if forward:
        x_high, x_low, rows_lane = take(3)

    strip = lax.axis_index("view")
    block = lax.axis_index("blk")
    first_column = pl.multiple_of(strip * LANE, LANE)

    def stash(view):
        return received[view, :, SEEN:]

    if mode == "forward":
        build_column_bands(received, col_high, col_low)

    lane = lanes_of((2 * ROWS, LANE))
    column = lane + strip * LANE - HALF
    columns = LANE * VIEWS
    inside = [
        (column >= 0) & (column < columns),
        (column + LANE >= 0) & (column + LANE < columns),
    ]
    wide = lanes_of((ROWS, 2 * LANE))
    wide_column = wide + strip * LANE - HALF
    kept = (wide >= Q_FIRST) & (wide <= Q_LAST) & (wide_column >= 0) & (wide_column < columns)

    if forward:
        if mode == "forward":
            rows_lane[...] = jnp.transpose(moves[:, 0:2].reshape(VIEWS * 2 * ROWS, LANE))
        unused = slice((OWN + 1) * 2 * ROWS, VIEWS * 2 * ROWS)
        x_high[:, unused, :] = jnp.zeros((VIEWS, 2 * ROWS, 2 * LANE), BF16)
        x_low[:, unused, :] = jnp.zeros((VIEWS, 2 * ROWS, 2 * LANE), BF16)

    def prepare(view):
        own_dst = pick_lane(moves[OWN, 0:2].reshape(2 * ROWS, LANE), view)
        last = jnp.max(own_dst) - ROW_MARK
        phase = (last >= ((block + 1) * ROWS).astype(F32)).astype(jnp.int32)
        first_row = (block - 2 + phase) * ROWS
        shift = pick_lane(moves[OWN, 0:2].reshape(2 * ROWS, LANE), VIEWS + view).astype(jnp.int32)
        if mode == "adjoint":
            build_turned_bands(
                view, first_row, stash(view), own_dst[:ROWS], turned_high, turned_low
            )
        if not forward:
            return phase, shift
        if mode == "forward":
            build_row_bands(view, first_row, stash(view), rows_lane, row_high, row_low)
        for slot in range(OWN + 1):
            step = pick_lane(moves[slot, 0:2].reshape(2 * ROWS, LANE), VIEWS + view)
            where = lane + step.astype(jnp.int32)
            index = where & (LANE - 1)
            left = look_up(field[slot, 0:2].reshape(2 * ROWS, LANE), index)
            right = look_up(field[slot, 2:4].reshape(2 * ROWS, LANE), index)
            moved = (jnp.where(where < LANE, left, right), jnp.where(where < 0, left, right))
            for part in range(2):
                high, low = halves(jnp.where(inside[part], moved[part], 0.0))
                rows = slice(slot * 2 * ROWS, (slot + 1) * 2 * ROWS)
                x_high[view, rows, part * LANE : (part + 1) * LANE] = high
                x_low[view, rows, part * LANE : (part + 1) * LANE] = low
        return phase, shift

    def blur(view):
        xh, xl = x_high[view], x_low[view]
        layers = triple(row_high[view], row_low[view], xh, xl, dot)
        blurred = None
        height = 8 * ROWS
        for term in range(RANK):
            high, low = halves(layers[term * height : (term + 1) * height])
            part = triple(high, low, col_high[view, term], col_low[view, term], dot)
            blurred = part if blurred is None else blurred + part
        return blurred

    def finish(view, blurred, phase, shift):
        quotients = [None] * 8
        lower = lanes_of((ROWS, LANE)) < HALF
        for place in range(4):
            seen = [
                jnp.where(
                    phase == 1,
                    sides[place + 1][view, :, tile * LANE : (tile + 1) * LANE],
                    sides[place][view, :, tile * LANE : (tile + 1) * LANE],
                )
                for tile in range(3)
            ]
            edges = (seen[2], pltpu.roll(seen[2], HALF, 1))
            row_block = block - 2 + phase + place
            fine = kept & (row_block >= 0) & (row_block < VIEWS * 8)
            for plane in range(2):
                middle = seen[plane]
                left = jnp.where(lower, edges[plane], middle)
                right = jnp.where(lower, middle, edges[1 - plane])
                both = jnp.concatenate([left, right], axis=1)
                start = (plane * 4 + place) * ROWS
                ratio = both / blurred[start : start + ROWS]
                quotients[plane * 4 + place] = jnp.where(fine, ratio, 0.0)
        quotient = jnp.concatenate(quotients, axis=0)
        high, low = halves(quotient)
        layers = triple(turned_high[view], turned_low[view], high, low, dot)
        where = lane + shift
        index = where & (LANE - 1)
        adjoint = None
        height = 2 * ROWS
        for term in range(RANK):
            layer = layers[term * height : (term + 1) * height]
            left = look_up(layer[:, :LANE], index)
            right = look_up(layer[:, LANE:], index)
            moved = jnp.concatenate(
                [jnp.where(where < LANE, left, right), jnp.where(where < 0, left, right)], axis=1
            )
            high, low = halves(moved)
            band_high = col_high[view, term, HALF : HALF + LANE, :]
            band_low = col_low[view, term, HALF : HALF + LANE, :]
            part = triple(high, low, band_high, band_low, dot_turned)
            adjoint = part if adjoint is None else adjoint + part
        source = column + HALF + shift
        returned = jnp.where((source >= 0) & (source < columns), adjoint, 0.0)
        chosen = pick_lane(stash(view), TILE_LANE)
        weight = jnp.zeros((ROWS, LANE), F32)
        for tile in range(tiles.shape[0]):
            tall = jnp.concatenate([tiles[tile, :, pl.ds(first_column, LANE)]] * 2, axis=0)
            weight = jnp.where(chosen == tile, tall, weight)
        weight = jnp.concatenate([weight, weight], axis=0)
        return weight * returned, weight


    total = jnp.zeros((2 * ROWS, LANE), F32)
    weight_total = jnp.zeros((2 * ROWS, LANE), F32)
    for view in range(VIEWS):
        phase, shift = prepare(view)
        now = blur(view) if forward else blurred[view]
        if not backward:
            out[view] = now
            continue
        more, weight = finish(view, now, phase, shift)
        total = total + more
        weight_total = weight_total + weight

    if not backward:
        return
    lower = pltpu.roll(field[OWN, 0:2].reshape(2 * ROWS, LANE), HALF, 1)
    upper = pltpu.roll(field[OWN, 2:4].reshape(2 * ROWS, LANE), HALF, 1)
    own = jnp.where(lane < HALF, lower, upper)
    result = own * total / weight_total
    for place in range(VIEWS):
        out[place] = result


def iteration(mode, operands):
    rows = 2 * ROWS
    blurred = jax.ShapeDtypeStruct((VIEWS, 8 * ROWS, 2 * LANE), F32)
    col_band = jax.ShapeDtypeStruct((VIEWS, RANK, 2 * LANE, 2 * LANE), BF16)
    row_band = jax.ShapeDtypeStruct((VIEWS, RANK * 8 * ROWS, 2 * LANE), BF16)
    turned_band = jax.ShapeDtypeStruct((VIEWS, RANK * 2 * ROWS, LANE), BF16)
    outs = [jax.ShapeDtypeStruct((VIEWS, rows, LANE), F32)]
    scratch = []
    if mode == "forward":
        outs = [blurred, col_band, col_band, row_band, row_band]
    if mode == "adjoint":
        outs += [turned_band, turned_band]
    if mode != "adjoint":
        scratch = [
            pltpu.VMEM((VIEWS, 2 * LANE, 2 * LANE), BF16),
            pltpu.VMEM((VIEWS, 2 * LANE, 2 * LANE), BF16),
            pltpu.VMEM((LANE, 2 * LANE), F32),
        ]
    return pl.pallas_call(
        lambda *refs: iteration_kernel(mode, *refs),
        out_shape=outs,
        in_specs=[IN_VMEM] * len(operands),
        out_specs=[IN_VMEM] * len(outs),
        scratch_shapes=scratch,
        compiler_params=pltpu.CompilerParams(vmem_limit_bytes=VMEM_LIMIT),
        cost_estimate=pl.CostEstimate(
            flops=8_000_000_000, bytes_accessed=1_000_000, transcendentals=0
        ),
        name=f"iteration_{mode}",
    )(*operands)


def step_by_view(values):
    blocks = lax.axis_size("blk")
    route = []
    for view, step in enumerate(STEPS):
        for block in range(blocks):
            if 0 <= block + step < blocks:
                route.append((view * blocks + block, view * blocks + block + step))
    return lax.ppermute(values, ("view", "blk"), route)


def from_block(values, offset):
    blocks = lax.axis_size("blk")
    route = [(b + offset, b) for b in range(blocks) if 0 <= b + offset < blocks]
    return lax.ppermute(values, "blk", route)


def over_views(values):
    return lax.all_to_all(values, "view", 0, 0)


def body(
    estimate,
    measured,
    psf_z,
    psf_y,
    psf_x,
    psf_mix,
    weight_tiles,
    tile_index,
    src_row,
    dst_row,
    col_shift,
    back_shift,
):
    planes, row_count, col_count = estimate.shape
    stepped = step_by_view(estimate)
    received = over_views(
        pack_measured(measured, dst_row, back_shift, tile_index, psf_z, psf_y, psf_x, psf_mix)
    )
    moves = jnp.sum(received[:, :, SEEN:], axis=0)
    moves, seen = lax.optimization_barrier((moves, received[:, :, :SEEN]))
    packed = pack_estimate(stepped, step_by_view(moves))
    far = hand_on([from_block(seen, offset) for offset in (-2, 2)])
    packed, seen = lax.optimization_barrier((packed, seen))
    near = [from_block(seen, offset) for offset in (-1, 1)]
    sides = [far[0], near[0], near[1], far[1]]
    field = over_views(packed)
    moves = field
    blurred, *bands = iteration("forward", [received, field])
    strips, *turned = iteration(
        "adjoint", [received, field, blurred, *sides, weight_tiles, *bands[:2]]
    )
    bands += turned
    for _ in range(ITERS - 1):
        field = over_views(pack_field(step_by_view(over_views(strips))))
        (strips,) = iteration(
            "both", [received, field, moves, *sides, weight_tiles, *bands]
        )
    strips = over_views(strips).reshape(VIEWS, planes, row_count, LANE)
    return jnp.transpose(strips, (1, 2, 0, 3)).reshape(planes, row_count, col_count)


def solution(mesh):
    in_specs = (
        P(None, "blk", None),
        P("view", None, "blk", None),
        P("view", None, None),
        P("view", None, None),
        P("view", None, None),
        P("view", None),
        P(),
        P("view", "blk"),
        P("view", "blk"),
        P("view", "blk"),
        P("view", "blk"),
        P("view", "blk"),
    )
    out_specs = P(None, "blk", None)
    return jax.shard_map(body, mesh=mesh, in_specs=in_specs, out_specs=out_specs, check_vma=False)
```

```python
import jax
import jax.numpy as jnp
from jax import lax
from jax.experimental import pallas as pl
from jax.experimental.pallas import tpu as pltpu
from jax.sharding import PartitionSpec as P

ITERS = 2
LANE = 128
HALF = 64
TAPS = 31
RADIUS = 15
RANK = 3
ROWS = 16
VIEWS = 8
TAP_LANE = 96
TILE_LANE = 2 * 8
ROW_MARK = 1024
Q_FIRST, Q_LAST = 41, 214
STEPS = (1, -1, 2, -2, 3, -3, 0, 0)
OWN = 6
SEEN = 3 * LANE
F32 = jnp.float32
BF16 = jnp.bfloat16
VMEM_LIMIT = 24 * 1024 * 1024
SMALL_LIMIT = 4 * 1024 * 1024


def start_all(copies):
    for copy in copies:
        copy.start()
    return copies


def wait_all(copies):
    for copy in copies:
        copy.wait()


def lanes_of(shape):
    return lax.broadcasted_iota(jnp.int32, shape, len(shape) - 1)


def rows_of(shape):
    return lax.broadcasted_iota(jnp.int32, shape, len(shape) - 2)


def pick_lane(values, lane):
    index = jnp.full(values.shape, lane, jnp.int32)
    return jnp.take_along_axis(values, index, axis=1, mode="promise_in_bounds")


def look_up(values, index):
    return jnp.take_along_axis(values, index, axis=1, mode="promise_in_bounds")


def halves(values):
    high = values.astype(BF16)
    low = (values - high.astype(F32)).astype(BF16)
    return high, low


def dot(left, right):
    return jnp.dot(left, right, preferred_element_type=F32)


def dot_turned(left, right):
    return lax.dot_general(left, right, (((1,), (1,)), ((), ())), preferred_element_type=F32)


def triple(high, low, right_high, right_low, multiply):
    both = multiply(jnp.concatenate([high, low], axis=0), right_high)
    height = high.shape[0]
    return both[:height] + both[height:] + multiply(high, right_low)


def windows_of(strips):
    count = len(strips)
    turned = [pltpu.roll(strip, HALF, 1) for strip in strips]
    lower = lanes_of(strips[0].shape) < HALF
    zero = jnp.zeros_like(strips[0])
    tiles = []
    for place in range(count + 1):
        left = turned[place - 1] if place > 0 else zero
        right = turned[place] if place < count else zero
        tiles.append(jnp.where(lower, left, right))
    return tiles


def pack_measured_kernel(*refs):
    sources, out, table = refs[:8], refs[8], refs[9]
    targets, sems = refs[10:18], refs[18]
    wait_all(
        start_all(
            [
                pltpu.make_async_copy(source, target, sems.at[number])
                for number, (source, target) in enumerate(zip(sources, targets))
            ]
        )
    )
    measured, dst_row, back_shift, tile_index, psf_z, psf_y, psf_x, psf_mix = targets
    rows = 2 * ROWS
    view = lax.axis_index("view")
    table[...] = jnp.zeros_like(table)
    dst = dst_row[...].astype(F32) + ROW_MARK
    back = back_shift[...].astype(F32)
    tiles = tile_index[...].astype(F32)
    for plane in range(2):
        first = plane * ROWS
        table[0:1, first : first + ROWS] = dst
        table[1:2, first : first + ROWS] = back
        for part in range(2):
            start = first + part * 8
            table[2:3, start : start + 8] = jnp.broadcast_to(tiles[:, part : part + 1], (1, 8))
    upright = jnp.transpose(table[...])[:rows]
    lane = lanes_of((rows, LANE))
    moves = jnp.where(lane == view, upright[:, 0:1], 0.0)
    moves = jnp.where(lane == VIEWS + view, upright[:, 1:2], moves)
    moves = jnp.where(lane == TILE_LANE, upright[:, 2:3], moves)
    table[...] = jnp.zeros_like(table)
    for place, psf in enumerate((psf_z, psf_y, psf_x)):
        for term in range(RANK):
            values = psf[term]
            normal = values / jnp.sum(values, axis=1, keepdims=True)
            row = place * RANK + term
            table[row : row + 1, TAP_LANE : TAP_LANE + TAPS] = normal
    mix = psf_mix[...]
    table[9:10, TAP_LANE : TAP_LANE + RANK] = mix / jnp.sum(mix, axis=1, keepdims=True)
    taps = table[:rows, :]
    stash = jnp.where(lane < TAP_LANE, moves, taps)[:ROWS]
    lane = lanes_of((ROWS, LANE))
    zero = jnp.zeros((ROWS, LANE), F32)
    strips = []
    for plane in range(2):
        values = measured[0, plane]
        strips.append([values[:, place * LANE : (place + 1) * LANE] for place in range(VIEWS)])
    for place in range(VIEWS):
        before = [row[place - 1] if place > 0 else zero for row in strips]
        after = [row[place + 1] if place < VIEWS - 1 else zero for row in strips]
        edges = jnp.where(lane < 96, pltpu.roll(after[1], HALF, 1), before[1])
        edges = jnp.where(lane < HALF, pltpu.roll(before[0], HALF, 1), edges)
        edges = jnp.where(lane < 32, after[0], edges)
        turned = [pltpu.roll(row[place], HALF, 1) for row in strips]
        for number, tile in enumerate((turned[0], turned[1], edges, stash)):
            out[place, :, number * LANE : (number + 1) * LANE] = tile


ANYWHERE = pl.BlockSpec(memory_space=pl.ANY)
IN_VMEM = pl.BlockSpec(memory_space=pltpu.VMEM)


def pack_measured(measured, dst_row, back_shift, tile_index, psf_z, psf_y, psf_x, psf_mix):
    turned = [jnp.transpose(psf, (1, 0, 2)) for psf in (psf_z, psf_y, psf_x)]
    operands = (measured, dst_row, back_shift, tile_index, *turned, psf_mix)
    return pl.pallas_call(
        pack_measured_kernel,
        out_shape=jax.ShapeDtypeStruct((VIEWS, ROWS, 4 * LANE), F32),
        in_specs=[ANYWHERE] * len(operands),
        out_specs=IN_VMEM,
        scratch_shapes=[
            pltpu.VMEM((LANE, LANE), F32),
            *[pltpu.VMEM(operand.shape, operand.dtype) for operand in operands],
            pltpu.SemaphoreType.DMA((len(operands),)),
        ],
        name="pack_measured",
    )(*operands)


def pack_estimate_kernel(field, moves, out):
    lane = lanes_of((ROWS, LANE))
    for plane in range(2):
        strips = [field[plane, :, place * LANE : (place + 1) * LANE] for place in range(VIEWS)]
        tiles = windows_of(strips)
        for place in range(VIEWS):
            out[place, plane] = jnp.where(lane < 2 * VIEWS, moves[...], tiles[place])
            out[place, 2 + plane] = tiles[place + 1]


def pack_estimate(field, moves):
    return pl.pallas_call(
        pack_estimate_kernel,
        out_shape=jax.ShapeDtypeStruct((VIEWS, 4, ROWS, LANE), F32),
        in_specs=[IN_VMEM] * 2,
        out_specs=IN_VMEM,
        cost_estimate=pl.CostEstimate(
            flops=40_000_000_000, bytes_accessed=100_000_000, transcendentals=0
        ),
        compiler_params=pltpu.CompilerParams(vmem_limit_bytes=SMALL_LIMIT),
        name="pack_estimate",
    )(field, moves)


def hand_on_kernel(*refs):
    del refs


def hand_on(arrays):
    count = len(arrays)
    return pl.pallas_call(
        hand_on_kernel,
        out_shape=[jax.ShapeDtypeStruct(array.shape, array.dtype) for array in arrays],
        in_specs=[ANYWHERE] * count,
        out_specs=[ANYWHERE] * count,
        input_output_aliases={number: number for number in range(count)},
        cost_estimate=pl.CostEstimate(
            flops=2_000_000_000, bytes_accessed=1_000_000, transcendentals=0
        ),
        compiler_params=pltpu.CompilerParams(vmem_limit_bytes=SMALL_LIMIT),
        name="hand_on",
    )(*arrays)


def pack_field_kernel(field, out):
    tiles = windows_of([field[place] for place in range(VIEWS)])
    for place in range(VIEWS):
        out[place, 0:2] = tiles[place].reshape(2, ROWS, LANE)
        out[place, 2:4] = tiles[place + 1].reshape(2, ROWS, LANE)


def pack_field(field):
    return pl.pallas_call(
        pack_field_kernel,
        out_shape=jax.ShapeDtypeStruct((VIEWS, 4, ROWS, LANE), F32),
        in_specs=[IN_VMEM],
        out_specs=IN_VMEM,
        compiler_params=pltpu.CompilerParams(vmem_limit_bytes=SMALL_LIMIT),
        name="pack_field",
    )(field)


def tap_index(spread):
    inside = (spread >= 0) & (spread < TAPS)
    return jnp.where(inside, spread + TAP_LANE, LANE - 1)


def build_column_bands(received, high, low):
    high[...] = jnp.zeros_like(high)
    low[...] = jnp.zeros_like(low)
    shape = (LANE, LANE)
    square = tap_index(rows_of(shape) - lanes_of(shape) + RADIUS)
    shape = (ROWS, LANE)
    below = tap_index(rows_of(shape) - lanes_of(shape) + RADIUS + LANE)
    above = tap_index(rows_of(shape) - lanes_of(shape) + RADIUS - ROWS)
    for view in range(VIEWS):
        for term in range(RANK):
            taps = received[view, 6 + term : 7 + term, SEEN:]
            band = halves(look_up(jnp.broadcast_to(taps, square.shape), square))
            lower = halves(look_up(jnp.broadcast_to(taps, below.shape), below))
            upper = halves(look_up(jnp.broadcast_to(taps, above.shape), above))
            for place, target in enumerate((high, low)):
                target[view, term, :LANE, :LANE] = band[place]
                target[view, term, LANE:, LANE:] = band[place]
                target[view, term, LANE : LANE + ROWS, :LANE] = lower[place]
                target[view, term, LANE - ROWS : LANE, LANE:] = upper[place]


def build_row_bands(view, first_row, stash, rows_lane, high, low):
    taps_rows = [stash[3 + term : 4 + term, :] for term in range(RANK)]
    depth_rows = [stash[term : term + 1, :] for term in range(RANK)]
    mix_row = stash[9:10, :]
    centre = TAP_LANE + RADIUS
    dst_lane = rows_lane[pl.ds(view, 1), :]
    shape = (4 * ROWS, LANE)
    row = rows_of(shape)
    lane = lanes_of(shape)
    for part in range(2):
        dst = jnp.broadcast_to(dst_lane[:, part * LANE : (part + 1) * LANE], shape)
        spread = dst.astype(jnp.int32) - ROW_MARK - first_row - row + RADIUS
        index = tap_index(spread)
        if part == 1:
            index = jnp.where(lane < 3 * 2 * ROWS, index, LANE - 1)
        upper = (lane // ROWS) % 2 == 0
        for term in range(RANK):
            taps = jnp.broadcast_to(taps_rows[term], shape)
            band = look_up(taps, index)
            mix = mix_row[:, TAP_LANE + term : TAP_LANE + term + 1]
            depth = depth_rows[term] * mix
            for plane in range(2):
                from_first = depth[:, centre - plane : centre - plane + 1]
                from_second = depth[:, centre + 1 - plane : centre + 2 - plane]
                scaled = band * jnp.where(upper, from_first, from_second)
                band_high, band_low = halves(scaled)
                start = (term * 2 + plane) * 4 * ROWS
                columns = slice(part * LANE, (part + 1) * LANE)
                high[view, start : start + 4 * ROWS, columns] = band_high
                low[view, start : start + 4 * ROWS, columns] = band_low

def build_turned_bands(view, first_row, stash, own_dst, high, low):
    taps_rows = [stash[3 + term : 4 + term, :] for term in range(RANK)]
    depth_rows = [stash[term : term + 1, :] for term in range(RANK)]
    mix_row = stash[9:10, :]
    centre = TAP_LANE + RADIUS
    shape = (ROWS, LANE)
    lane = lanes_of(shape)
    spread = own_dst.astype(jnp.int32) - ROW_MARK - first_row - lane % (4 * ROWS) + RADIUS
    index = tap_index(spread)
    upper = lane < 4 * ROWS
    for term in range(RANK):
        taps = jnp.broadcast_to(taps_rows[term], shape)
        band = look_up(taps, index)
        mix = mix_row[:, TAP_LANE + term : TAP_LANE + term + 1]
        depth = depth_rows[term] * mix
        for plane in range(2):
            from_first = depth[:, centre + plane : centre + plane + 1]
            from_second = depth[:, centre + plane - 1 : centre + plane]
            scaled = band * jnp.where(upper, from_first, from_second)
            band_high, band_low = halves(scaled)
            start = (term * 2 + plane) * ROWS
            high[view, start : start + ROWS, :] = band_high
            low[view, start : start + ROWS, :] = band_low


LAGS = (0, 1, 2, 4, 6)


def iteration_kernel(mode, *refs):
    refs = list(refs)

    def take(count):
        taken = refs[:count]
        del refs[:count]
        return taken

    forward = mode != "adjoint"
    backward = mode != "forward"
    received, field = take(2)
    moves = take(1)[0] if mode == "both" else field
    blurred = take(1)[0] if mode == "adjoint" else None
    if backward:
        sides = take(4)
        sides.insert(2, received)
        tiles, col_high, col_low = take(3)
    if mode == "both":
        row_high, row_low, turned_high, turned_low = take(4)
    (out,) = take(1)
    if mode == "forward":
        col_high, col_low, row_high, row_low = take(4)
    if mode == "adjoint":
        turned_high, turned_low = take(2)
    if forward:
        x_high, x_low, rows_lane = take(3)

    strip = lax.axis_index("view")
    block = lax.axis_index("blk")
    first_column = pl.multiple_of(strip * LANE, LANE)

    def stash(view):
        return received[view, :, SEEN:]

    if mode == "forward":
        build_column_bands(received, col_high, col_low)

    lane = lanes_of((2 * ROWS, LANE))
    column = lane + strip * LANE - HALF
    columns = LANE * VIEWS
    inside = [
        (column >= 0) & (column < columns),
        (column + LANE >= 0) & (column + LANE < columns),
    ]
    wide = lanes_of((ROWS, 2 * LANE))
    wide_column = wide + strip * LANE - HALF
    kept = (wide >= Q_FIRST) & (wide <= Q_LAST) & (wide_column >= 0) & (wide_column < columns)

    if forward:
        if mode == "forward":
            rows_lane[...] = jnp.transpose(moves[:, 0:2].reshape(VIEWS * 2 * ROWS, LANE))
        unused = slice((OWN + 1) * 2 * ROWS, VIEWS * 2 * ROWS)
        x_high[:, unused, :] = jnp.zeros((VIEWS, 2 * ROWS, 2 * LANE), BF16)
        x_low[:, unused, :] = jnp.zeros((VIEWS, 2 * ROWS, 2 * LANE), BF16)

    def prepare(view):
        own_dst = pick_lane(moves[OWN, 0:2].reshape(2 * ROWS, LANE), view)
        last = jnp.max(own_dst) - ROW_MARK
        phase = (last >= ((block + 1) * ROWS).astype(F32)).astype(jnp.int32)
        first_row = (block - 2 + phase) * ROWS
        shift = pick_lane(moves[OWN, 0:2].reshape(2 * ROWS, LANE), VIEWS + view).astype(jnp.int32)
        if mode == "adjoint":
            build_turned_bands(
                view, first_row, stash(view), own_dst[:ROWS], turned_high, turned_low
            )
        if not forward:
            return phase, shift
        if mode == "forward":
            build_row_bands(view, first_row, stash(view), rows_lane, row_high, row_low)
        for slot in range(OWN + 1):
            step = pick_lane(moves[slot, 0:2].reshape(2 * ROWS, LANE), VIEWS + view)
            where = lane + step.astype(jnp.int32)
            index = where & (LANE - 1)
            left = look_up(field[slot, 0:2].reshape(2 * ROWS, LANE), index)
            right = look_up(field[slot, 2:4].reshape(2 * ROWS, LANE), index)
            moved = (jnp.where(where < LANE, left, right), jnp.where(where < 0, left, right))
            for part in range(2):
                high, low = halves(jnp.where(inside[part], moved[part], 0.0))
                rows = slice(slot * 2 * ROWS, (slot + 1) * 2 * ROWS)
                x_high[view, rows, part * LANE : (part + 1) * LANE] = high
                x_low[view, rows, part * LANE : (part + 1) * LANE] = low
        return phase, shift

    def row_stage(view):
        xh, xl = x_high[view], x_low[view]
        return halves(triple(row_high[view], row_low[view], xh, xl, dot))

    def column_stage(view, layers):
        blurred = None
        height = 8 * ROWS
        for term in range(RANK):
            high, low = [half[term * height : (term + 1) * height] for half in layers]
            part = triple(high, low, col_high[view, term], col_low[view, term], dot)
            blurred = part if blurred is None else blurred + part
        return blurred

    def turned_stage(view, blurred, phase):
        quotients = [None] * 8
        lower = lanes_of((ROWS, LANE)) < HALF
        for place in range(4):
            seen = [
                jnp.where(
                    phase == 1,
                    sides[place + 1][view, :, tile * LANE : (tile + 1) * LANE],
                    sides[place][view, :, tile * LANE : (tile + 1) * LANE],
                )
                for tile in range(3)
            ]
            edges = (seen[2], pltpu.roll(seen[2], HALF, 1))
            row_block = block - 2 + phase + place
            fine = kept & (row_block >= 0) & (row_block < VIEWS * 8)
            for plane in range(2):
                middle = seen[plane]
                left = jnp.where(lower, edges[plane], middle)
                right = jnp.where(lower, middle, edges[1 - plane])
                both = jnp.concatenate([left, right], axis=1)
                start = (plane * 4 + place) * ROWS
                ratio = both / blurred[start : start + ROWS]
                quotients[plane * 4 + place] = jnp.where(fine, ratio, 0.0)
        quotient = jnp.concatenate(quotients, axis=0)
        high, low = halves(quotient)
        return triple(turned_high[view], turned_low[view], high, low, dot)

    def last_stage(view, layers, shift):
        where = lane + shift
        index = where & (LANE - 1)
        adjoint = None
        height = 2 * ROWS
        for term in range(RANK):
            layer = layers[term * height : (term + 1) * height]
            left = look_up(layer[:, :LANE], index)
            right = look_up(layer[:, LANE:], index)
            moved = jnp.concatenate(
                [jnp.where(where < LANE, left, right), jnp.where(where < 0, left, right)], axis=1
            )
            high, low = halves(moved)
            band_high = col_high[view, term, HALF : HALF + LANE, :]
            band_low = col_low[view, term, HALF : HALF + LANE, :]
            part = triple(high, low, band_high, band_low, dot_turned)
            adjoint = part if adjoint is None else adjoint + part
        source = column + HALF + shift
        returned = jnp.where((source >= 0) & (source < columns), adjoint, 0.0)
        chosen = pick_lane(stash(view), TILE_LANE)
        weight = jnp.zeros((ROWS, LANE), F32)
        for tile in range(tiles.shape[0]):
            tall = jnp.concatenate([tiles[tile, :, pl.ds(first_column, LANE)]] * 2, axis=0)
            weight = jnp.where(chosen == tile, tall, weight)
        weight = jnp.concatenate([weight, weight], axis=0)
        return weight * returned, weight


    total = jnp.zeros((2 * ROWS, LANE), F32)
    weight_total = jnp.zeros((2 * ROWS, LANE), F32)
    known = [None] * VIEWS
    values = [None] * VIEWS
    stages = []
    if forward:
        stages += ["prepare", "rows", "columns"]
    else:
        stages += ["prepare"]
    if backward:
        stages += ["turned", "last"]
    for step in range(VIEWS + LAGS[len(stages) - 1]):
        for stage, lag in zip(stages, LAGS):
            view = step - lag
            if not 0 <= view < VIEWS:
                continue
            if stage == "prepare":
                known[view] = prepare(view)
                if not forward:
                    values[view] = blurred[view]
            elif stage == "rows":
                values[view] = row_stage(view)
            elif stage == "columns":
                values[view] = column_stage(view, values[view])
                if not backward:
                    out[view] = values[view]
            elif stage == "turned":
                values[view] = turned_stage(view, values[view], known[view][0])
            else:
                more, weight = last_stage(view, values[view], known[view][1])
                total = total + more
                weight_total = weight_total + weight
    if not backward:
        return
    lower = pltpu.roll(field[OWN, 0:2].reshape(2 * ROWS, LANE), HALF, 1)
    upper = pltpu.roll(field[OWN, 2:4].reshape(2 * ROWS, LANE), HALF, 1)
    own = jnp.where(lane < HALF, lower, upper)
    result = own * total / weight_total
    for place in range(VIEWS):
        out[place] = result


def iteration(mode, operands):
    rows = 2 * ROWS
    blurred = jax.ShapeDtypeStruct((VIEWS, 8 * ROWS, 2 * LANE), F32)
    col_band = jax.ShapeDtypeStruct((VIEWS, RANK, 2 * LANE, 2 * LANE), BF16)
    row_band = jax.ShapeDtypeStruct((VIEWS, RANK * 8 * ROWS, 2 * LANE), BF16)
    turned_band = jax.ShapeDtypeStruct((VIEWS, RANK * 2 * ROWS, LANE), BF16)
    outs = [jax.ShapeDtypeStruct((VIEWS, rows, LANE), F32)]
    scratch = []
    if mode == "forward":
        outs = [blurred, col_band, col_band, row_band, row_band]
    if mode == "adjoint":
        outs += [turned_band, turned_band]
    if mode != "adjoint":
        scratch = [
            pltpu.VMEM((VIEWS, 2 * LANE, 2 * LANE), BF16),
            pltpu.VMEM((VIEWS, 2 * LANE, 2 * LANE), BF16),
            pltpu.VMEM((LANE, 2 * LANE), F32),
        ]
    return pl.pallas_call(
        lambda *refs: iteration_kernel(mode, *refs),
        out_shape=outs,
        in_specs=[IN_VMEM] * len(operands),
        out_specs=[IN_VMEM] * len(outs),
        scratch_shapes=scratch,
        compiler_params=pltpu.CompilerParams(vmem_limit_bytes=VMEM_LIMIT),
        cost_estimate=pl.CostEstimate(
            flops=8_000_000_000, bytes_accessed=1_000_000, transcendentals=0
        ),
        name=f"iteration_{mode}",
    )(*operands)


def step_by_view(values):
    blocks = lax.axis_size("blk")
    route = []
    for view, step in enumerate(STEPS):
        for block in range(blocks):
            if 0 <= block + step < blocks:
                route.append((view * blocks + block, view * blocks + block + step))
    return lax.ppermute(values, ("view", "blk"), route)


def from_block(values, offset):
    blocks = lax.axis_size("blk")
    route = [(b + offset, b) for b in range(blocks) if 0 <= b + offset < blocks]
    return lax.ppermute(values, "blk", route)


def over_views(values):
    return lax.all_to_all(values, "view", 0, 0)


def body(
    estimate,
    measured,
    psf_z,
    psf_y,
    psf_x,
    psf_mix,
    weight_tiles,
    tile_index,
    src_row,
    dst_row,
    col_shift,
    back_shift,
):
    planes, row_count, col_count = estimate.shape
    stepped = step_by_view(estimate)
    received = over_views(
        pack_measured(measured, dst_row, back_shift, tile_index, psf_z, psf_y, psf_x, psf_mix)
    )
    moves = jnp.sum(received[:, :, SEEN:], axis=0)
    moves, seen = lax.optimization_barrier((moves, received[:, :, :SEEN]))
    packed = pack_estimate(stepped, step_by_view(moves))
    far = hand_on([from_block(seen, offset) for offset in (-2, 2)])
    packed, seen = lax.optimization_barrier((packed, seen))
    near = [from_block(seen, offset) for offset in (-1, 1)]
    sides = [far[0], near[0], near[1], far[1]]
    field = over_views(packed)
    moves = field
    blurred, *bands = iteration("forward", [received, field])
    strips, *turned = iteration(
        "adjoint", [received, field, blurred, *sides, weight_tiles, *bands[:2]]
    )
    bands += turned
    for _ in range(ITERS - 1):
        field = over_views(pack_field(step_by_view(over_views(strips))))
        (strips,) = iteration(
            "both", [received, field, moves, *sides, weight_tiles, *bands]
        )
    strips = over_views(strips).reshape(VIEWS, planes, row_count, LANE)
    return jnp.transpose(strips, (1, 2, 0, 3)).reshape(planes, row_count, col_count)


def solution(mesh):
    in_specs = (
        P(None, "blk", None),
        P("view", None, "blk", None),
        P("view", None, None),
        P("view", None, None),
        P("view", None, None),
        P("view", None),
        P(),
        P("view", "blk"),
        P("view", "blk"),
        P("view", "blk"),
        P("view", "blk"),
        P("view", "blk"),
    )
    out_specs = P(None, "blk", None)
    return jax.shard_map(body, mesh=mesh, in_specs=in_specs, out_specs=out_specs, check_vma=False)
```

```python
import jax
import jax.numpy as jnp
from jax import lax
from jax.experimental import pallas as pl
from jax.experimental.pallas import tpu as pltpu
from jax.sharding import PartitionSpec as P

ITERS = 2
LANE = 128
HALF = 64
TAPS = 31
RADIUS = 15
RANK = 3
ROWS = 16
VIEWS = 8
TAP_LANE = 96
TILE_LANE = 2 * 8
ROW_MARK = 1024
Q_FIRST, Q_LAST = 41, 214
STEPS = (1, -1, 2, -2, 3, -3, 0, 0)
OWN = 6
SEEN = 3 * LANE
F32 = jnp.float32
BF16 = jnp.bfloat16
VMEM_LIMIT = 24 * 1024 * 1024
SMALL_LIMIT = 4 * 1024 * 1024


def start_all(copies):
    for copy in copies:
        copy.start()
    return copies


def wait_all(copies):
    for copy in copies:
        copy.wait()


def lanes_of(shape):
    return lax.broadcasted_iota(jnp.int32, shape, len(shape) - 1)


def rows_of(shape):
    return lax.broadcasted_iota(jnp.int32, shape, len(shape) - 2)


def pick_lane(values, lane):
    index = jnp.full(values.shape, lane, jnp.int32)
    return jnp.take_along_axis(values, index, axis=1, mode="promise_in_bounds")


def look_up(values, index):
    return jnp.take_along_axis(values, index, axis=1, mode="promise_in_bounds")


def halves(values):
    high = values.astype(BF16)
    low = (values - high.astype(F32)).astype(BF16)
    return high, low


def dot(left, right):
    return jnp.dot(left, right, preferred_element_type=F32)


def dot_turned(left, right):
    return lax.dot_general(left, right, (((1,), (1,)), ((), ())), preferred_element_type=F32)


def triple(high, low, right_high, right_low, multiply):
    both = multiply(jnp.concatenate([high, low], axis=0), right_high)
    height = high.shape[0]
    return both[:height] + both[height:] + multiply(high, right_low)


def windows_of(strips):
    count = len(strips)
    turned = [pltpu.roll(strip, HALF, 1) for strip in strips]
    lower = lanes_of(strips[0].shape) < HALF
    zero = jnp.zeros_like(strips[0])
    tiles = []
    for place in range(count + 1):
        left = turned[place - 1] if place > 0 else zero
        right = turned[place] if place < count else zero
        tiles.append(jnp.where(lower, left, right))
    return tiles


def pack_measured_kernel(*refs):
    sources, out, table = refs[:8], refs[8], refs[9]
    targets, sems = refs[10:18], refs[18]
    wait_all(
        start_all(
            [
                pltpu.make_async_copy(source, target, sems.at[number])
                for number, (source, target) in enumerate(zip(sources, targets))
            ]
        )
    )
    measured, dst_row, back_shift, tile_index, psf_z, psf_y, psf_x, psf_mix = targets
    rows = 2 * ROWS
    view = lax.axis_index("view")
    table[...] = jnp.zeros_like(table)
    dst = dst_row[...].astype(F32) + ROW_MARK
    back = back_shift[...].astype(F32)
    tiles = tile_index[...].astype(F32)
    for plane in range(2):
        first = plane * ROWS
        table[0:1, first : first + ROWS] = dst
        table[1:2, first : first + ROWS] = back
        for part in range(2):
            start = first + part * 8
            table[2:3, start : start + 8] = jnp.broadcast_to(tiles[:, part : part + 1], (1, 8))
    upright = jnp.transpose(table[...])[:rows]
    lane = lanes_of((rows, LANE))
    moves = jnp.where(lane == view, upright[:, 0:1], 0.0)
    moves = jnp.where(lane == VIEWS + view, upright[:, 1:2], moves)
    moves = jnp.where(lane == TILE_LANE, upright[:, 2:3], moves)
    table[...] = jnp.zeros_like(table)
    for place, psf in enumerate((psf_z, psf_y, psf_x)):
        for term in range(RANK):
            values = psf[term]
            normal = values / jnp.sum(values, axis=1, keepdims=True)
            row = place * RANK + term
            table[row : row + 1, TAP_LANE : TAP_LANE + TAPS] = normal
    mix = psf_mix[...]
    table[9:10, TAP_LANE : TAP_LANE + RANK] = mix / jnp.sum(mix, axis=1, keepdims=True)
    taps = table[:rows, :]
    stash = jnp.where(lane < TAP_LANE, moves, taps)[:ROWS]
    lane = lanes_of((ROWS, LANE))
    zero = jnp.zeros((ROWS, LANE), F32)
    strips = []
    for plane in range(2):
        values = measured[0, plane]
        strips.append([values[:, place * LANE : (place + 1) * LANE] for place in range(VIEWS)])
    for place in range(VIEWS):
        before = [row[place - 1] if place > 0 else zero for row in strips]
        after = [row[place + 1] if place < VIEWS - 1 else zero for row in strips]
        edges = jnp.where(lane < 96, pltpu.roll(after[1], HALF, 1), before[1])
        edges = jnp.where(lane < HALF, pltpu.roll(before[0], HALF, 1), edges)
        edges = jnp.where(lane < 32, after[0], edges)
        turned = [pltpu.roll(row[place], HALF, 1) for row in strips]
        for number, tile in enumerate((turned[0], turned[1], edges, stash)):
            out[place, :, number * LANE : (number + 1) * LANE] = tile


ANYWHERE = pl.BlockSpec(memory_space=pl.ANY)
IN_VMEM = pl.BlockSpec(memory_space=pltpu.VMEM)


def pack_measured(measured, dst_row, back_shift, tile_index, psf_z, psf_y, psf_x, psf_mix):
    turned = [jnp.transpose(psf, (1, 0, 2)) for psf in (psf_z, psf_y, psf_x)]
    operands = (measured, dst_row, back_shift, tile_index, *turned, psf_mix)
    return pl.pallas_call(
        pack_measured_kernel,
        out_shape=jax.ShapeDtypeStruct((VIEWS, ROWS, 4 * LANE), F32),
        in_specs=[ANYWHERE] * len(operands),
        out_specs=IN_VMEM,
        scratch_shapes=[
            pltpu.VMEM((LANE, LANE), F32),
            *[pltpu.VMEM(operand.shape, operand.dtype) for operand in operands],
            pltpu.SemaphoreType.DMA((len(operands),)),
        ],
        name="pack_measured",
    )(*operands)


def pack_estimate_kernel(field, moves, out):
    lane = lanes_of((ROWS, LANE))
    for plane in range(2):
        strips = [field[plane, :, place * LANE : (place + 1) * LANE] for place in range(VIEWS)]
        tiles = windows_of(strips)
        for place in range(VIEWS):
            out[place, plane] = jnp.where(lane < 2 * VIEWS, moves[...], tiles[place])
            out[place, 2 + plane] = tiles[place + 1]


def pack_estimate(field, moves):
    return pl.pallas_call(
        pack_estimate_kernel,
        out_shape=jax.ShapeDtypeStruct((VIEWS, 4, ROWS, LANE), F32),
        in_specs=[IN_VMEM] * 2,
        out_specs=IN_VMEM,
        cost_estimate=pl.CostEstimate(
            flops=40_000_000_000, bytes_accessed=100_000_000, transcendentals=0
        ),
        compiler_params=pltpu.CompilerParams(vmem_limit_bytes=SMALL_LIMIT),
        name="pack_estimate",
    )(field, moves)


def hand_on_kernel(*refs):
    del refs


def hand_on(arrays):
    count = len(arrays)
    return pl.pallas_call(
        hand_on_kernel,
        out_shape=[jax.ShapeDtypeStruct(array.shape, array.dtype) for array in arrays],
        in_specs=[ANYWHERE] * count,
        out_specs=[ANYWHERE] * count,
        input_output_aliases={number: number for number in range(count)},
        cost_estimate=pl.CostEstimate(
            flops=2_000_000_000, bytes_accessed=1_000_000, transcendentals=0
        ),
        compiler_params=pltpu.CompilerParams(vmem_limit_bytes=SMALL_LIMIT),
        name="hand_on",
    )(*arrays)


def pack_field_kernel(field, out):
    tiles = windows_of([field[place] for place in range(VIEWS)])
    for place in range(VIEWS):
        out[place, 0:2] = tiles[place].reshape(2, ROWS, LANE)
        out[place, 2:4] = tiles[place + 1].reshape(2, ROWS, LANE)


def pack_field(field):
    return pl.pallas_call(
        pack_field_kernel,
        out_shape=jax.ShapeDtypeStruct((VIEWS, 4, ROWS, LANE), F32),
        in_specs=[IN_VMEM],
        out_specs=IN_VMEM,
        compiler_params=pltpu.CompilerParams(vmem_limit_bytes=SMALL_LIMIT),
        name="pack_field",
    )(field)


def tap_index(spread):
    inside = (spread >= 0) & (spread < TAPS)
    return jnp.where(inside, spread + TAP_LANE, LANE - 1)


def build_column_bands(received, high, low):
    high[...] = jnp.zeros_like(high)
    low[...] = jnp.zeros_like(low)
    shape = (LANE, LANE)
    square = tap_index(rows_of(shape) - lanes_of(shape) + RADIUS)
    shape = (ROWS, LANE)
    below = tap_index(rows_of(shape) - lanes_of(shape) + RADIUS + LANE)
    above = tap_index(rows_of(shape) - lanes_of(shape) + RADIUS - ROWS)
    for view in range(VIEWS):
        for term in range(RANK):
            taps = received[view, 6 + term : 7 + term, SEEN:]
            band = halves(look_up(jnp.broadcast_to(taps, square.shape), square))
            lower = halves(look_up(jnp.broadcast_to(taps, below.shape), below))
            upper = halves(look_up(jnp.broadcast_to(taps, above.shape), above))
            for place, target in enumerate((high, low)):
                target[view, term, :LANE, :LANE] = band[place]
                target[view, term, LANE:, LANE:] = band[place]
                target[view, term, LANE : LANE + ROWS, :LANE] = lower[place]
                target[view, term, LANE - ROWS : LANE, LANE:] = upper[place]


def build_row_bands(view, first_row, stash, rows_lane, high, low):
    taps_rows = [stash[3 + term : 4 + term, :] for term in range(RANK)]
    depth_rows = [stash[term : term + 1, :] for term in range(RANK)]
    mix_row = stash[9:10, :]
    centre = TAP_LANE + RADIUS
    dst_lane = rows_lane[pl.ds(view, 1), :]
    shape = (4 * ROWS, LANE)
    row = rows_of(shape)
    lane = lanes_of(shape)
    for part in range(2):
        dst = jnp.broadcast_to(dst_lane[:, part * LANE : (part + 1) * LANE], shape)
        spread = dst.astype(jnp.int32) - ROW_MARK - first_row - row + RADIUS
        index = tap_index(spread)
        if part == 1:
            index = jnp.where(lane < 3 * 2 * ROWS, index, LANE - 1)
        upper = (lane // ROWS) % 2 == 0
        for term in range(RANK):
            taps = jnp.broadcast_to(taps_rows[term], shape)
            band = look_up(taps, index)
            mix = mix_row[:, TAP_LANE + term : TAP_LANE + term + 1]
            depth = depth_rows[term] * mix
            for plane in range(2):
                from_first = depth[:, centre - plane : centre - plane + 1]
                from_second = depth[:, centre + 1 - plane : centre + 2 - plane]
                scaled = band * jnp.where(upper, from_first, from_second)
                band_high, band_low = halves(scaled)
                start = (term * 2 + plane) * 4 * ROWS
                columns = slice(part * LANE, (part + 1) * LANE)
                high[view, start : start + 4 * ROWS, columns] = band_high
                low[view, start : start + 4 * ROWS, columns] = band_low

def build_turned_bands(view, first_row, stash, own_dst, high, low):
    taps_rows = [stash[3 + term : 4 + term, :] for term in range(RANK)]
    depth_rows = [stash[term : term + 1, :] for term in range(RANK)]
    mix_row = stash[9:10, :]
    centre = TAP_LANE + RADIUS
    shape = (ROWS, LANE)
    lane = lanes_of(shape)
    spread = own_dst.astype(jnp.int32) - ROW_MARK - first_row - lane % (4 * ROWS) + RADIUS
    index = tap_index(spread)
    upper = lane < 4 * ROWS
    for term in range(RANK):
        taps = jnp.broadcast_to(taps_rows[term], shape)
        band = look_up(taps, index)
        mix = mix_row[:, TAP_LANE + term : TAP_LANE + term + 1]
        depth = depth_rows[term] * mix
        for plane in range(2):
            from_first = depth[:, centre + plane : centre + plane + 1]
            from_second = depth[:, centre + plane - 1 : centre + plane]
            scaled = band * jnp.where(upper, from_first, from_second)
            band_high, band_low = halves(scaled)
            start = (term * 2 + plane) * ROWS
            high[view, start : start + ROWS, :] = band_high
            low[view, start : start + ROWS, :] = band_low


LAGS = (0, 1, 2, 4, 6)


def iteration_kernel(mode, *refs):
    refs = list(refs)

    def take(count):
        taken = refs[:count]
        del refs[:count]
        return taken

    forward = mode != "adjoint"
    backward = mode != "forward"
    received, field = take(2)
    moves = take(1)[0] if mode == "both" else field
    blurred = take(1)[0] if mode == "adjoint" else None
    if backward:
        sides = take(4)
        sides.insert(2, received)
        tiles, col_high, col_low = take(3)
    if mode == "both":
        row_high, row_low, turned_high, turned_low = take(4)
    (out,) = take(1)
    if mode == "forward":
        col_high, col_low, row_high, row_low = take(4)
    if mode == "adjoint":
        turned_high, turned_low = take(2)
    if forward:
        x_high, x_low, rows_lane = take(3)

    strip = lax.axis_index("view")
    block = lax.axis_index("blk")
    first_column = pl.multiple_of(strip * LANE, LANE)

    def stash(view):
        return received[view, :, SEEN:]

    if mode == "forward":
        build_column_bands(received, col_high, col_low)

    lane = lanes_of((2 * ROWS, LANE))
    column = lane + strip * LANE - HALF
    columns = LANE * VIEWS
    inside = [
        (column >= 0) & (column < columns),
        (column + LANE >= 0) & (column + LANE < columns),
    ]
    wide = lanes_of((ROWS, 2 * LANE))
    wide_column = wide + strip * LANE - HALF
    kept = (wide >= Q_FIRST) & (wide <= Q_LAST) & (wide_column >= 0) & (wide_column < columns)

    if forward:
        if mode == "forward":
            rows_lane[...] = jnp.transpose(moves[:, 0:2].reshape(VIEWS * 2 * ROWS, LANE))
        unused = slice((OWN + 1) * 2 * ROWS, VIEWS * 2 * ROWS)
        x_high[:, unused, :] = jnp.zeros((VIEWS, 2 * ROWS, 2 * LANE), BF16)
        x_low[:, unused, :] = jnp.zeros((VIEWS, 2 * ROWS, 2 * LANE), BF16)

    def prepare(view):
        own_dst = pick_lane(moves[OWN, 0:2].reshape(2 * ROWS, LANE), view)
        last = jnp.max(own_dst) - ROW_MARK
        phase = (last >= ((block + 1) * ROWS).astype(F32)).astype(jnp.int32)
        first_row = (block - 2 + phase) * ROWS
        shift = pick_lane(moves[OWN, 0:2].reshape(2 * ROWS, LANE), VIEWS + view).astype(jnp.int32)
        if mode == "adjoint":
            build_turned_bands(
                view, first_row, stash(view), own_dst[:ROWS], turned_high, turned_low
            )
        if not forward:
            return phase, shift
        if mode == "forward":
            build_row_bands(view, first_row, stash(view), rows_lane, row_high, row_low)
        for slot in range(OWN + 1):
            step = pick_lane(moves[slot, 0:2].reshape(2 * ROWS, LANE), VIEWS + view)
            where = lane + step.astype(jnp.int32)
            index = where & (LANE - 1)
            left = look_up(field[slot, 0:2].reshape(2 * ROWS, LANE), index)
            right = look_up(field[slot, 2:4].reshape(2 * ROWS, LANE), index)
            moved = (jnp.where(where < LANE, left, right), jnp.where(where < 0, left, right))
            for part in range(2):
                high, low = halves(jnp.where(inside[part], moved[part], 0.0))
                rows = slice(slot * 2 * ROWS, (slot + 1) * 2 * ROWS)
                x_high[view, rows, part * LANE : (part + 1) * LANE] = high
                x_low[view, rows, part * LANE : (part + 1) * LANE] = low
        return phase, shift

    def row_stage(view):
        xh, xl = x_high[view], x_low[view]
        return halves(triple(row_high[view], row_low[view], xh, xl, dot))

    def column_stage(view, layers):
        blurred = None
        height = 8 * ROWS
        for term in range(RANK):
            high, low = [half[term * height : (term + 1) * height] for half in layers]
            part = triple(high, low, col_high[view, term], col_low[view, term], dot)
            blurred = part if blurred is None else blurred + part
        return blurred

    def turned_stage(view, blurred, phase):
        quotients = [None] * 8
        lower = lanes_of((ROWS, LANE)) < HALF
        for place in range(4):
            seen = [
                jnp.where(
                    phase == 1,
                    sides[place + 1][view, :, tile * LANE : (tile + 1) * LANE],
                    sides[place][view, :, tile * LANE : (tile + 1) * LANE],
                )
                for tile in range(3)
            ]
            edges = (seen[2], pltpu.roll(seen[2], HALF, 1))
            row_block = block - 2 + phase + place
            fine = kept & (row_block >= 0) & (row_block < VIEWS * 8)
            for plane in range(2):
                middle = seen[plane]
                left = jnp.where(lower, edges[plane], middle)
                right = jnp.where(lower, middle, edges[1 - plane])
                both = jnp.concatenate([left, right], axis=1)
                start = (plane * 4 + place) * ROWS
                ratio = both / blurred[start : start + ROWS]
                quotients[plane * 4 + place] = jnp.where(fine, ratio, 0.0)
        quotient = jnp.concatenate(quotients, axis=0)
        high, low = halves(quotient)
        return triple(turned_high[view], turned_low[view], high, low, dot)

    def last_stage(view, layers, shift):
        where = lane + shift
        index = where & (LANE - 1)
        adjoint = None
        height = 2 * ROWS
        for term in range(RANK):
            layer = layers[term * height : (term + 1) * height]
            left = look_up(layer[:, :LANE], index)
            right = look_up(layer[:, LANE:], index)
            moved = jnp.concatenate(
                [jnp.where(where < LANE, left, right), jnp.where(where < 0, left, right)], axis=1
            )
            high, low = halves(moved)
            band_high = col_high[view, term, HALF : HALF + LANE, :]
            band_low = col_low[view, term, HALF : HALF + LANE, :]
            part = triple(high, low, band_high, band_low, dot_turned)
            adjoint = part if adjoint is None else adjoint + part
        source = column + HALF + shift
        returned = jnp.where((source >= 0) & (source < columns), adjoint, 0.0)
        chosen = pick_lane(stash(view), TILE_LANE)
        weight = jnp.zeros((ROWS, LANE), F32)
        for tile in range(tiles.shape[0]):
            tall = jnp.concatenate([tiles[tile, :, pl.ds(first_column, LANE)]] * 2, axis=0)
            weight = jnp.where(chosen == tile, tall, weight)
        weight = jnp.concatenate([weight, weight], axis=0)
        return weight * returned, weight


    total = jnp.zeros((2 * ROWS, LANE), F32)
    weight_total = jnp.zeros((2 * ROWS, LANE), F32)
    known = [None] * VIEWS
    values = [None] * VIEWS
    stages = []
    if forward:
        stages += ["prepare", "rows", "columns"]
    else:
        stages += ["prepare"]
    if backward:
        stages += ["turned", "last"]
    for step in range(VIEWS + LAGS[len(stages) - 1]):
        for stage, lag in zip(stages, LAGS):
            view = step - lag
            if not 0 <= view < VIEWS:
                continue
            if stage == "prepare":
                known[view] = prepare(view)
                if not forward:
                    values[view] = blurred[view]
            elif stage == "rows":
                values[view] = row_stage(view)
            elif stage == "columns":
                values[view] = column_stage(view, values[view])
                if not backward:
                    out[view] = values[view]
            elif stage == "turned":
                values[view] = turned_stage(view, values[view], known[view][0])
            else:
                more, weight = last_stage(view, values[view], known[view][1])
                total = total + more
                weight_total = weight_total + weight
    if not backward:
        return
    lower = pltpu.roll(field[OWN, 0:2].reshape(2 * ROWS, LANE), HALF, 1)
    upper = pltpu.roll(field[OWN, 2:4].reshape(2 * ROWS, LANE), HALF, 1)
    own = jnp.where(lane < HALF, lower, upper)
    result = own * total / weight_total
    for place in range(VIEWS):
        out[place] = result


def iteration(mode, operands):
    rows = 2 * ROWS
    blurred = jax.ShapeDtypeStruct((VIEWS, 8 * ROWS, 2 * LANE), F32)
    col_band = jax.ShapeDtypeStruct((VIEWS, RANK, 2 * LANE, 2 * LANE), BF16)
    row_band = jax.ShapeDtypeStruct((VIEWS, RANK * 8 * ROWS, 2 * LANE), BF16)
    turned_band = jax.ShapeDtypeStruct((VIEWS, RANK * 2 * ROWS, LANE), BF16)
    outs = [jax.ShapeDtypeStruct((VIEWS, rows, LANE), F32)]
    scratch = []
    if mode == "forward":
        outs = [blurred, col_band, col_band, row_band, row_band]
    if mode == "adjoint":
        outs += [turned_band, turned_band]
    if mode != "adjoint":
        scratch = [
            pltpu.VMEM((VIEWS, 2 * LANE, 2 * LANE), BF16),
            pltpu.VMEM((VIEWS, 2 * LANE, 2 * LANE), BF16),
            pltpu.VMEM((LANE, 2 * LANE), F32),
        ]
    return pl.pallas_call(
        lambda *refs: iteration_kernel(mode, *refs),
        out_shape=outs,
        in_specs=[IN_VMEM] * len(operands),
        out_specs=[IN_VMEM] * len(outs),
        scratch_shapes=scratch,
        compiler_params=pltpu.CompilerParams(vmem_limit_bytes=VMEM_LIMIT),
        cost_estimate=pl.CostEstimate(
            flops=8_000_000_000, bytes_accessed=1_000_000, transcendentals=0
        ),
        name=f"iteration_{mode}",
    )(*operands)


def step_by_view(values):
    blocks = lax.axis_size("blk")
    route = []
    for view, step in enumerate(STEPS):
        for block in range(blocks):
            if 0 <= block + step < blocks:
                route.append((view * blocks + block, view * blocks + block + step))
    return lax.ppermute(values, ("view", "blk"), route)


def from_block(values, offset):
    blocks = lax.axis_size("blk")
    route = [(b + offset, b) for b in range(blocks) if 0 <= b + offset < blocks]
    return lax.ppermute(values, "blk", route)


def over_views(values):
    return lax.all_to_all(values, "view", 0, 0)


def body(
    estimate,
    measured,
    psf_z,
    psf_y,
    psf_x,
    psf_mix,
    weight_tiles,
    tile_index,
    src_row,
    dst_row,
    col_shift,
    back_shift,
):
    planes, row_count, col_count = estimate.shape
    stepped = step_by_view(estimate)
    received = over_views(
        pack_measured(measured, dst_row, back_shift, tile_index, psf_z, psf_y, psf_x, psf_mix)
    )
    moves = jnp.sum(received[:, :, SEEN:], axis=0)
    moves, seen = lax.optimization_barrier((moves, received[:, :, :SEEN]))
    packed = pack_estimate(stepped, step_by_view(moves))
    near = [from_block(seen, offset) for offset in (-1, 1)]
    near = hand_on(near)
    _, *relayed = lax.optimization_barrier((packed, *near))
    far = [from_block(values, offset) for values, offset in zip(relayed, (-1, 1))]
    sides = [far[0], near[0], near[1], far[1]]
    field = over_views(packed)
    moves = field
    blurred, *bands = iteration("forward", [received, field])
    strips, *turned = iteration(
        "adjoint", [received, field, blurred, *sides, weight_tiles, *bands[:2]]
    )
    bands += turned
    for _ in range(ITERS - 1):
        field = over_views(pack_field(step_by_view(over_views(strips))))
        (strips,) = iteration(
            "both", [received, field, moves, *sides, weight_tiles, *bands]
        )
    strips = over_views(strips).reshape(VIEWS, planes, row_count, LANE)
    return jnp.transpose(strips, (1, 2, 0, 3)).reshape(planes, row_count, col_count)


def solution(mesh):
    in_specs = (
        P(None, "blk", None),
        P("view", None, "blk", None),
        P("view", None, None),
        P("view", None, None),
        P("view", None, None),
        P("view", None),
        P(),
        P("view", "blk"),
        P("view", "blk"),
        P("view", "blk"),
        P("view", "blk"),
        P("view", "blk"),
    )
    out_specs = P(None, "blk", None)
    return jax.shard_map(body, mesh=mesh, in_specs=in_specs, out_specs=out_specs, check_vma=False)
```

```python
import jax
import jax.numpy as jnp
from jax import lax
from jax.experimental import pallas as pl
from jax.experimental.pallas import tpu as pltpu
from jax.sharding import PartitionSpec as P

ITERS = 2
LANE = 128
HALF = 64
TAPS = 31
RADIUS = 15
RANK = 3
ROWS = 16
VIEWS = 8
TAP_LANE = 96
TILE_LANE = 2 * 8
ROW_MARK = 1024
Q_FIRST, Q_LAST = 41, 214
STEPS = (1, -1, 2, -2, 3, -3, 0, 0)
OWN = 6
SEEN = 3 * LANE
F32 = jnp.float32
BF16 = jnp.bfloat16
VMEM_LIMIT = 24 * 1024 * 1024
SMALL_LIMIT = 4 * 1024 * 1024


def start_all(copies):
    for copy in copies:
        copy.start()
    return copies


def wait_all(copies):
    for copy in copies:
        copy.wait()


def lanes_of(shape):
    return lax.broadcasted_iota(jnp.int32, shape, len(shape) - 1)


def rows_of(shape):
    return lax.broadcasted_iota(jnp.int32, shape, len(shape) - 2)


def pick_lane(values, lane):
    index = jnp.full(values.shape, lane, jnp.int32)
    return jnp.take_along_axis(values, index, axis=1, mode="promise_in_bounds")


def look_up(values, index):
    return jnp.take_along_axis(values, index, axis=1, mode="promise_in_bounds")


def halves(values):
    high = values.astype(BF16)
    low = (values - high.astype(F32)).astype(BF16)
    return high, low


def dot(left, right):
    return jnp.dot(left, right, preferred_element_type=F32)


def dot_turned(left, right):
    return lax.dot_general(left, right, (((1,), (1,)), ((), ())), preferred_element_type=F32)


def triple(high, low, right_high, right_low, multiply):
    both = multiply(jnp.concatenate([high, low], axis=0), right_high)
    height = high.shape[0]
    return both[:height] + both[height:] + multiply(high, right_low)


def windows_of(strips):
    count = len(strips)
    turned = [pltpu.roll(strip, HALF, 1) for strip in strips]
    lower = lanes_of(strips[0].shape) < HALF
    zero = jnp.zeros_like(strips[0])
    tiles = []
    for place in range(count + 1):
        left = turned[place - 1] if place > 0 else zero
        right = turned[place] if place < count else zero
        tiles.append(jnp.where(lower, left, right))
    return tiles


def pack_measured_kernel(*refs):
    sources, out, table = refs[:8], refs[8], refs[9]
    targets, sems = refs[10:18], refs[18]
    wait_all(
        start_all(
            [
                pltpu.make_async_copy(source, target, sems.at[number])
                for number, (source, target) in enumerate(zip(sources, targets))
            ]
        )
    )
    measured, dst_row, back_shift, tile_index, psf_z, psf_y, psf_x, psf_mix = targets
    rows = 2 * ROWS
    view = lax.axis_index("view")
    table[...] = jnp.zeros_like(table)
    dst = dst_row[...].astype(F32) + ROW_MARK
    back = back_shift[...].astype(F32)
    tiles = tile_index[...].astype(F32)
    for plane in range(2):
        first = plane * ROWS
        table[0:1, first : first + ROWS] = dst
        table[1:2, first : first + ROWS] = back
        for part in range(2):
            start = first + part * 8
            table[2:3, start : start + 8] = jnp.broadcast_to(tiles[:, part : part + 1], (1, 8))
    upright = jnp.transpose(table[...])[:rows]
    lane = lanes_of((rows, LANE))
    moves = jnp.where(lane == view, upright[:, 0:1], 0.0)
    moves = jnp.where(lane == VIEWS + view, upright[:, 1:2], moves)
    moves = jnp.where(lane == TILE_LANE, upright[:, 2:3], moves)
    table[...] = jnp.zeros_like(table)
    for place, psf in enumerate((psf_z, psf_y, psf_x)):
        for term in range(RANK):
            values = psf[term]
            normal = values / jnp.sum(values, axis=1, keepdims=True)
            row = place * RANK + term
            table[row : row + 1, TAP_LANE : TAP_LANE + TAPS] = normal
    mix = psf_mix[...]
    table[9:10, TAP_LANE : TAP_LANE + RANK] = mix / jnp.sum(mix, axis=1, keepdims=True)
    taps = table[:rows, :]
    stash = jnp.where(lane < TAP_LANE, moves, taps)[:ROWS]
    lane = lanes_of((ROWS, LANE))
    zero = jnp.zeros((ROWS, LANE), F32)
    strips = []
    for plane in range(2):
        values = measured[0, plane]
        strips.append([values[:, place * LANE : (place + 1) * LANE] for place in range(VIEWS)])
    for place in range(VIEWS):
        before = [row[place - 1] if place > 0 else zero for row in strips]
        after = [row[place + 1] if place < VIEWS - 1 else zero for row in strips]
        edges = jnp.where(lane < 96, pltpu.roll(after[1], HALF, 1), before[1])
        edges = jnp.where(lane < HALF, pltpu.roll(before[0], HALF, 1), edges)
        edges = jnp.where(lane < 32, after[0], edges)
        turned = [pltpu.roll(row[place], HALF, 1) for row in strips]
        for number, tile in enumerate((turned[0], turned[1], edges, stash)):
            out[place, :, number * LANE : (number + 1) * LANE] = tile


ANYWHERE = pl.BlockSpec(memory_space=pl.ANY)
IN_VMEM = pl.BlockSpec(memory_space=pltpu.VMEM)


def pack_measured(measured, dst_row, back_shift, tile_index, psf_z, psf_y, psf_x, psf_mix):
    turned = [jnp.transpose(psf, (1, 0, 2)) for psf in (psf_z, psf_y, psf_x)]
    operands = (measured, dst_row, back_shift, tile_index, *turned, psf_mix)
    return pl.pallas_call(
        pack_measured_kernel,
        out_shape=jax.ShapeDtypeStruct((VIEWS, ROWS, 4 * LANE), F32),
        in_specs=[ANYWHERE] * len(operands),
        out_specs=IN_VMEM,
        scratch_shapes=[
            pltpu.VMEM((LANE, LANE), F32),
            *[pltpu.VMEM(operand.shape, operand.dtype) for operand in operands],
            pltpu.SemaphoreType.DMA((len(operands),)),
        ],
        name="pack_measured",
    )(*operands)


def pack_estimate_kernel(field, moves, out):
    lane = lanes_of((ROWS, LANE))
    for plane in range(2):
        strips = [field[plane, :, place * LANE : (place + 1) * LANE] for place in range(VIEWS)]
        tiles = windows_of(strips)
        for place in range(VIEWS):
            out[place, plane] = jnp.where(lane < 2 * VIEWS, moves[...], tiles[place])
            out[place, 2 + plane] = tiles[place + 1]


def pack_estimate(field, moves):
    return pl.pallas_call(
        pack_estimate_kernel,
        out_shape=jax.ShapeDtypeStruct((VIEWS, 4, ROWS, LANE), F32),
        in_specs=[IN_VMEM] * 2,
        out_specs=IN_VMEM,
        cost_estimate=pl.CostEstimate(
            flops=40_000_000_000, bytes_accessed=100_000_000, transcendentals=0
        ),
        compiler_params=pltpu.CompilerParams(vmem_limit_bytes=SMALL_LIMIT),
        name="pack_estimate",
    )(field, moves)


def hand_on_kernel(*refs):
    del refs


def hand_on(arrays):
    count = len(arrays)
    return pl.pallas_call(
        hand_on_kernel,
        out_shape=[jax.ShapeDtypeStruct(array.shape, array.dtype) for array in arrays],
        in_specs=[ANYWHERE] * count,
        out_specs=[ANYWHERE] * count,
        input_output_aliases={number: number for number in range(count)},
        cost_estimate=pl.CostEstimate(
            flops=2_000_000_000, bytes_accessed=1_000_000, transcendentals=0
        ),
        compiler_params=pltpu.CompilerParams(vmem_limit_bytes=SMALL_LIMIT),
        name="hand_on",
    )(*arrays)


def pack_field_kernel(field, out):
    tiles = windows_of([field[place] for place in range(VIEWS)])
    for place in range(VIEWS):
        out[place, 0:2] = tiles[place].reshape(2, ROWS, LANE)
        out[place, 2:4] = tiles[place + 1].reshape(2, ROWS, LANE)


def pack_field(field):
    return pl.pallas_call(
        pack_field_kernel,
        out_shape=jax.ShapeDtypeStruct((VIEWS, 4, ROWS, LANE), F32),
        in_specs=[IN_VMEM],
        out_specs=IN_VMEM,
        compiler_params=pltpu.CompilerParams(vmem_limit_bytes=SMALL_LIMIT),
        name="pack_field",
    )(field)


def tap_index(spread):
    inside = (spread >= 0) & (spread < TAPS)
    return jnp.where(inside, spread + TAP_LANE, LANE - 1)


def build_column_bands(received, high, low):
    high[...] = jnp.zeros_like(high)
    low[...] = jnp.zeros_like(low)
    shape = (LANE, LANE)
    square = tap_index(rows_of(shape) - lanes_of(shape) + RADIUS)
    shape = (ROWS, LANE)
    below = tap_index(rows_of(shape) - lanes_of(shape) + RADIUS + LANE)
    above = tap_index(rows_of(shape) - lanes_of(shape) + RADIUS - ROWS)
    for view in range(VIEWS):
        for term in range(RANK):
            taps = received[view, 6 + term : 7 + term, SEEN:]
            band = halves(look_up(jnp.broadcast_to(taps, square.shape), square))
            lower = halves(look_up(jnp.broadcast_to(taps, below.shape), below))
            upper = halves(look_up(jnp.broadcast_to(taps, above.shape), above))
            for place, target in enumerate((high, low)):
                target[view, term, :LANE, :LANE] = band[place]
                target[view, term, LANE:, LANE:] = band[place]
                target[view, term, LANE : LANE + ROWS, :LANE] = lower[place]
                target[view, term, LANE - ROWS : LANE, LANE:] = upper[place]


def build_row_bands(view, first_row, stash, rows_lane, high, low):
    taps_rows = [stash[3 + term : 4 + term, :] for term in range(RANK)]
    depth_rows = [stash[term : term + 1, :] for term in range(RANK)]
    mix_row = stash[9:10, :]
    centre = TAP_LANE + RADIUS
    dst_lane = rows_lane[pl.ds(view, 1), :]
    shape = (4 * ROWS, LANE)
    row = rows_of(shape)
    lane = lanes_of(shape)
    for part in range(2):
        dst = jnp.broadcast_to(dst_lane[:, part * LANE : (part + 1) * LANE], shape)
        spread = dst.astype(jnp.int32) - ROW_MARK - first_row - row + RADIUS
        index = tap_index(spread)
        if part == 1:
            index = jnp.where(lane < 3 * 2 * ROWS, index, LANE - 1)
        upper = (lane // ROWS) % 2 == 0
        for term in range(RANK):
            taps = jnp.broadcast_to(taps_rows[term], shape)
            band = look_up(taps, index)
            mix = mix_row[:, TAP_LANE + term : TAP_LANE + term + 1]
            depth = depth_rows[term] * mix
            for plane in range(2):
                from_first = depth[:, centre - plane : centre - plane + 1]
                from_second = depth[:, centre + 1 - plane : centre + 2 - plane]
                scaled = band * jnp.where(upper, from_first, from_second)
                band_high, band_low = halves(scaled)
                start = (term * 2 + plane) * 4 * ROWS
                columns = slice(part * LANE, (part + 1) * LANE)
                high[view, start : start + 4 * ROWS, columns] = band_high
                low[view, start : start + 4 * ROWS, columns] = band_low

def build_turned_bands(view, first_row, stash, own_dst, high, low):
    taps_rows = [stash[3 + term : 4 + term, :] for term in range(RANK)]
    depth_rows = [stash[term : term + 1, :] for term in range(RANK)]
    mix_row = stash[9:10, :]
    centre = TAP_LANE + RADIUS
    shape = (ROWS, LANE)
    lane = lanes_of(shape)
    spread = own_dst.astype(jnp.int32) - ROW_MARK - first_row - lane % (4 * ROWS) + RADIUS
    index = tap_index(spread)
    upper = lane < 4 * ROWS
    for term in range(RANK):
        taps = jnp.broadcast_to(taps_rows[term], shape)
        band = look_up(taps, index)
        mix = mix_row[:, TAP_LANE + term : TAP_LANE + term + 1]
        depth = depth_rows[term] * mix
        for plane in range(2):
            from_first = depth[:, centre + plane : centre + plane + 1]
            from_second = depth[:, centre + plane - 1 : centre + plane]
            scaled = band * jnp.where(upper, from_first, from_second)
            band_high, band_low = halves(scaled)
            start = (term * 2 + plane) * ROWS
            high[view, start : start + ROWS, :] = band_high
            low[view, start : start + ROWS, :] = band_low


LAGS = (0, 1, 2, 4, 6)


def iteration_kernel(mode, *refs):
    refs = list(refs)

    def take(count):
        taken = refs[:count]
        del refs[:count]
        return taken

    forward = mode != "adjoint"
    backward = mode != "forward"
    received, field = take(2)
    moves = take(1)[0] if mode == "both" else field
    blurred = take(1)[0] if mode == "adjoint" else None
    if backward:
        sides = take(4)
        sides.insert(2, received)
        tiles, col_high, col_low = take(3)
    if mode == "both":
        row_high, row_low, turned_high, turned_low = take(4)
    (out,) = take(1)
    if mode == "forward":
        col_high, col_low, row_high, row_low = take(4)
    if mode == "adjoint":
        turned_high, turned_low = take(2)
    if forward:
        x_high, x_low, rows_lane = take(3)

    strip = lax.axis_index("view")
    block = lax.axis_index("blk")
    even = block % 2 == 0
    first_column = pl.multiple_of(strip * LANE, LANE)

    def stash(view):
        return received[view, :, SEEN:]

    if mode == "forward":
        build_column_bands(received, col_high, col_low)

    lane = lanes_of((2 * ROWS, LANE))
    column = lane + strip * LANE - HALF
    columns = LANE * VIEWS
    inside = [
        (column >= 0) & (column < columns),
        (column + LANE >= 0) & (column + LANE < columns),
    ]
    wide = lanes_of((ROWS, 2 * LANE))
    wide_column = wide + strip * LANE - HALF
    kept = (wide >= Q_FIRST) & (wide <= Q_LAST) & (wide_column >= 0) & (wide_column < columns)

    if forward:
        if mode == "forward":
            rows_lane[...] = jnp.transpose(moves[:, 0:2].reshape(VIEWS * 2 * ROWS, LANE))
        unused = slice((OWN + 1) * 2 * ROWS, VIEWS * 2 * ROWS)
        x_high[:, unused, :] = jnp.zeros((VIEWS, 2 * ROWS, 2 * LANE), BF16)
        x_low[:, unused, :] = jnp.zeros((VIEWS, 2 * ROWS, 2 * LANE), BF16)

    def prepare(view):
        own_dst = pick_lane(moves[OWN, 0:2].reshape(2 * ROWS, LANE), view)
        last = jnp.max(own_dst) - ROW_MARK
        phase = (last >= ((block + 1) * ROWS).astype(F32)).astype(jnp.int32)
        first_row = (block - 2 + phase) * ROWS
        shift = pick_lane(moves[OWN, 0:2].reshape(2 * ROWS, LANE), VIEWS + view).astype(jnp.int32)
        if mode == "adjoint":
            build_turned_bands(
                view, first_row, stash(view), own_dst[:ROWS], turned_high, turned_low
            )
        if not forward:
            return phase, shift
        if mode == "forward":
            build_row_bands(view, first_row, stash(view), rows_lane, row_high, row_low)
        for slot in range(OWN + 1):
            step = pick_lane(moves[slot, 0:2].reshape(2 * ROWS, LANE), VIEWS + view)
            where = lane + step.astype(jnp.int32)
            index = where & (LANE - 1)
            left = look_up(field[slot, 0:2].reshape(2 * ROWS, LANE), index)
            right = look_up(field[slot, 2:4].reshape(2 * ROWS, LANE), index)
            moved = (jnp.where(where < LANE, left, right), jnp.where(where < 0, left, right))
            for part in range(2):
                high, low = halves(jnp.where(inside[part], moved[part], 0.0))
                rows = slice(slot * 2 * ROWS, (slot + 1) * 2 * ROWS)
                x_high[view, rows, part * LANE : (part + 1) * LANE] = high
                x_low[view, rows, part * LANE : (part + 1) * LANE] = low
        return phase, shift

    def row_stage(view):
        xh, xl = x_high[view], x_low[view]
        return halves(triple(row_high[view], row_low[view], xh, xl, dot))

    def column_stage(view, layers):
        blurred = None
        height = 8 * ROWS
        for term in range(RANK):
            high, low = [half[term * height : (term + 1) * height] for half in layers]
            part = triple(high, low, col_high[view, term], col_low[view, term], dot)
            blurred = part if blurred is None else blurred + part
        return blurred

    def turned_stage(view, blurred, phase):
        quotients = [None] * 8
        lower = lanes_of((ROWS, LANE)) < HALF
        for place in range(4):
            seen = []
            for tile in range(3):
                columns = slice(tile * LANE, (tile + 1) * LANE)
                seen.append(
                    jnp.where(
                        even,
                        jnp.where(
                            phase == 1,
                            sides[place + 1][view, :, columns],
                            sides[place][view, :, columns],
                        ),
                        jnp.where(
                            phase == 1,
                            sides[3 - place][view, :, columns],
                            sides[4 - place][view, :, columns],
                        ),
                    )
                )
            edges = (seen[2], pltpu.roll(seen[2], HALF, 1))
            row_block = block - 2 + phase + place
            fine = kept & (row_block >= 0) & (row_block < VIEWS * 8)
            for plane in range(2):
                middle = seen[plane]
                left = jnp.where(lower, edges[plane], middle)
                right = jnp.where(lower, middle, edges[1 - plane])
                both = jnp.concatenate([left, right], axis=1)
                start = (plane * 4 + place) * ROWS
                ratio = both / blurred[start : start + ROWS]
                quotients[plane * 4 + place] = jnp.where(fine, ratio, 0.0)
        quotient = jnp.concatenate(quotients, axis=0)
        high, low = halves(quotient)
        return triple(turned_high[view], turned_low[view], high, low, dot)

    def last_stage(view, layers, shift):
        where = lane + shift
        index = where & (LANE - 1)
        adjoint = None
        height = 2 * ROWS
        for term in range(RANK):
            layer = layers[term * height : (term + 1) * height]
            left = look_up(layer[:, :LANE], index)
            right = look_up(layer[:, LANE:], index)
            moved = jnp.concatenate(
                [jnp.where(where < LANE, left, right), jnp.where(where < 0, left, right)], axis=1
            )
            high, low = halves(moved)
            band_high = col_high[view, term, HALF : HALF + LANE, :]
            band_low = col_low[view, term, HALF : HALF + LANE, :]
            part = triple(high, low, band_high, band_low, dot_turned)
            adjoint = part if adjoint is None else adjoint + part
        source = column + HALF + shift
        returned = jnp.where((source >= 0) & (source < columns), adjoint, 0.0)
        chosen = pick_lane(stash(view), TILE_LANE)
        weight = jnp.zeros((ROWS, LANE), F32)
        for tile in range(tiles.shape[0]):
            tall = jnp.concatenate([tiles[tile, :, pl.ds(first_column, LANE)]] * 2, axis=0)
            weight = jnp.where(chosen == tile, tall, weight)
        weight = jnp.concatenate([weight, weight], axis=0)
        return weight * returned, weight


    total = jnp.zeros((2 * ROWS, LANE), F32)
    weight_total = jnp.zeros((2 * ROWS, LANE), F32)
    known = [None] * VIEWS
    values = [None] * VIEWS
    stages = []
    if forward:
        stages += ["prepare", "rows", "columns"]
    else:
        stages += ["prepare"]
    if backward:
        stages += ["turned", "last"]
    for step in range(VIEWS + LAGS[len(stages) - 1]):
        for stage, lag in zip(stages, LAGS):
            view = step - lag
            if not 0 <= view < VIEWS:
                continue
            if stage == "prepare":
                known[view] = prepare(view)
                if not forward:
                    values[view] = blurred[view]
            elif stage == "rows":
                values[view] = row_stage(view)
            elif stage == "columns":
                values[view] = column_stage(view, values[view])
                if not backward:
                    out[view] = values[view]
            elif stage == "turned":
                values[view] = turned_stage(view, values[view], known[view][0])
            else:
                more, weight = last_stage(view, values[view], known[view][1])
                total = total + more
                weight_total = weight_total + weight
    if not backward:
        return
    lower = pltpu.roll(field[OWN, 0:2].reshape(2 * ROWS, LANE), HALF, 1)
    upper = pltpu.roll(field[OWN, 2:4].reshape(2 * ROWS, LANE), HALF, 1)
    own = jnp.where(lane < HALF, lower, upper)
    result = own * total / weight_total
    for place in range(VIEWS):
        out[place] = result


def iteration(mode, operands):
    rows = 2 * ROWS
    blurred = jax.ShapeDtypeStruct((VIEWS, 8 * ROWS, 2 * LANE), F32)
    col_band = jax.ShapeDtypeStruct((VIEWS, RANK, 2 * LANE, 2 * LANE), BF16)
    row_band = jax.ShapeDtypeStruct((VIEWS, RANK * 8 * ROWS, 2 * LANE), BF16)
    turned_band = jax.ShapeDtypeStruct((VIEWS, RANK * 2 * ROWS, LANE), BF16)
    outs = [jax.ShapeDtypeStruct((VIEWS, rows, LANE), F32)]
    scratch = []
    if mode == "forward":
        outs = [blurred, col_band, col_band, row_band, row_band]
    if mode == "adjoint":
        outs += [turned_band, turned_band]
    if mode != "adjoint":
        scratch = [
            pltpu.VMEM((VIEWS, 2 * LANE, 2 * LANE), BF16),
            pltpu.VMEM((VIEWS, 2 * LANE, 2 * LANE), BF16),
            pltpu.VMEM((LANE, 2 * LANE), F32),
        ]
    return pl.pallas_call(
        lambda *refs: iteration_kernel(mode, *refs),
        out_shape=outs,
        in_specs=[IN_VMEM] * len(operands),
        out_specs=[IN_VMEM] * len(outs),
        scratch_shapes=scratch,
        compiler_params=pltpu.CompilerParams(vmem_limit_bytes=VMEM_LIMIT),
        cost_estimate=pl.CostEstimate(
            flops=8_000_000_000, bytes_accessed=1_000_000, transcendentals=0
        ),
        name=f"iteration_{mode}",
    )(*operands)


def step_by_view(values):
    blocks = lax.axis_size("blk")
    route = []
    for view, step in enumerate(STEPS):
        for block in range(blocks):
            if 0 <= block + step < blocks:
                route.append((view * blocks + block, view * blocks + block + step))
    return lax.ppermute(values, ("view", "blk"), route)


def with_neighbour(values, first):
    blocks = lax.axis_size("blk")
    route = []
    for block in range(first, blocks - 1, 2):
        route += [(block, block + 1), (block + 1, block)]
    return lax.ppermute(values, "blk", route)


def over_views(values):
    return lax.all_to_all(values, "view", 0, 0)


def body(
    estimate,
    measured,
    psf_z,
    psf_y,
    psf_x,
    psf_mix,
    weight_tiles,
    tile_index,
    src_row,
    dst_row,
    col_shift,
    back_shift,
):
    planes, row_count, col_count = estimate.shape
    stepped = step_by_view(estimate)
    received = over_views(
        pack_measured(measured, dst_row, back_shift, tile_index, psf_z, psf_y, psf_x, psf_mix)
    )
    moves = jnp.sum(received[:, :, SEEN:], axis=0)
    moves, seen = lax.optimization_barrier((moves, received[:, :, :SEEN]))
    packed = pack_estimate(stepped, step_by_view(moves))
    near = hand_on([with_neighbour(seen, first) for first in (0, 1)])
    _, *relayed = lax.optimization_barrier((packed, *near))
    far = [with_neighbour(relayed[1 - first], first) for first in (0, 1)]
    sides = [far[1], near[1], near[0], far[0]]
    field = over_views(packed)
    moves = field
    blurred, *bands = iteration("forward", [received, field])
    strips, *turned = iteration(
        "adjoint", [received, field, blurred, *sides, weight_tiles, *bands[:2]]
    )
    bands += turned
    for _ in range(ITERS - 1):
        field = over_views(pack_field(step_by_view(over_views(strips))))
        (strips,) = iteration(
            "both", [received, field, moves, *sides, weight_tiles, *bands]
        )
    strips = over_views(strips).reshape(VIEWS, planes, row_count, LANE)
    return jnp.transpose(strips, (1, 2, 0, 3)).reshape(planes, row_count, col_count)


def solution(mesh):
    in_specs = (
        P(None, "blk", None),
        P("view", None, "blk", None),
        P("view", None, None),
        P("view", None, None),
        P("view", None, None),
        P("view", None),
        P(),
        P("view", "blk"),
        P("view", "blk"),
        P("view", "blk"),
        P("view", "blk"),
        P("view", "blk"),
    )
    out_specs = P(None, "blk", None)
    return jax.shard_map(body, mesh=mesh, in_specs=in_specs, out_specs=out_specs, check_vma=False)
```

```python
import jax
import jax.numpy as jnp
from jax import lax
from jax.experimental import pallas as pl
from jax.experimental.pallas import tpu as pltpu
from jax.sharding import PartitionSpec as P

ITERS = 2
LANE = 128
HALF = 64
TAPS = 31
RADIUS = 15
RANK = 3
ROWS = 16
VIEWS = 8
TAP_LANE = 96
TILE_LANE = 2 * 8
ROW_MARK = 1024
Q_FIRST, Q_LAST = 41, 214
STEPS = (1, 1, 2, 2, 3, 3, 0, 0)
OWN = 6
SEEN = 3 * LANE
F32 = jnp.float32
BF16 = jnp.bfloat16
VMEM_LIMIT = 24 * 1024 * 1024
SMALL_LIMIT = 4 * 1024 * 1024


def start_all(copies):
    for copy in copies:
        copy.start()
    return copies


def wait_all(copies):
    for copy in copies:
        copy.wait()


def lanes_of(shape):
    return lax.broadcasted_iota(jnp.int32, shape, len(shape) - 1)


def rows_of(shape):
    return lax.broadcasted_iota(jnp.int32, shape, len(shape) - 2)


def pick_lane(values, lane):
    index = jnp.full(values.shape, lane, jnp.int32)
    return jnp.take_along_axis(values, index, axis=1, mode="promise_in_bounds")


def look_up(values, index):
    return jnp.take_along_axis(values, index, axis=1, mode="promise_in_bounds")


def halves(values):
    high = values.astype(BF16)
    low = (values - high.astype(F32)).astype(BF16)
    return high, low


def dot(left, right):
    return jnp.dot(left, right, preferred_element_type=F32)


def dot_turned(left, right):
    return lax.dot_general(left, right, (((1,), (1,)), ((), ())), preferred_element_type=F32)


def triple(high, low, right_high, right_low, multiply):
    both = multiply(jnp.concatenate([high, low], axis=0), right_high)
    height = high.shape[0]
    return both[:height] + both[height:] + multiply(high, right_low)


def windows_of(strips):
    count = len(strips)
    turned = [pltpu.roll(strip, HALF, 1) for strip in strips]
    lower = lanes_of(strips[0].shape) < HALF
    zero = jnp.zeros_like(strips[0])
    tiles = []
    for place in range(count + 1):
        left = turned[place - 1] if place > 0 else zero
        right = turned[place] if place < count else zero
        tiles.append(jnp.where(lower, left, right))
    return tiles


def pack_measured_kernel(*refs):
    sources, out, table = refs[:8], refs[8], refs[9]
    targets, sems = refs[10:18], refs[18]
    wait_all(
        start_all(
            [
                pltpu.make_async_copy(source, target, sems.at[number])
                for number, (source, target) in enumerate(zip(sources, targets))
            ]
        )
    )
    measured, dst_row, back_shift, tile_index, psf_z, psf_y, psf_x, psf_mix = targets
    rows = 2 * ROWS
    view = lax.axis_index("view")
    table[...] = jnp.zeros_like(table)
    dst = dst_row[...].astype(F32) + ROW_MARK
    back = back_shift[...].astype(F32)
    tiles = tile_index[...].astype(F32)
    for plane in range(2):
        first = plane * ROWS
        table[0:1, first : first + ROWS] = dst
        table[1:2, first : first + ROWS] = back
        for part in range(2):
            start = first + part * 8
            table[2:3, start : start + 8] = jnp.broadcast_to(tiles[:, part : part + 1], (1, 8))
    upright = jnp.transpose(table[...])[:rows]
    lane = lanes_of((rows, LANE))
    moves = jnp.where(lane == view, upright[:, 0:1], 0.0)
    moves = jnp.where(lane == VIEWS + view, upright[:, 1:2], moves)
    moves = jnp.where(lane == TILE_LANE, upright[:, 2:3], moves)
    table[...] = jnp.zeros_like(table)
    for place, psf in enumerate((psf_z, psf_y, psf_x)):
        for term in range(RANK):
            values = psf[term]
            normal = values / jnp.sum(values, axis=1, keepdims=True)
            row = place * RANK + term
            table[row : row + 1, TAP_LANE : TAP_LANE + TAPS] = normal
    mix = psf_mix[...]
    table[9:10, TAP_LANE : TAP_LANE + RANK] = mix / jnp.sum(mix, axis=1, keepdims=True)
    taps = table[:rows, :]
    stash = jnp.where(lane < TAP_LANE, moves, taps)[:ROWS]
    lane = lanes_of((ROWS, LANE))
    zero = jnp.zeros((ROWS, LANE), F32)
    strips = []
    for plane in range(2):
        values = measured[0, plane]
        strips.append([values[:, place * LANE : (place + 1) * LANE] for place in range(VIEWS)])
    for place in range(VIEWS):
        before = [row[place - 1] if place > 0 else zero for row in strips]
        after = [row[place + 1] if place < VIEWS - 1 else zero for row in strips]
        edges = jnp.where(lane < 96, pltpu.roll(after[1], HALF, 1), before[1])
        edges = jnp.where(lane < HALF, pltpu.roll(before[0], HALF, 1), edges)
        edges = jnp.where(lane < 32, after[0], edges)
        turned = [pltpu.roll(row[place], HALF, 1) for row in strips]
        for number, tile in enumerate((turned[0], turned[1], edges, stash)):
            out[place, :, number * LANE : (number + 1) * LANE] = tile


ANYWHERE = pl.BlockSpec(memory_space=pl.ANY)
IN_VMEM = pl.BlockSpec(memory_space=pltpu.VMEM)


def pack_measured(measured, dst_row, back_shift, tile_index, psf_z, psf_y, psf_x, psf_mix):
    turned = [jnp.transpose(psf, (1, 0, 2)) for psf in (psf_z, psf_y, psf_x)]
    operands = (measured, dst_row, back_shift, tile_index, *turned, psf_mix)
    return pl.pallas_call(
        pack_measured_kernel,
        out_shape=jax.ShapeDtypeStruct((VIEWS, ROWS, 4 * LANE), F32),
        in_specs=[ANYWHERE] * len(operands),
        out_specs=IN_VMEM,
        scratch_shapes=[
            pltpu.VMEM((LANE, LANE), F32),
            *[pltpu.VMEM(operand.shape, operand.dtype) for operand in operands],
            pltpu.SemaphoreType.DMA((len(operands),)),
        ],
        name="pack_measured",
    )(*operands)


def pack_estimate_kernel(field, moves, out):
    lane = lanes_of((ROWS, LANE))
    for plane in range(2):
        strips = [field[plane, :, place * LANE : (place + 1) * LANE] for place in range(VIEWS)]
        tiles = windows_of(strips)
        for place in range(VIEWS):
            out[place, plane] = jnp.where(lane < 2 * VIEWS, moves[...], tiles[place])
            out[place, 2 + plane] = tiles[place + 1]


def pack_estimate(field, moves):
    return pl.pallas_call(
        pack_estimate_kernel,
        out_shape=jax.ShapeDtypeStruct((VIEWS, 4, ROWS, LANE), F32),
        in_specs=[IN_VMEM] * 2,
        out_specs=IN_VMEM,
        cost_estimate=pl.CostEstimate(
            flops=40_000_000_000, bytes_accessed=100_000_000, transcendentals=0
        ),
        compiler_params=pltpu.CompilerParams(vmem_limit_bytes=SMALL_LIMIT),
        name="pack_estimate",
    )(field, moves)


def hand_on_kernel(*refs):
    del refs


def hand_on(arrays):
    count = len(arrays)
    return pl.pallas_call(
        hand_on_kernel,
        out_shape=[jax.ShapeDtypeStruct(array.shape, array.dtype) for array in arrays],
        in_specs=[ANYWHERE] * count,
        out_specs=[ANYWHERE] * count,
        input_output_aliases={number: number for number in range(count)},
        cost_estimate=pl.CostEstimate(
            flops=2_000_000_000, bytes_accessed=1_000_000, transcendentals=0
        ),
        compiler_params=pltpu.CompilerParams(vmem_limit_bytes=SMALL_LIMIT),
        name="hand_on",
    )(*arrays)


def pack_field_kernel(field, out):
    tiles = windows_of([field[place] for place in range(VIEWS)])
    for place in range(VIEWS):
        out[place, 0:2] = tiles[place].reshape(2, ROWS, LANE)
        out[place, 2:4] = tiles[place + 1].reshape(2, ROWS, LANE)


def pack_field(field):
    return pl.pallas_call(
        pack_field_kernel,
        out_shape=jax.ShapeDtypeStruct((VIEWS, 4, ROWS, LANE), F32),
        in_specs=[IN_VMEM],
        out_specs=IN_VMEM,
        compiler_params=pltpu.CompilerParams(vmem_limit_bytes=SMALL_LIMIT),
        name="pack_field",
    )(field)


def tap_index(spread):
    inside = (spread >= 0) & (spread < TAPS)
    return jnp.where(inside, spread + TAP_LANE, LANE - 1)


def build_column_bands(received, high, low):
    high[...] = jnp.zeros_like(high)
    low[...] = jnp.zeros_like(low)
    shape = (LANE, LANE)
    square = tap_index(rows_of(shape) - lanes_of(shape) + RADIUS)
    shape = (ROWS, LANE)
    below = tap_index(rows_of(shape) - lanes_of(shape) + RADIUS + LANE)
    above = tap_index(rows_of(shape) - lanes_of(shape) + RADIUS - ROWS)
    for view in range(VIEWS):
        for term in range(RANK):
            taps = received[view, 6 + term : 7 + term, SEEN:]
            band = halves(look_up(jnp.broadcast_to(taps, square.shape), square))
            lower = halves(look_up(jnp.broadcast_to(taps, below.shape), below))
            upper = halves(look_up(jnp.broadcast_to(taps, above.shape), above))
            for place, target in enumerate((high, low)):
                target[view, term, :LANE, :LANE] = band[place]
                target[view, term, LANE:, LANE:] = band[place]
                target[view, term, LANE : LANE + ROWS, :LANE] = lower[place]
                target[view, term, LANE - ROWS : LANE, LANE:] = upper[place]


def build_row_bands(view, first_row, stash, rows_lane, high, low):
    taps_rows = [stash[3 + term : 4 + term, :] for term in range(RANK)]
    depth_rows = [stash[term : term + 1, :] for term in range(RANK)]
    mix_row = stash[9:10, :]
    centre = TAP_LANE + RADIUS
    dst_lane = rows_lane[pl.ds(view, 1), :]
    shape = (4 * ROWS, LANE)
    row = rows_of(shape)
    lane = lanes_of(shape)
    for part in range(2):
        dst = jnp.broadcast_to(dst_lane[:, part * LANE : (part + 1) * LANE], shape)
        spread = dst.astype(jnp.int32) - ROW_MARK - first_row - row + RADIUS
        index = tap_index(spread)
        if part == 1:
            index = jnp.where(lane < 3 * 2 * ROWS, index, LANE - 1)
        upper = (lane // ROWS) % 2 == 0
        for term in range(RANK):
            taps = jnp.broadcast_to(taps_rows[term], shape)
            band = look_up(taps, index)
            mix = mix_row[:, TAP_LANE + term : TAP_LANE + term + 1]
            depth = depth_rows[term] * mix
            for plane in range(2):
                from_first = depth[:, centre - plane : centre - plane + 1]
                from_second = depth[:, centre + 1 - plane : centre + 2 - plane]
                scaled = band * jnp.where(upper, from_first, from_second)
                band_high, band_low = halves(scaled)
                start = (term * 2 + plane) * 4 * ROWS
                columns = slice(part * LANE, (part + 1) * LANE)
                high[view, start : start + 4 * ROWS, columns] = band_high
                low[view, start : start + 4 * ROWS, columns] = band_low

def build_turned_bands(view, first_row, stash, own_dst, high, low):
    taps_rows = [stash[3 + term : 4 + term, :] for term in range(RANK)]
    depth_rows = [stash[term : term + 1, :] for term in range(RANK)]
    mix_row = stash[9:10, :]
    centre = TAP_LANE + RADIUS
    shape = (ROWS, LANE)
    lane = lanes_of(shape)
    spread = own_dst.astype(jnp.int32) - ROW_MARK - first_row - lane % (4 * ROWS) + RADIUS
    index = tap_index(spread)
    upper = lane < 4 * ROWS
    for term in range(RANK):
        taps = jnp.broadcast_to(taps_rows[term], shape)
        band = look_up(taps, index)
        mix = mix_row[:, TAP_LANE + term : TAP_LANE + term + 1]
        depth = depth_rows[term] * mix
        for plane in range(2):
            from_first = depth[:, centre + plane : centre + plane + 1]
            from_second = depth[:, centre + plane - 1 : centre + plane]
            scaled = band * jnp.where(upper, from_first, from_second)
            band_high, band_low = halves(scaled)
            start = (term * 2 + plane) * ROWS
            high[view, start : start + ROWS, :] = band_high
            low[view, start : start + ROWS, :] = band_low


LAGS = (0, 1, 2, 4, 6)


def iteration_kernel(mode, *refs):
    refs = list(refs)

    def take(count):
        taken = refs[:count]
        del refs[:count]
        return taken

    forward = mode != "adjoint"
    backward = mode != "forward"
    received, field = take(2)
    moves = take(1)[0] if mode == "both" else field
    blurred = take(1)[0] if mode == "adjoint" else None
    if backward:
        sides = take(4)
        sides.insert(2, received)
        tiles, col_high, col_low = take(3)
    if mode == "both":
        row_high, row_low, turned_high, turned_low = take(4)
    (out,) = take(1)
    if mode == "forward":
        col_high, col_low, row_high, row_low = take(4)
    if mode == "adjoint":
        turned_high, turned_low = take(2)
    if forward:
        x_high, x_low, rows_lane = take(3)

    strip = lax.axis_index("view")
    block = lax.axis_index("blk")
    even = block % 2 == 0
    first_column = pl.multiple_of(strip * LANE, LANE)

    def stash(view):
        return received[view, :, SEEN:]

    if mode == "forward":
        build_column_bands(received, col_high, col_low)

    lane = lanes_of((2 * ROWS, LANE))
    column = lane + strip * LANE - HALF
    columns = LANE * VIEWS
    inside = [
        (column >= 0) & (column < columns),
        (column + LANE >= 0) & (column + LANE < columns),
    ]
    wide = lanes_of((ROWS, 2 * LANE))
    wide_column = wide + strip * LANE - HALF
    kept = (wide >= Q_FIRST) & (wide <= Q_LAST) & (wide_column >= 0) & (wide_column < columns)

    if forward:
        if mode == "forward":
            rows_lane[...] = jnp.transpose(moves[:, 0:2].reshape(VIEWS * 2 * ROWS, LANE))
        unused = slice((OWN + 1) * 2 * ROWS, VIEWS * 2 * ROWS)
        x_high[:, unused, :] = jnp.zeros((VIEWS, 2 * ROWS, 2 * LANE), BF16)
        x_low[:, unused, :] = jnp.zeros((VIEWS, 2 * ROWS, 2 * LANE), BF16)

    def prepare(view):
        own_dst = pick_lane(moves[OWN, 0:2].reshape(2 * ROWS, LANE), view)
        last = jnp.max(own_dst) - ROW_MARK
        phase = (last >= ((block + 1) * ROWS).astype(F32)).astype(jnp.int32)
        first_row = (block - 2 + phase) * ROWS
        shift = pick_lane(moves[OWN, 0:2].reshape(2 * ROWS, LANE), VIEWS + view).astype(jnp.int32)
        if mode == "adjoint":
            build_turned_bands(
                view, first_row, stash(view), own_dst[:ROWS], turned_high, turned_low
            )
        if not forward:
            return phase, shift
        if mode == "forward":
            build_row_bands(view, first_row, stash(view), rows_lane, row_high, row_low)
        for slot in range(OWN + 1):
            step = pick_lane(moves[slot, 0:2].reshape(2 * ROWS, LANE), VIEWS + view)
            where = lane + step.astype(jnp.int32)
            index = where & (LANE - 1)
            left = look_up(field[slot, 0:2].reshape(2 * ROWS, LANE), index)
            right = look_up(field[slot, 2:4].reshape(2 * ROWS, LANE), index)
            moved = (jnp.where(where < LANE, left, right), jnp.where(where < 0, left, right))
            for part in range(2):
                high, low = halves(jnp.where(inside[part], moved[part], 0.0))
                rows = slice(slot * 2 * ROWS, (slot + 1) * 2 * ROWS)
                x_high[view, rows, part * LANE : (part + 1) * LANE] = high
                x_low[view, rows, part * LANE : (part + 1) * LANE] = low
        return phase, shift

    def row_stage(view):
        xh, xl = x_high[view], x_low[view]
        return halves(triple(row_high[view], row_low[view], xh, xl, dot))

    def column_stage(view, layers):
        blurred = None
        height = 8 * ROWS
        for term in range(RANK):
            high, low = [half[term * height : (term + 1) * height] for half in layers]
            part = triple(high, low, col_high[view, term], col_low[view, term], dot)
            blurred = part if blurred is None else blurred + part
        return blurred

    def turned_stage(view, blurred, phase):
        quotients = [None] * 8
        lower = lanes_of((ROWS, LANE)) < HALF
        for place in range(4):
            seen = []
            for tile in range(3):
                columns = slice(tile * LANE, (tile + 1) * LANE)
                seen.append(
                    jnp.where(
                        even,
                        jnp.where(
                            phase == 1,
                            sides[place + 1][view, :, columns],
                            sides[place][view, :, columns],
                        ),
                        jnp.where(
                            phase == 1,
                            sides[3 - place][view, :, columns],
                            sides[4 - place][view, :, columns],
                        ),
                    )
                )
            edges = (seen[2], pltpu.roll(seen[2], HALF, 1))
            row_block = block - 2 + phase + place
            fine = kept & (row_block >= 0) & (row_block < VIEWS * 8)
            for plane in range(2):
                middle = seen[plane]
                left = jnp.where(lower, edges[plane], middle)
                right = jnp.where(lower, middle, edges[1 - plane])
                both = jnp.concatenate([left, right], axis=1)
                start = (plane * 4 + place) * ROWS
                ratio = both / blurred[start : start + ROWS]
                quotients[plane * 4 + place] = jnp.where(fine, ratio, 0.0)
        quotient = jnp.concatenate(quotients, axis=0)
        high, low = halves(quotient)
        return triple(turned_high[view], turned_low[view], high, low, dot)

    def last_stage(view, layers, shift):
        where = lane + shift
        index = where & (LANE - 1)
        adjoint = None
        height = 2 * ROWS
        for term in range(RANK):
            layer = layers[term * height : (term + 1) * height]
            left = look_up(layer[:, :LANE], index)
            right = look_up(layer[:, LANE:], index)
            moved = jnp.concatenate(
                [jnp.where(where < LANE, left, right), jnp.where(where < 0, left, right)], axis=1
            )
            high, low = halves(moved)
            band_high = col_high[view, term, HALF : HALF + LANE, :]
            band_low = col_low[view, term, HALF : HALF + LANE, :]
            part = triple(high, low, band_high, band_low, dot_turned)
            adjoint = part if adjoint is None else adjoint + part
        source = column + HALF + shift
        returned = jnp.where((source >= 0) & (source < columns), adjoint, 0.0)
        chosen = pick_lane(stash(view), TILE_LANE)
        weight = jnp.zeros((ROWS, LANE), F32)
        for tile in range(tiles.shape[0]):
            tall = jnp.concatenate([tiles[tile, :, pl.ds(first_column, LANE)]] * 2, axis=0)
            weight = jnp.where(chosen == tile, tall, weight)
        weight = jnp.concatenate([weight, weight], axis=0)
        return weight * returned, weight


    total = jnp.zeros((2 * ROWS, LANE), F32)
    weight_total = jnp.zeros((2 * ROWS, LANE), F32)
    known = [None] * VIEWS
    values = [None] * VIEWS
    stages = []
    if forward:
        stages += ["prepare", "rows", "columns"]
    else:
        stages += ["prepare"]
    if backward:
        stages += ["turned", "last"]
    for step in range(VIEWS + LAGS[len(stages) - 1]):
        for stage, lag in zip(stages, LAGS):
            view = step - lag
            if not 0 <= view < VIEWS:
                continue
            if stage == "prepare":
                known[view] = prepare(view)
                if not forward:
                    values[view] = blurred[view]
            elif stage == "rows":
                values[view] = row_stage(view)
            elif stage == "columns":
                values[view] = column_stage(view, values[view])
                if not backward:
                    out[view] = values[view]
            elif stage == "turned":
                values[view] = turned_stage(view, values[view], known[view][0])
            else:
                more, weight = last_stage(view, values[view], known[view][1])
                total = total + more
                weight_total = weight_total + weight
    if not backward:
        return
    lower = pltpu.roll(field[OWN, 0:2].reshape(2 * ROWS, LANE), HALF, 1)
    upper = pltpu.roll(field[OWN, 2:4].reshape(2 * ROWS, LANE), HALF, 1)
    own = jnp.where(lane < HALF, lower, upper)
    result = own * total / weight_total
    for place in range(VIEWS):
        out[place] = result


def iteration(mode, operands):
    rows = 2 * ROWS
    blurred = jax.ShapeDtypeStruct((VIEWS, 8 * ROWS, 2 * LANE), F32)
    col_band = jax.ShapeDtypeStruct((VIEWS, RANK, 2 * LANE, 2 * LANE), BF16)
    row_band = jax.ShapeDtypeStruct((VIEWS, RANK * 8 * ROWS, 2 * LANE), BF16)
    turned_band = jax.ShapeDtypeStruct((VIEWS, RANK * 2 * ROWS, LANE), BF16)
    outs = [jax.ShapeDtypeStruct((VIEWS, rows, LANE), F32)]
    scratch = []
    if mode == "forward":
        outs = [blurred, col_band, col_band, row_band, row_band]
    if mode == "adjoint":
        outs += [turned_band, turned_band]
    if mode != "adjoint":
        scratch = [
            pltpu.VMEM((VIEWS, 2 * LANE, 2 * LANE), BF16),
            pltpu.VMEM((VIEWS, 2 * LANE, 2 * LANE), BF16),
            pltpu.VMEM((LANE, 2 * LANE), F32),
        ]
    return pl.pallas_call(
        lambda *refs: iteration_kernel(mode, *refs),
        out_shape=outs,
        in_specs=[IN_VMEM] * len(operands),
        out_specs=[IN_VMEM] * len(outs),
        scratch_shapes=scratch,
        compiler_params=pltpu.CompilerParams(vmem_limit_bytes=VMEM_LIMIT),
        cost_estimate=pl.CostEstimate(
            flops=8_000_000_000, bytes_accessed=1_000_000, transcendentals=0
        ),
        name=f"iteration_{mode}",
    )(*operands)


def step_by_view(values):
    blocks = lax.axis_size("blk")
    route = []
    for view, step in enumerate(STEPS):
        here = view * blocks
        if step == 0:
            route += [(here + block, here + block) for block in range(blocks)]
            continue
        for block in range(blocks - step):
            if (block // step) % 2 == view % 2:
                route += [(here + block, here + block + step), (here + block + step, here + block)]
    return lax.ppermute(values, ("view", "blk"), route)


def with_neighbour(values, first):
    blocks = lax.axis_size("blk")
    route = []
    for block in range(first, blocks - 1, 2):
        route += [(block, block + 1), (block + 1, block)]
    return lax.ppermute(values, "blk", route)


def over_views(values):
    return lax.all_to_all(values, "view", 0, 0)


def body(
    estimate,
    measured,
    psf_z,
    psf_y,
    psf_x,
    psf_mix,
    weight_tiles,
    tile_index,
    src_row,
    dst_row,
    col_shift,
    back_shift,
):
    planes, row_count, col_count = estimate.shape
    stepped = step_by_view(estimate)
    received = over_views(
        pack_measured(measured, dst_row, back_shift, tile_index, psf_z, psf_y, psf_x, psf_mix)
    )
    moves = jnp.sum(received[:, :, SEEN:], axis=0)
    moves, seen = lax.optimization_barrier((moves, received[:, :, :SEEN]))
    packed = pack_estimate(stepped, step_by_view(moves))
    near = hand_on([with_neighbour(seen, first) for first in (0, 1)])
    _, *relayed = lax.optimization_barrier((packed, *near))
    far = [with_neighbour(relayed[1 - first], first) for first in (0, 1)]
    sides = [far[1], near[1], near[0], far[0]]
    field = over_views(packed)
    moves = field
    blurred, *bands = iteration("forward", [received, field])
    strips, *turned = iteration(
        "adjoint", [received, field, blurred, *sides, weight_tiles, *bands[:2]]
    )
    bands += turned
    for _ in range(ITERS - 1):
        field = over_views(pack_field(step_by_view(over_views(strips))))
        (strips,) = iteration(
            "both", [received, field, moves, *sides, weight_tiles, *bands]
        )
    strips = over_views(strips).reshape(VIEWS, planes, row_count, LANE)
    return jnp.transpose(strips, (1, 2, 0, 3)).reshape(planes, row_count, col_count)


def solution(mesh):
    in_specs = (
        P(None, "blk", None),
        P("view", None, "blk", None),
        P("view", None, None),
        P("view", None, None),
        P("view", None, None),
        P("view", None),
        P(),
        P("view", "blk"),
        P("view", "blk"),
        P("view", "blk"),
        P("view", "blk"),
        P("view", "blk"),
    )
    out_specs = P(None, "blk", None)
    return jax.shard_map(body, mesh=mesh, in_specs=in_specs, out_specs=out_specs, check_vma=False)
```
